512 devices in a mesh: vtx: 64 (over y, z_lo, core), col: 8 (over z_hi, x).
Axes of the slice: x: 4, y: 8, z: 8 (z_hi: 2, z_lo: 4; z = z_hi * 4 + z_lo), core: 2. Of those that a mesh axis runs over, the one named last changes fastest.
Arguments:
- features: bfloat16 [128, 65536], P('col', 'vtx'), may hold values from -6 to 6
- tile_values: bfloat16 [4096, 128, 128], P('vtx'), may hold values from 0 to 1
- tile_source: int32 [4096], P('vtx'), may hold values from 0 to 7
- tile_dest: int32 [4096], P('vtx'), may hold values from 0 to 511, as said below
- tile_count: int32 [64], P('vtx'), may hold values from 8 to 64, as said below
- degree: int32 [65536], P('vtx'), may hold values from 8 to 64
- w_self: bfloat16 [128, 256], replicated, may hold values from -0.5 to 0.5
- w_neigh: bfloat16 [128, 256], replicated, may hold values from -0.5 to 0.5
- bias: float32 [256], replicated, may hold values from -3 to 3
- cotangent: bfloat16 [256, 65536], P(None, ('vtx', 'col')), may hold values from -6 to 6
Outputs:
- hidden: bfloat16 [256, 65536], P(None, ('vtx', 'col'))
- grad_x: bfloat16 [128, 65536], P('col', 'vtx')
- grad_self: float32 [128, 256], replicated
- grad_neigh: float32 [128, 256], replicated
- grad_bias: float32 [256], replicated
The draws below stay inside these ranges and needn't reach their ends.
Inputs may be any that keep to these rules, and one draw needn't show every extreme that they name: Index v of vtx uses its first tile_count[v] slots; the others are ignored. Some index uses all 64 slots in every draw. `tile_dest`: among the first 32 slots of one index of vtx, and likewise among its last 32, at most 2 have destination blocks at any one index j of vtx (blocks j * 8 to (j + 1) * 8 - 1); this most is reached.
All inputs are finite; a program needn't handle non-finite values.
Results may differ from the reference program's by a relative error of at most 0.007.
Values may be sent and summed in bfloat16 or wider, within the bound.
No kernel may reach another device: no remote copies, remote signals or barrier semaphores. Data moves between devices by JAX's collectives and lax.ppermute only.
A program may use at most 64 MiB of HBM per device.

```python
import jax
import jax.numpy as jnp
from jax import lax

F_IN = 128
OUT_F = 256
TB = 128
RB_DEV = 8
TILES_DEV = 64
CAP = 2
NODES = 65536
NT_ALL = 4096
N_VTX = 64


def draw_tile_dest(key, part):
    key = jax.random.fold_in(key, 11)
    half_slots = TILES_DEV // 2
    key_list = jax.random.split(key, N_VTX * 2 + 1)

    def one_half(half_key):
        first_key, second_key = jax.random.split(half_key)
        owner_ids = jax.random.permutation(first_key, N_VTX)[:half_slots // CAP]
        owner_ids = jnp.repeat(owner_ids, CAP)
        return jax.random.permutation(second_key, owner_ids)
    owner_ids = jax.vmap(one_half)(key_list[:-1]).reshape(N_VTX * TILES_DEV)
    within = jax.random.randint(key_list[-1], (N_VTX * TILES_DEV,), 0, RB_DEV)
    return (owner_ids * RB_DEV + within).astype(jnp.int32)


def draw_tile_count(key, part):
    key = jax.random.fold_in(key, 23)
    first_key, second_key = jax.random.split(key)
    levels = jax.random.randint(first_key, (N_VTX,), 0, 4)
    divisors = jnp.array([1, 2, 4, 8], jnp.int32)[levels]
    counts = TILES_DEV // divisors
    full_index = jax.random.randint(second_key, (), 0, N_VTX)
    counts = jnp.where(jnp.arange(N_VTX) == full_index, TILES_DEV, counts)
    return counts.astype(jnp.int32)


def touch_ends(values, stream_key, low, top_value):
    longest = values.shape.index(max(values.shape))
    spots = []
    for shift in (0, 1):
        where = [jax.random.randint(jax.random.fold_in(stream_key, axis), (), 0, length) for axis, length in enumerate(values.shape)]
        where[longest] = (where[longest] + shift) % values.shape[longest]
        spots.append(tuple(where))
    return values.at[spots[0]].set(low).at[spots[1]].set(top_value)


def level_of(own_key, dims, cuts, least, largest):
    loudness = 1.0
    for dim, parts in cuts:
        draws = jax.random.uniform(jax.random.fold_in(jax.random.fold_in(own_key, 6), dim), (parts,), jnp.float32, least / len(cuts), largest / len(cuts))
        loudness = loudness * jnp.repeat(jnp.exp(draws), dims[dim] // parts).reshape((-1,) + (1,) * (len(dims) - 1 - dim))
    return loudness


def scatter_about(stream_key, dims, spread, reach, shards=(), held_as=jnp.bfloat16):
    values = spread * jax.random.normal(stream_key, dims, jnp.float32)
    if shards:
        values = values * level_of(stream_key, dims, shards, -0.22, 0.18)
    return jnp.clip(values, -reach, reach).astype(held_as)


def setup_inputs(seed: int = 0) -> dict:
    seeds = jax.random.split(jax.random.key(seed), 11)
    features = scatter_about(seeds[0], (F_IN, NODES), 1.0, 6.0, ((0, 8), (1, 64)))
    tile_values = jnp.clip(1.0 * jax.random.uniform(seeds[1], (NT_ALL, TB, TB), jnp.float32) ** level_of(seeds[1], (NT_ALL, TB, TB), ((0, 64),), -0.2, 0.2), 0.0, 1.0).astype(jnp.bfloat16)
    tile_source = touch_ends(jax.random.randint(seeds[2], (NT_ALL,), 0, RB_DEV), jax.random.fold_in(seeds[2], 1), 0, RB_DEV - 1).astype(jnp.int32)
    tile_dest = draw_tile_dest(jax.random.fold_in(seeds[10], 71), 0)
    tile_count = draw_tile_count(jax.random.fold_in(seeds[10], 71), 0)
    degree = touch_ends(jax.random.randint(seeds[5], (NODES,), 8, 65), jax.random.fold_in(seeds[5], 1), 8, 64).astype(jnp.int32)
    w_self = scatter_about(seeds[6], (F_IN, OUT_F), F_IN ** -0.5, 0.5)
    w_neigh = scatter_about(seeds[7], (F_IN, OUT_F), F_IN ** -0.5, 0.5)
    bias = scatter_about(seeds[8], (OUT_F,), 0.5, 3.0, (), jnp.float32)
    cotangent = scatter_about(seeds[9], (OUT_F, NODES), 1.0, 6.0, ((1, 512),))
    return dict(features=features, tile_values=tile_values, tile_source=tile_source, tile_dest=tile_dest, tile_count=tile_count, degree=degree, w_self=w_self, w_neigh=w_neigh, bias=bias, cotangent=cotangent)


epsilon = 1e-06

def normalized(summed):
    return summed / jnp.sqrt(jnp.mean(summed * summed) + epsilon)

def silu_slope(preact):
    sigma = jax.nn.sigmoid(preact)
    return sigma * (1.0 + preact * (1.0 - sigma))

def reference(features, tile_values, tile_source, tile_dest, tile_count, degree, w_self, w_neigh, bias, cotangent):
    node_total = features.shape[1]
    block_total = node_total // TB
    slot_ids = jnp.arange(TILES_DEV, dtype=jnp.int32)
    device_ids = jnp.arange(N_VTX, dtype=jnp.int32)
    values_dev = tile_values.reshape(N_VTX, TILES_DEV, TB, TB)
    source_dev = tile_source.reshape(N_VTX, TILES_DEV)
    dest_dev = tile_dest.reshape(N_VTX, TILES_DEV)
    feat_blocks = features.reshape(F_IN, block_total, TB)

    def forward_step(summed, item):
        device, values, sources, dests, used = item
        blocks = device * RB_DEV + sources
        gathered = jnp.take(feat_blocks, blocks, axis=1).astype(jnp.float32)
        terms = jnp.einsum('ftj,tij->tfi', gathered, values.astype(jnp.float32), precision=lax.Precision.HIGHEST)
        terms = jnp.where((slot_ids < used)[:, None, None], terms, 0.0)
        return (summed.at[dests].add(terms), None)
    start_sum = jnp.zeros((block_total, F_IN, TB), jnp.float32)
    agg_blocks, _ = lax.scan(forward_step, start_sum, (device_ids, values_dev, source_dev, dest_dev, tile_count))
    agg_sum = agg_blocks.transpose(1, 0, 2).reshape(F_IN, node_total)
    deg_float = degree.astype(jnp.float32)
    agg = (agg_sum / deg_float[None, :]).astype(jnp.bfloat16)
    preact = jnp.dot(w_self.T, features, preferred_element_type=jnp.float32)
    preact = preact + jnp.dot(w_neigh.T, agg, preferred_element_type=jnp.float32) + bias[:, None]
    hidden = jax.nn.silu(preact).astype(jnp.bfloat16)
    grad_pre = (cotangent.astype(jnp.float32) * silu_slope(preact)).astype(jnp.bfloat16)
    sum_self = jnp.dot(features, grad_pre.T, preferred_element_type=jnp.float32)
    sum_neigh = jnp.dot(agg, grad_pre.T, preferred_element_type=jnp.float32)
    sum_bias = lax.optimization_barrier(jnp.sum(grad_pre.astype(jnp.float32), axis=1))
    dx_self = jnp.dot(w_self, grad_pre, preferred_element_type=jnp.float32).astype(jnp.bfloat16)
    dagg = jnp.dot(w_neigh, grad_pre, preferred_element_type=jnp.float32).astype(jnp.bfloat16)
    dagg = lax.optimization_barrier(dagg)
    dsum = (dagg.astype(jnp.float32) / deg_float[None, :]).astype(jnp.bfloat16)
    dsum_blocks = dsum.reshape(F_IN, block_total, TB)

    def backward_step(summed, item):
        device, values, sources, dests, used = item
        blocks = device * RB_DEV + sources
        gathered = jnp.take(dsum_blocks, dests, axis=1).astype(jnp.float32)
        terms = jnp.einsum('fti,tij->tfj', gathered, values.astype(jnp.float32), precision=lax.Precision.HIGHEST)
        terms = jnp.where((slot_ids < used)[:, None, None], terms, 0.0)
        return (summed.at[blocks].add(terms), None)
    back_blocks, _ = lax.scan(backward_step, start_sum, (device_ids, values_dev, source_dev, dest_dev, tile_count))
    dx_neigh = back_blocks.transpose(1, 0, 2).reshape(F_IN, node_total)
    dx_self = lax.optimization_barrier(dx_self)
    grad_x = (dx_self.astype(jnp.float32) + dx_neigh).astype(jnp.bfloat16)
    return (hidden, grad_x, normalized(sum_self), normalized(sum_neigh), normalized(sum_bias))
```

```python
import jax
import jax.numpy as jnp
from jax import lax
from jax.experimental import pallas as pl
from jax.experimental.pallas import tpu as pltpu
from jax.sharding import Mesh
from jax.sharding import PartitionSpec as P

TB = 128
TILES_DEV = 64
RB = 8
F_LOC = 16
Y = 8
STEP = 16

EPS = 1e-06
BF = jnp.bfloat16
F32 = jnp.float32

AXES = ("y", "zl", "k", "col")
VTX = ("y", "zl", "k")
YZ = ("y", "zl")

VMEM = pl.BlockSpec(memory_space=pltpu.VMEM)
SMEM = pl.BlockSpec(memory_space=pltpu.SMEM)
PARAMS = pltpu.CompilerParams(vmem_limit_bytes=32 * 1024 * 1024)


def whole(kernel, out_shape, in_specs, scratch=()):
    many = isinstance(out_shape, (tuple, list))
    return pl.pallas_call(
        kernel,
        out_shape=out_shape,
        in_specs=in_specs,
        out_specs=[VMEM] * len(out_shape) if many else VMEM,
        scratch_shapes=list(scratch),
        compiler_params=PARAMS,
    )


def sds(shape, dtype):
    return jax.ShapeDtypeStruct(shape, dtype)


def terms_kernel(src, feats, vals, out):
    first = pl.program_id(0) * STEP
    for t in range(STEP):
        start = pl.multiple_of(src[first + t] * TB, TB)
        block = feats[:, pl.ds(start, TB)]
        term = lax.dot_general(
            block, vals[t], (((1,), (1,)), ((), ())), preferred_element_type=F32
        )
        out[t] = term.astype(BF)


def tile_terms(src, feats, vals):
    return pl.pallas_call(
        terms_kernel,
        out_shape=sds((TILES_DEV, F_LOC, TB), BF),
        grid_spec=pltpu.PrefetchScalarGridSpec(
            num_scalar_prefetch=1,
            grid=(TILES_DEV // STEP,),
            in_specs=[
                pl.BlockSpec((F_LOC, RB * TB), lambda g, s: (0, 0)),
                pl.BlockSpec((STEP, TB, TB), lambda g, s: (g, 0, 0)),
            ],
            out_specs=pl.BlockSpec((STEP, F_LOC, TB), lambda g, s: (g, 0, 0)),
        ),
        compiler_params=PARAMS,
    )(src, feats, vals)


def dense_kernel(dest_own, dest_other, own, other, out, acc):
    k = lax.axis_index("k")
    dump = acc.shape[0] - 1
    acc[...] = jnp.zeros_like(acc)
    for dests, terms in ((dest_own, own), (dest_other, other)):

        def add(s, carry, dests=dests, terms=terms):
            d = dests[s]
            mine = jnp.logical_and(d >= 0, ((d >> 3) & 1) == k)
            at = jnp.where(mine, (d >> 4) * RB + (d & 7), dump)
            acc[at] = acc[at] + terms[s].astype(F32)
            return carry

        lax.fori_loop(0, TILES_DEV, add, 0, unroll=8)
    out[...] = acc[0:dump].astype(BF)


def agg_kernel(recv, degree, feats, out):
    for b in range(RB):
        total = jnp.sum(recv[:, b].astype(F32), axis=0)
        deg = degree[b : b + 1, :].astype(F32)
        out[b, 0:F_LOC] = (total / deg).astype(BF)
        out[b, F_LOC : 2 * F_LOC] = feats[:, b * TB : (b + 1) * TB]


def dense_layer_kernel(recv, w_self, w_neigh, bias, cot, degree, hidden, out):
    agg = recv[:, 0:F_LOC].reshape(RB * F_LOC, TB)
    feats = recv[:, F_LOC : 2 * F_LOC].reshape(RB * F_LOC, TB)
    ws = w_self[...]
    wn = w_neigh[...]
    first = (((0,), (0,)), ((), ()))
    last = (((1,), (1,)), ((), ()))
    preact = lax.dot_general(ws, feats, first, preferred_element_type=F32)
    preact = preact + lax.dot_general(wn, agg, first, preferred_element_type=F32)
    preact = preact + bias[...]
    sigma = 1.0 / (1.0 + jnp.exp(-preact))
    hidden[...] = (preact * sigma).astype(BF)
    slope = sigma * (1.0 + preact * (1.0 - sigma))
    grad_pre = (cot[...].astype(F32) * slope).astype(BF)
    part_self = lax.dot_general(feats, grad_pre, last, preferred_element_type=F32)
    part_neigh = lax.dot_general(agg, grad_pre, last, preferred_element_type=F32)
    ones = jnp.ones((8, TB), BF)
    part_bias = lax.dot_general(ones, grad_pre, last, preferred_element_type=F32)[0:1]
    dx_self = jnp.dot(ws, grad_pre, preferred_element_type=F32).astype(BF)
    dagg = jnp.dot(wn, grad_pre, preferred_element_type=F32).astype(BF)
    deg = degree[pl.ds(lax.axis_index("col"), 1), :].astype(F32)
    dsum = (dagg.astype(F32) / deg).astype(BF)
    two = jnp.concatenate([part_bias[:, 0:TB], part_bias[:, TB:]], axis=0)
    high = two.astype(BF).astype(F32)
    tail = jnp.concatenate([high, two - high, jnp.zeros((12, TB), F32)], axis=0).astype(BF)
    for c in range(RB):
        rows = slice(c * F_LOC, (c + 1) * F_LOC)
        out[c, 0:16] = dsum[rows]
        out[c, 16:32] = dx_self[rows]
        out[c, 32:48] = part_self[rows, 0:TB].astype(BF)
        out[c, 48:64] = part_self[rows, TB:].astype(BF)
        out[c, 64:80] = part_neigh[rows, 0:TB].astype(BF)
        out[c, 80:96] = part_neigh[rows, TB:].astype(BF)
        out[c, 96:112] = tail


def spread_kernel(recv, out):
    places = out.shape[0]
    chunk = jnp.sum(recv[:, 32:96].astype(F32), axis=0)
    tail = jnp.sum(recv[:, 96:112].astype(F32), axis=0)
    two = tail[0:2] + tail[2:4]
    high = two.astype(BF).astype(F32)
    low_half = jnp.concatenate([high, two - high, jnp.zeros((4, TB), F32)], axis=0)
    blocks = recv[:, 0:16]
    for p in range(places):
        g = p // (places // Y)
        out[p, 0:RB] = blocks
        out[p, RB] = jnp.concatenate([chunk[8 * g : 8 * g + 8], low_half], axis=0).astype(BF)


def pick_kernel(dest_own, dest_other, recv, own, other, sums):
    k = lax.axis_index("k")
    for dests, picked in ((dest_own, own), (dest_other, other)):

        def pick(s, carry, dests=dests, picked=picked):
            d = dests[s]
            mine = jnp.logical_and(d >= 0, ((d >> 3) & 1) == k)
            at = jnp.where(mine, d, 0)
            tile = recv[at >> 4, at & 7]
            picked[s] = jnp.where(mine, tile, jnp.zeros_like(tile))
            return carry

        lax.fori_loop(0, TILES_DEV, pick, 0, unroll=8)
    total = jnp.sum(recv[:, RB].astype(F32), axis=0)
    high = total.astype(BF)
    low = (total - high.astype(F32)).astype(BF)
    other[TILES_DEV] = high
    other[TILES_DEV + 1] = low
    sums[...] = high.astype(F32) + low.astype(F32)


def joined_kernel(sums, other, out, bias_out):
    given = other[TILES_DEV].astype(F32) + other[TILES_DEV + 1].astype(F32)
    total = sums[...] + given
    for p in range(out.shape[0]):
        out[p] = total[0:8]
    two = total[8:10] + total[10:12]
    bias_out[...] = two / jnp.sqrt(jnp.mean(two * two) + EPS)


def back_kernel(src, own, other, vals, recv, out, acc):
    g = pl.program_id(0)

    @pl.when(g == 0)
    def _():
        acc[...] = recv[:, 16:32].astype(F32)

    first = g * STEP
    for t in range(STEP):
        grad = own[t] + other[t]
        at = src[first + t]
        acc[at] = acc[at] + jnp.dot(grad, vals[t], preferred_element_type=F32)

    @pl.when(g == pl.num_programs(0) - 1)
    def _():
        for b in range(RB):
            out[:, b * TB : (b + 1) * TB] = acc[b].astype(BF)


def tile_back(src, own, other, vals, recv):
    return pl.pallas_call(
        back_kernel,
        out_shape=sds((F_LOC, RB * TB), BF),
        grid_spec=pltpu.PrefetchScalarGridSpec(
            num_scalar_prefetch=1,
            grid=(TILES_DEV // STEP,),
            in_specs=[
                pl.BlockSpec((STEP, F_LOC, TB), lambda g, s: (g, 0, 0)),
                pl.BlockSpec((STEP, F_LOC, TB), lambda g, s: (g, 0, 0)),
                pl.BlockSpec((STEP, TB, TB), lambda g, s: (g, 0, 0)),
                pl.BlockSpec(recv.shape, lambda g, s: (0, 0, 0)),
            ],
            out_specs=pl.BlockSpec((F_LOC, RB * TB), lambda g, s: (0, 0)),
            scratch_shapes=[pltpu.VMEM((RB, F_LOC, TB), F32)],
        ),
        compiler_params=PARAMS,
    )(src, own, other, vals, recv)


def normal_kernel(x, grad_self, grad_neigh):
    for first, out in ((0, grad_self), (32, grad_neigh)):
        part = x[:, first : first + 32]
        scale = jnp.sqrt(jnp.sum(part * part) / (RB * 32 * TB) + EPS)
        scaled = part / scale
        for c in range(RB):
            rows = slice(c * F_LOC, (c + 1) * F_LOC)
            out[rows, 0:TB] = scaled[c, 0:16]
            out[rows, TB:] = scaled[c, 16:32]


def local(
    features,
    tile_values,
    tile_source,
    tile_dest,
    tile_count,
    degree,
    w_self,
    w_neigh,
    bias,
    cotangent,
):
    places = lax.axis_size(YZ)
    swap = [(0, 1), (1, 0)]
    live = jnp.arange(TILES_DEV, dtype=jnp.int32) < tile_count[0]
    dest = jnp.where(live, tile_dest, -1)
    dest_other = lax.ppermute(dest, "k", swap)
    degree2 = degree.reshape(RB, TB)

    terms = tile_terms(tile_source, features, tile_values)
    terms_other = lax.ppermute(terms, "k", swap)
    dense = whole(
        dense_kernel,
        sds((places * RB, F_LOC, TB), BF),
        [SMEM, SMEM, VMEM, VMEM],
        [pltpu.VMEM((places * RB + 1, F_LOC, TB), F32)],
    )(dest, dest_other, terms, terms_other)
    summed = lax.all_to_all(
        dense.reshape(places, RB, F_LOC, TB), YZ, split_axis=0, concat_axis=0, tiled=True
    )
    packed = whole(agg_kernel, sds((RB, 2 * F_LOC, TB), BF), [VMEM] * 3)(
        summed, degree2, features
    )
    full = lax.all_to_all(packed, "col", split_axis=0, concat_axis=0, tiled=True)
    hidden, back = whole(
        dense_layer_kernel,
        (sds(cotangent.shape, BF), sds((RB, 112, TB), BF)),
        [VMEM] * 6,
    )(full, w_self, w_neigh, bias[:, None], cotangent, degree2)
    back = lax.all_to_all(back, "col", split_axis=0, concat_axis=0, tiled=True)
    spread = whole(spread_kernel, sds((places, RB + 1, F_LOC, TB), BF), [VMEM])(back)
    portion = lax.all_to_all(spread, YZ, split_axis=0, concat_axis=0, tiled=True)
    own, other, sums = whole(
        pick_kernel,
        (
            sds((TILES_DEV, F_LOC, TB), BF),
            sds((TILES_DEV + 2, F_LOC, TB), BF),
            sds((16, TB), F32),
        ),
        [SMEM, SMEM, VMEM],
    )(dest, dest_other, portion)
    given = lax.ppermute(other, "k", swap)
    joined, grad_bias = whole(
        joined_kernel, (sds((RB * Y, 8, TB), F32), sds((2, TB), F32)), [VMEM] * 2
    )(sums, given)
    chunks = lax.all_to_all(joined, ("col", "y"), split_axis=0, concat_axis=0, tiled=True)
    grad_x = tile_back(tile_source, own, given, tile_values, back)
    grad_self, grad_neigh = whole(
        normal_kernel, (sds(w_self.shape, F32), sds(w_self.shape, F32)), [VMEM]
    )(chunks.reshape(RB, 8 * Y, TB))
    return hidden, grad_x, grad_self, grad_neigh, grad_bias.reshape(-1)


def solution(mesh):
    vtx, col = mesh.shape["vtx"], mesh.shape["col"]
    fine = Mesh(mesh.devices.reshape(Y, vtx // (2 * Y), 2, col), AXES)
    placed = (
        P("col", VTX),
        P(VTX, None, None),
        P(VTX),
        P(VTX),
        P(VTX),
        P(VTX),
        P(),
        P(),
        P(),
        P(None, AXES),
    )
    return jax.shard_map(
        local,
        mesh=fine,
        in_specs=placed,
        out_specs=(P(None, AXES), P("col", VTX), P(), P(), P()),
        check_vma=False,
    )
```

```python
import functools

import jax
import jax.numpy as jnp
from jax import lax
from jax.experimental import pallas as pl
from jax.experimental.pallas import tpu as pltpu
from jax.sharding import Mesh
from jax.sharding import PartitionSpec as P

TB = 128
TILES_DEV = 64
RB = 8
F_LOC = 16
Y = 8
STEP = 16
EXTRA = 5

EPS = 1e-06
BF = jnp.bfloat16
F32 = jnp.float32

AXES = ("y", "zl", "k", "col")
VTX = ("y", "zl", "k")
YZ = ("y", "zl")

VMEM = pl.BlockSpec(memory_space=pltpu.VMEM)
SMEM = pl.BlockSpec(memory_space=pltpu.SMEM)
HBM = pl.BlockSpec(memory_space=pltpu.HBM)
PARAMS = pltpu.CompilerParams(vmem_limit_bytes=32 * 1024 * 1024)
FULL_PARAMS = pltpu.CompilerParams(vmem_limit_bytes=59 * 1024 * 1024)


def whole(kernel, out_shape, in_specs, scratch=(), out_specs=None, cost=None):
    many = isinstance(out_shape, (tuple, list))
    return pl.pallas_call(
        kernel,
        out_shape=out_shape,
        in_specs=in_specs,
        out_specs=out_specs or ([VMEM] * len(out_shape) if many else VMEM),
        scratch_shapes=list(scratch),
        compiler_params=PARAMS,
        cost_estimate=cost,
    )


def lasting(us):
    return pl.CostEstimate(flops=0, transcendentals=0, bytes_accessed=int(us * 3.6e6))


def sds(shape, dtype):
    return jax.ShapeDtypeStruct(shape, dtype)


def terms_kernel(
    src_h, dest_h, count_h, feats_h, vals_h, out, src, dest, count, feats, vals, sems, val_sems
):
    small = [
        pltpu.make_async_copy(a, b, sems.at[n])
        for n, (a, b) in enumerate(
            ((src_h, src), (feats_h, feats), (dest_h, dest), (count_h, count))
        )
    ]
    parts = TILES_DEV // STEP
    large = [
        pltpu.make_async_copy(
            vals_h.at[pl.ds(g * STEP, STEP)], vals.at[pl.ds(g * STEP, STEP)], val_sems.at[g]
        )
        for g in range(parts)
    ]
    for copy in small + large:
        copy.start()
    for copy in small:
        copy.wait()
    slot = lax.broadcasted_iota(jnp.int32, (16, TB), 1)
    row = lax.broadcasted_iota(jnp.int32, (16, TB), 0)
    d = jnp.concatenate([dest[...], dest[...]], axis=1)
    d = jnp.where(slot < count[0], jnp.broadcast_to(d, (16, TB)), -1)
    coded = jnp.where(row == 0, d >> 3, d & 7)
    out[TILES_DEV] = coded.astype(F32).astype(BF)
    for g in range(parts):
        large[g].wait()
        for t in range(g * STEP, (g + 1) * STEP):
            start = pl.multiple_of(src[t] * TB, TB)
            block = feats[:, pl.ds(start, TB)]
            term = lax.dot_general(
                block, vals[t], (((1,), (1,)), ((), ())), preferred_element_type=F32
            )
            out[t] = term.astype(BF)


def tile_terms(src, dest, count, feats, vals):
    return pl.pallas_call(
        terms_kernel,
        out_shape=sds((TILES_DEV + 1, F_LOC, TB), BF),
        in_specs=[HBM] * 5,
        out_specs=VMEM,
        scratch_shapes=[
            pltpu.SMEM((TILES_DEV,), jnp.int32),
            pltpu.VMEM((1, TILES_DEV), jnp.int32),
            pltpu.SMEM((1,), jnp.int32),
            pltpu.VMEM(feats.shape, BF),
            pltpu.VMEM(vals.shape, BF),
            pltpu.SemaphoreType.DMA((4,)),
            pltpu.SemaphoreType.DMA((TILES_DEV // STEP,)),
        ],
        compiler_params=FULL_PARAMS,
    )(src, dest, count, feats, vals)


def dense_kernel(dest_own, count, own, other, out, dest_other, acc, coded, sem):
    k = lax.axis_index("k")
    dump = acc.shape[0] - 1
    given = other[TILES_DEV].astype(F32)
    coded[...] = (given[0:1] * 8.0 + given[1:2]).astype(jnp.int32)
    copy = pltpu.make_async_copy(coded, dest_other, sem)
    copy.start()
    acc[...] = jnp.zeros_like(acc)

    def add_to(d, used, term):
        mine = jnp.logical_and(used, ((d >> 3) & 1) == k)
        at = jnp.where(mine, (d >> 4) * RB + (d & 7), dump)
        acc[at] = acc[at] + term.astype(F32)

    def add_own(s, carry):
        add_to(dest_own[s], s < count[0], own[s])
        return carry

    lax.fori_loop(0, TILES_DEV, add_own, 0, unroll=8)
    copy.wait()

    def add_other(s, carry):
        d = dest_other[0, s]
        add_to(d, d >= 0, other[s])
        return carry

    lax.fori_loop(0, TILES_DEV, add_other, 0, unroll=8)
    out[...] = acc[0:dump].astype(BF)


def agg_kernel(recv, degree, feats, out):
    for b in range(RB):
        total = jnp.sum(recv[:, b].astype(F32), axis=0)
        deg = degree[b : b + 1, :].astype(F32)
        out[b, 0:F_LOC] = (total / deg).astype(BF)
        out[b, F_LOC : 2 * F_LOC] = feats[:, b * TB : (b + 1) * TB]


def dense_layer_kernel(recv, w_self, w_neigh, bias, cot, degree, hidden, out):
    agg = recv[:, 0:F_LOC].reshape(RB * F_LOC, TB)
    feats = recv[:, F_LOC : 2 * F_LOC].reshape(RB * F_LOC, TB)
    ws = w_self[...]
    wn = w_neigh[...]
    first = (((0,), (0,)), ((), ()))
    last = (((1,), (1,)), ((), ()))
    preact = lax.dot_general(ws, feats, first, preferred_element_type=F32)
    preact = preact + lax.dot_general(wn, agg, first, preferred_element_type=F32)
    preact = preact + jnp.broadcast_to(bias[...], (TB, bias.shape[1])).T
    sigma = 1.0 / (1.0 + jnp.exp(-preact))
    hidden[...] = (preact * sigma).astype(BF)
    slope = sigma * (1.0 + preact * (1.0 - sigma))
    grad_pre = (cot[...].astype(F32) * slope).astype(BF)
    part_self = lax.dot_general(feats, grad_pre, last, preferred_element_type=F32)
    part_neigh = lax.dot_general(agg, grad_pre, last, preferred_element_type=F32)
    ones = jnp.ones((8, TB), BF)
    part_bias = lax.dot_general(ones, grad_pre, last, preferred_element_type=F32)[0:1]
    dx_self = jnp.dot(ws, grad_pre, preferred_element_type=F32).astype(BF)
    dagg = jnp.dot(wn, grad_pre, preferred_element_type=F32).astype(BF)
    deg = degree[pl.ds(lax.axis_index("col"), 1), :].astype(F32)
    dsum = (dagg.astype(F32) / deg).astype(BF)
    two = jnp.concatenate([part_bias[:, 0:TB], part_bias[:, TB:]], axis=0)
    high = two.astype(BF).astype(F32)
    tail = jnp.concatenate([high, two - high, jnp.zeros((12, TB), F32)], axis=0).astype(BF)
    for c in range(RB):
        rows = slice(c * F_LOC, (c + 1) * F_LOC)
        out[c, 0:16] = dsum[rows]
        out[c, 16:32] = dx_self[rows]
        out[c, 32:48] = part_self[rows, 0:TB].astype(BF)
        out[c, 48:64] = part_self[rows, TB:].astype(BF)
        out[c, 64:80] = part_neigh[rows, 0:TB].astype(BF)
        out[c, 80:96] = part_neigh[rows, TB:].astype(BF)
        out[c, 96:112] = tail


def parted(tail):
    two = tail[0:2] + tail[2:4]
    high = two.astype(BF).astype(F32)
    return jnp.concatenate([high, two - high, jnp.zeros((12, TB), F32)], axis=0).astype(BF)


def first_step_kernel(recv, out):
    blocks = recv[:, 0:F_LOC]
    sums = jnp.sum(recv[:, 32:96].astype(F32), axis=0).astype(BF)
    tail = parted(jnp.sum(recv[:, 96:112].astype(F32), axis=0))
    for p in range(out.shape[0]):
        out[p, 0:RB] = blocks
        for n in range(4):
            out[p, RB + n] = sums[n * F_LOC : (n + 1) * F_LOC]
        out[p, RB + 4] = tail


def second_step_kernel(recv, out):
    came = recv.shape[0]
    sums = [jnp.sum(recv[:, RB + n].astype(F32), axis=0) for n in range(EXTRA)]
    sums = [x.astype(BF) for x in sums[:4]] + [parted(sums[4])]
    for p in range(out.shape[0]):
        for q in range(came):
            out[p, q * RB : (q + 1) * RB] = recv[q, 0:RB]
        for n in range(EXTRA):
            out[p, came * RB + n] = sums[n]


def share_kernel(first, recv, out, bias_out):
    sums = [jnp.sum(recv[:, first + n].astype(F32), axis=0) for n in range(EXTRA)]
    for p in range(out.shape[0]):
        for n in range(4):
            out[p, n * F_LOC : (n + 1) * F_LOC] = sums[n].astype(BF)
    bias_out[...] = parted(sums[4])


def pick_kernel(ny, nz, dest_own, count, dest_other, recv, bias_sum, own, other):
    k = lax.axis_index("k")
    of_y = jnp.where(k == 0, nz * RB + EXTRA, RB)
    of_z = jnp.where(k == 0, RB, ny * (nz * RB + EXTRA) // nz)

    def pick(d, used):
        mine = jnp.logical_and(used, ((d >> 3) & 1) == k)
        d = jnp.where(mine, d, 0)
        place = d >> 4
        at = (place // nz) * of_y + (place % nz) * of_z + (d & 7)
        tile = recv[at]
        return jnp.where(mine, tile, jnp.zeros_like(tile))

    def step(s, carry):
        own[s] = pick(dest_own[s], s < count[0])
        d = dest_other[0, s]
        other[s] = pick(d, d >= 0)
        return carry

    lax.fori_loop(0, TILES_DEV, step, 0, unroll=8)
    other[TILES_DEV] = bias_sum[...]


def back_kernel(src, own, given, recv, vals, out, acc):
    g = pl.program_id(0)

    @pl.when(g == 0)
    def _():
        acc[...] = recv[:, F_LOC : 2 * F_LOC].astype(F32)

    first = g * STEP
    for t in range(STEP):
        grad = own[t] + given[t]
        at = src[first + t]
        acc[at] = acc[at] + jnp.dot(grad, vals[t], preferred_element_type=F32)

    @pl.when(g == pl.num_programs(0) - 1)
    def _():
        for b in range(RB):
            out[:, b * TB : (b + 1) * TB] = acc[b].astype(BF)


def tile_back(src, own, given, recv, vals):
    tiles = pl.BlockSpec((STEP, F_LOC, TB), lambda g, s: (g, 0, 0))
    return pl.pallas_call(
        back_kernel,
        out_shape=sds((F_LOC, RB * TB), BF),
        grid_spec=pltpu.PrefetchScalarGridSpec(
            num_scalar_prefetch=1,
            grid=(TILES_DEV // STEP,),
            in_specs=[
                tiles,
                tiles,
                pl.BlockSpec(recv.shape, lambda g, s: (0, 0, 0)),
                pl.BlockSpec((STEP, TB, TB), lambda g, s: (g, 0, 0)),
            ],
            out_specs=pl.BlockSpec((F_LOC, RB * TB), lambda g, s: (0, 0)),
            scratch_shapes=[pltpu.VMEM((RB, F_LOC, TB), F32)],
        ),
        compiler_params=PARAMS,
        cost_estimate=lasting(2.2),
    )(src, own, given, recv, vals)


def normal_kernel(x, bias_sum, given, grad_self, grad_neigh, grad_bias):
    for first, out in ((0, grad_self), (32, grad_neigh)):
        rows = slice(first, first + 32)
        part = x[0:RB, rows].astype(F32) + x[RB : 2 * RB, rows].astype(F32)
        scale = jnp.sqrt(jnp.sum(part * part) / (RB * 32 * TB) + EPS)
        scaled = part / scale
        for c in range(RB):
            at = slice(c * F_LOC, (c + 1) * F_LOC)
            out[at, 0:TB] = scaled[c, 0:16]
            out[at, TB:] = scaled[c, 16:32]
    mine = bias_sum[...].astype(F32)
    theirs = given[TILES_DEV].astype(F32)
    two = (mine[0:2] + mine[2:4]) + (theirs[0:2] + theirs[2:4])
    grad_bias[...] = two / jnp.sqrt(jnp.mean(two * two) + EPS)


def local(
    features,
    tile_values,
    tile_source,
    tile_dest,
    tile_count,
    degree,
    w_self,
    w_neigh,
    bias,
    cotangent,
):
    places = lax.axis_size(YZ)
    swap = [(0, 1), (1, 0)]
    degree2 = degree.reshape(RB, TB)

    terms = tile_terms(
        tile_source, tile_dest.reshape(1, -1), tile_count, features, tile_values
    )
    terms_other = lax.ppermute(terms, "k", swap)
    dense, dest_other = whole(
        dense_kernel,
        (sds((places * RB, F_LOC, TB), BF), sds((1, TB), jnp.int32)),
        [SMEM, SMEM, VMEM, VMEM],
        [
            pltpu.VMEM((places * RB + 1, F_LOC, TB), F32),
            pltpu.VMEM((1, TB), jnp.int32),
            pltpu.SemaphoreType.DMA,
        ],
        [VMEM, SMEM],
    )(tile_dest, tile_count, terms, terms_other)
    summed = lax.all_to_all(
        dense.reshape(places, RB, F_LOC, TB), YZ, split_axis=0, concat_axis=0, tiled=True
    )
    packed = whole(agg_kernel, sds((RB, 2 * F_LOC, TB), BF), [VMEM] * 3)(
        summed, degree2, features
    )
    full = lax.all_to_all(packed, "col", split_axis=0, concat_axis=0, tiled=True)
    hidden, back = whole(
        dense_layer_kernel,
        (sds(cotangent.shape, BF), sds((RB, 112, TB), BF)),
        [VMEM] * 6,
    )(full, w_self, w_neigh, bias.reshape(1, -1), cotangent, degree2)
    back = lax.all_to_all(back, "col", split_axis=0, concat_axis=0, tiled=True)

    ny, nz = lax.axis_size("y"), lax.axis_size("zl")
    tiles = ny * (nz * RB + EXTRA)

    def in_two_steps(first, second):
        def run(back):
            n1, n2 = lax.axis_size(first), lax.axis_size(second)
            one = whole(first_step_kernel, sds((n1, RB + EXTRA, F_LOC, TB), BF), [VMEM])(back)
            one = lax.all_to_all(one, first, split_axis=0, concat_axis=0, tiled=True)
            two = whole(second_step_kernel, sds((n2, tiles // n2, F_LOC, TB), BF), [VMEM])(one)
            two = lax.all_to_all(two, second, split_axis=0, concat_axis=0, tiled=True)
            share, bias_sum = whole(
                functools.partial(share_kernel, n1 * RB),
                (sds((2 * RB, 64, TB), BF), sds((F_LOC, TB), BF)),
                [VMEM],
            )(two)
            return two.reshape(tiles, F_LOC, TB), share, bias_sum

        return run

    portion, share, bias_sum = lax.cond(
        lax.axis_index("k") == 0, in_two_steps("zl", "y"), in_two_steps("y", "zl"), back
    )
    chunks = lax.all_to_all(share, ("k", "col"), split_axis=0, concat_axis=0, tiled=True)
    own, other = whole(
        functools.partial(pick_kernel, ny, nz),
        (sds((TILES_DEV, F_LOC, TB), BF), sds((TILES_DEV + 1, F_LOC, TB), BF)),
        [SMEM, SMEM, SMEM, VMEM, VMEM],
        cost=lasting(1.2),
    )(tile_dest, tile_count, dest_other, portion, bias_sum)
    given = lax.ppermute(other, "k", swap)
    grad_x = tile_back(tile_source, own, given, back, tile_values)
    grad_self, grad_neigh, grad_bias = whole(
        normal_kernel,
        (sds(w_self.shape, F32), sds(w_self.shape, F32), sds((2, TB), F32)),
        [VMEM] * 3,
    )(chunks, bias_sum, given)
    return hidden, grad_x, grad_self, grad_neigh, grad_bias.reshape(-1)


def solution(mesh):
    vtx, col = mesh.shape["vtx"], mesh.shape["col"]
    fine = Mesh(mesh.devices.reshape(Y, vtx // (2 * Y), 2, col), AXES)
    placed = (
        P("col", VTX),
        P(VTX, None, None),
        P(VTX),
        P(VTX),
        P(VTX),
        P(VTX),
        P(),
        P(),
        P(),
        P(None, AXES),
    )
    return jax.shard_map(
        local,
        mesh=fine,
        in_specs=placed,
        out_specs=(P(None, AXES), P("col", VTX), P(), P(), P()),
        check_vma=False,
    )
```

```python
import functools

import jax
import jax.numpy as jnp
from jax import lax
from jax.experimental import pallas as pl
from jax.experimental.pallas import tpu as pltpu
from jax.sharding import Mesh
from jax.sharding import PartitionSpec as P

TB = 128
TILES_DEV = 64
RB = 8
F_LOC = 16
Y = 8
NX = 4
STEP = 16
EXTRA = 5

EPS = 1e-06
BF = jnp.bfloat16
F32 = jnp.float32

AXES = ("y", "zl", "k", "zh", "x")
COL = ("zh", "x")
VTX = ("y", "zl", "k")

VMEM = pl.BlockSpec(memory_space=pltpu.VMEM)
SMEM = pl.BlockSpec(memory_space=pltpu.SMEM)
HBM = pl.BlockSpec(memory_space=pltpu.HBM)
ANY = pl.BlockSpec(memory_space=pl.ANY)
PARAMS = pltpu.CompilerParams(vmem_limit_bytes=32 * 1024 * 1024)
FULL_PARAMS = pltpu.CompilerParams(vmem_limit_bytes=59 * 1024 * 1024)


def whole(kernel, out_shape, in_specs, scratch=(), out_specs=None, cost=None):
    many = isinstance(out_shape, (tuple, list))
    return pl.pallas_call(
        kernel,
        out_shape=out_shape,
        in_specs=in_specs,
        out_specs=out_specs or ([VMEM] * len(out_shape) if many else VMEM),
        scratch_shapes=list(scratch),
        compiler_params=PARAMS,
        cost_estimate=cost,
    )


def lasting(us):
    return pl.CostEstimate(flops=0, transcendentals=0, bytes_accessed=int(us * 3.6e6))


def sds(shape, dtype):
    return jax.ShapeDtypeStruct(shape, dtype)


def terms_kernel(
    src_h, dest_h, count_h, feats_h, vals_h, out, src, dest, count, feats, vals, sems, val_sems
):
    small = [
        pltpu.make_async_copy(a, b, sems.at[n])
        for n, (a, b) in enumerate(
            ((src_h, src), (feats_h, feats), (dest_h, dest), (count_h, count))
        )
    ]
    parts = TILES_DEV // STEP
    large = [
        pltpu.make_async_copy(
            vals_h.at[pl.ds(g * STEP, STEP)], vals.at[pl.ds(g * STEP, STEP)], val_sems.at[g]
        )
        for g in range(parts)
    ]
    for copy in small + large:
        copy.start()
    for copy in small:
        copy.wait()
    slot = lax.broadcasted_iota(jnp.int32, (16, TB), 1)
    row = lax.broadcasted_iota(jnp.int32, (16, TB), 0)
    d = jnp.concatenate([dest[...], dest[...]], axis=1)
    d = jnp.where(slot < count[0], jnp.broadcast_to(d, (16, TB)), -1)
    coded = jnp.where(row == 0, d >> 3, d & 7)
    out[TILES_DEV] = coded.astype(F32).astype(BF)
    for g in range(parts):
        large[g].wait()
        for t in range(g * STEP, (g + 1) * STEP):
            start = pl.multiple_of(src[t] * TB, TB)
            block = feats[:, pl.ds(start, TB)]
            term = lax.dot_general(
                block, vals[t], (((1,), (1,)), ((), ())), preferred_element_type=F32
            )
            out[t] = term.astype(BF)


def tile_terms(src, dest, count, feats, vals):
    return pl.pallas_call(
        terms_kernel,
        out_shape=sds((TILES_DEV + 1, F_LOC, TB), BF),
        in_specs=[HBM] * 5,
        out_specs=VMEM,
        scratch_shapes=[
            pltpu.SMEM((TILES_DEV,), jnp.int32),
            pltpu.VMEM((1, TILES_DEV), jnp.int32),
            pltpu.SMEM((1,), jnp.int32),
            pltpu.VMEM(feats.shape, BF),
            pltpu.VMEM(vals.shape, BF),
            pltpu.SemaphoreType.DMA((4,)),
            pltpu.SemaphoreType.DMA((TILES_DEV // STEP,)),
        ],
        compiler_params=FULL_PARAMS,
    )(src, dest, count, feats, vals)


def dense_kernel(ny, nz, dest_own, count, own, other, feats, out, dest_other, acc, coded, sem):
    k = lax.axis_index("k")
    size = ny * NX + NX
    of_y = jnp.where(k == 0, NX, 2 * nz * size // ny)
    of_z = jnp.where(k == 0, size, RB)
    of_zh = jnp.where(k == 0, nz * size, NX)
    dump = acc.shape[0] - 1
    given = other[TILES_DEV].astype(F32)
    coded[...] = (given[0:1] * 8.0 + given[1:2]).astype(jnp.int32)
    copy = pltpu.make_async_copy(coded, dest_other, sem)
    copy.start()
    acc[...] = jnp.zeros_like(acc)

    def add_to(d, used, term):
        mine = jnp.logical_and(used, ((d >> 3) & 1) == k)
        place = d >> 4
        at = (place // nz) * of_y + (place % nz) * of_z
        at = at + ((d & 7) // NX) * of_zh + (d & 7) % NX
        at = jnp.where(mine, at, dump)
        acc[at] = acc[at] + term.astype(F32)

    def add_own(s, carry):
        add_to(dest_own[s], s < count[0], own[s])
        return carry

    lax.fori_loop(0, TILES_DEV, add_own, 0, unroll=8)
    copy.wait()

    def add_other(s, carry):
        d = dest_other[0, s]
        add_to(d, d >= 0, other[s])
        return carry

    lax.fori_loop(0, TILES_DEV, add_other, 0, unroll=8)
    out[...] = acc[0:dump].astype(BF)

    @pl.when(k == 0)
    def _():
        for m in range(2 * nz):
            for x in range(NX):
                b = (m // nz) * NX + x
                out[m * size + ny * NX + x] = feats[:, b * TB : (b + 1) * TB]


def middle_first_kernel(nz, recv, out):
    ny = out.shape[0] // NX
    here = lax.axis_index("zl")
    for h in range(2):
        for n in range(ny * NX):
            total = recv[h * nz, n].astype(F32)
            for z in range(1, nz):
                total = total + recv[h * nz + z, n].astype(F32)
            out[n, h * F_LOC : (h + 1) * F_LOC] = total.astype(BF)
        for x in range(NX):
            tile = recv[h * nz + here, ny * NX + x]
            for y in range(ny):
                out[y * NX + x, (2 + h) * F_LOC : (3 + h) * F_LOC] = tile


def middle_second_kernel(recv, feats, out):
    places = out.shape[0] // RB
    for b in range(RB):
        own = feats[:, b * TB : (b + 1) * TB]
        for p in range(places):
            total = jnp.sum(recv[:, p * RB + b].astype(F32), axis=0)
            out[p * RB + b, 0:F_LOC] = total.astype(BF)
            out[p * RB + b, F_LOC : 2 * F_LOC] = own


def agg_kernel(first_core, recv, degree, out):
    halves = 2 if first_core else 1
    size = RB // halves
    places = recv.shape[0] // size
    here = lax.axis_index("y" if first_core else "zl") * size
    deg = degree[pl.ds(lax.axis_index(COL), 1), :].astype(F32)
    for c in range(RB):
        h, n = c // size, c % size
        rows = slice(h * F_LOC, (h + 1) * F_LOC)
        total = recv[n, rows].astype(F32)
        for p in range(1, places):
            total = total + recv[p * size + n, rows].astype(F32)
        out[c, 0:F_LOC] = (total / deg).astype(BF)
        rows = slice((halves + h) * F_LOC, (halves + h + 1) * F_LOC)
        out[c, F_LOC : 2 * F_LOC] = recv[here + n, rows]


def dense_layer_kernel(recv, w_self, w_neigh, bias, cot, degree, hidden, out):
    agg = recv[:, 0:F_LOC].reshape(RB * F_LOC, TB)
    feats = recv[:, F_LOC : 2 * F_LOC].reshape(RB * F_LOC, TB)
    ws = w_self[...]
    wn = w_neigh[...]
    first = (((0,), (0,)), ((), ()))
    last = (((1,), (1,)), ((), ()))
    preact = lax.dot_general(ws, feats, first, preferred_element_type=F32)
    preact = preact + lax.dot_general(wn, agg, first, preferred_element_type=F32)
    preact = preact + jnp.broadcast_to(bias[...], (TB, bias.shape[1])).T
    sigma = 1.0 / (1.0 + jnp.exp(-preact))
    hidden[...] = (preact * sigma).astype(BF)
    slope = sigma * (1.0 + preact * (1.0 - sigma))
    grad_pre = (cot[...].astype(F32) * slope).astype(BF)
    part_self = lax.dot_general(feats, grad_pre, last, preferred_element_type=F32)
    part_neigh = lax.dot_general(agg, grad_pre, last, preferred_element_type=F32)
    ones = jnp.ones((8, TB), BF)
    part_bias = lax.dot_general(ones, grad_pre, last, preferred_element_type=F32)[0:1]
    dx_self = jnp.dot(ws, grad_pre, preferred_element_type=F32).astype(BF)
    dagg = jnp.dot(wn, grad_pre, preferred_element_type=F32).astype(BF)
    deg = degree[pl.ds(lax.axis_index(COL), 1), :].astype(F32)
    dsum = (dagg.astype(F32) / deg).astype(BF)
    two = jnp.concatenate([part_bias[:, 0:TB], part_bias[:, TB:]], axis=0)
    high = two.astype(BF).astype(F32)
    tail = jnp.concatenate([high, two - high, jnp.zeros((12, TB), F32)], axis=0).astype(BF)
    for c in range(RB):
        rows = slice(c * F_LOC, (c + 1) * F_LOC)
        out[c, 0:16] = dsum[rows]
        out[c, 16:32] = dx_self[rows]
        out[c, 32:48] = part_self[rows, 0:TB].astype(BF)
        out[c, 48:64] = part_self[rows, TB:].astype(BF)
        out[c, 64:80] = part_neigh[rows, 0:TB].astype(BF)
        out[c, 80:96] = part_neigh[rows, TB:].astype(BF)
        out[c, 96:112] = tail


def parted(tail):
    two = tail[0:2] + tail[2:4]
    high = two.astype(BF).astype(F32)
    return jnp.concatenate([high, two - high, jnp.zeros((12, TB), F32)], axis=0).astype(BF)


def first_step_kernel(recv, out):
    blocks = recv[:, 0:F_LOC]
    sums = jnp.sum(recv[:, 32:96].astype(F32), axis=0).astype(BF)
    tail = parted(jnp.sum(recv[:, 96:112].astype(F32), axis=0))
    for p in range(out.shape[0]):
        out[p, 0:RB] = blocks
        for n in range(4):
            out[p, RB + n] = sums[n * F_LOC : (n + 1) * F_LOC]
        out[p, RB + 4] = tail


def second_step_kernel(recv, out):
    came = recv.shape[0]
    sums = [jnp.sum(recv[:, RB + n].astype(F32), axis=0) for n in range(EXTRA)]
    sums = [x.astype(BF) for x in sums[:4]] + [parted(sums[4])]
    for p in range(out.shape[0]):
        for q in range(came):
            out[p, q * RB : (q + 1) * RB] = recv[q, 0:RB]
        for n in range(EXTRA):
            out[p, came * RB + n] = sums[n]


def share_kernel(first, recv_h, out, bias_out, recv, sems):
    copies = [
        pltpu.make_async_copy(recv_h.at[p, pl.ds(first, EXTRA)], recv.at[p], sems.at[p])
        for p in range(recv.shape[0])
    ]
    for copy in copies:
        copy.start()
    for copy in copies:
        copy.wait()
    sums = [jnp.sum(recv[:, n].astype(F32), axis=0) for n in range(EXTRA)]
    rows = [x.astype(BF) for x in sums[:4]]
    for p in range(out.shape[0]):
        for n in range(4):
            out[p, n * F_LOC : (n + 1) * F_LOC] = rows[n]
    bias_out[...] = parted(sums[4])


def pick_kernel(ny, nz, dest_own, count, dest_other, recv, bias_sum, own, other):
    k = lax.axis_index("k")
    of_y = jnp.where(k == 0, nz * RB + EXTRA, RB)
    of_z = jnp.where(k == 0, RB, ny * (nz * RB + EXTRA) // nz)

    def pick(d, used):
        mine = jnp.logical_and(used, ((d >> 3) & 1) == k)
        d = jnp.where(mine, d, 0)
        place = d >> 4
        at = (place // nz) * of_y + (place % nz) * of_z + (d & 7)
        tile = recv[at]
        return jnp.where(mine, tile, jnp.zeros_like(tile))

    def step(s, carry):
        own[s] = pick(dest_own[s], s < count[0])
        d = dest_other[0, s]
        other[s] = pick(d, d >= 0)
        return carry

    lax.fori_loop(0, TILES_DEV, step, 0, unroll=8)
    other[TILES_DEV] = bias_sum[...]


def back_kernel(src, own, given, recv, vals, out, acc):
    g = pl.program_id(0)

    @pl.when(g == 0)
    def _():
        acc[...] = recv[:, F_LOC : 2 * F_LOC].astype(F32)

    first = g * STEP
    for t in range(STEP):
        grad = own[t] + given[t]
        at = src[first + t]
        acc[at] = acc[at] + jnp.dot(grad, vals[t], preferred_element_type=F32)

    @pl.when(g == pl.num_programs(0) - 1)
    def _():
        for b in range(RB):
            out[:, b * TB : (b + 1) * TB] = acc[b].astype(BF)


def tile_back(src, own, given, recv, vals):
    tiles = pl.BlockSpec((STEP, F_LOC, TB), lambda g, s: (g, 0, 0))
    return pl.pallas_call(
        back_kernel,
        out_shape=sds((F_LOC, RB * TB), BF),
        grid_spec=pltpu.PrefetchScalarGridSpec(
            num_scalar_prefetch=1,
            grid=(TILES_DEV // STEP,),
            in_specs=[
                tiles,
                tiles,
                pl.BlockSpec(recv.shape, lambda g, s: (0, 0, 0)),
                pl.BlockSpec((STEP, TB, TB), lambda g, s: (g, 0, 0)),
            ],
            out_specs=pl.BlockSpec((F_LOC, RB * TB), lambda g, s: (0, 0)),
            scratch_shapes=[pltpu.VMEM((RB, F_LOC, TB), F32)],
        ),
        compiler_params=PARAMS,
        cost_estimate=lasting(2.2),
    )(src, own, given, recv, vals)


def normal_kernel(x, bias_sum, given, grad_self, grad_neigh, grad_bias):
    for first, out in ((0, grad_self), (32, grad_neigh)):
        rows = slice(first, first + 32)
        part = x[0:RB, rows].astype(F32) + x[RB : 2 * RB, rows].astype(F32)
        scale = jnp.sqrt(jnp.sum(part * part) / (RB * 32 * TB) + EPS)
        scaled = part / scale
        for c in range(RB):
            at = slice(c * F_LOC, (c + 1) * F_LOC)
            out[at, 0:TB] = scaled[c, 0:16]
            out[at, TB:] = scaled[c, 16:32]
    mine = bias_sum[...].astype(F32)
    theirs = given[TILES_DEV].astype(F32)
    two = (mine[0:2] + mine[2:4]) + (theirs[0:2] + theirs[2:4])
    grad_bias[...] = two / jnp.sqrt(jnp.mean(two * two) + EPS)


def local(
    features,
    tile_values,
    tile_source,
    tile_dest,
    tile_count,
    degree,
    w_self,
    w_neigh,
    bias,
    cotangent,
):
    ny, nz = lax.axis_size("y"), lax.axis_size("zl")
    swap = [(0, 1), (1, 0)]
    degree2 = degree.reshape(RB, TB)

    terms = tile_terms(
        tile_source, tile_dest.reshape(1, -1), tile_count, features, tile_values
    )
    terms_other = lax.ppermute(terms, "k", swap)
    sent = 2 * nz * (ny + 1) * NX
    dense, dest_other = whole(
        functools.partial(dense_kernel, ny, nz),
        (sds((sent, F_LOC, TB), BF), sds((1, TB), jnp.int32)),
        [SMEM, SMEM, VMEM, VMEM, VMEM],
        [
            pltpu.VMEM((sent + 1, F_LOC, TB), F32),
            pltpu.VMEM((1, TB), jnp.int32),
            pltpu.SemaphoreType.DMA,
        ],
        [VMEM, SMEM],
    )(tile_dest, tile_count, terms, terms_other, features)

    def exchange(array, axes):
        return lax.all_to_all(array, axes, split_axis=0, concat_axis=0, tiled=True)

    def first_collect(dense, features, degree2):
        one = exchange(dense.reshape(2 * nz, (ny + 1) * NX, F_LOC, TB), ("zh", "zl"))
        two = whole(
            functools.partial(middle_first_kernel, nz),
            sds((ny * NX, 4 * F_LOC, TB), BF),
            [VMEM],
        )(one)
        two = exchange(two, ("y", "x"))
        return whole(
            functools.partial(agg_kernel, True), sds((RB, 2 * F_LOC, TB), BF), [VMEM] * 2
        )(two, degree2)

    def second_collect(dense, features, degree2):
        one = exchange(dense.reshape(ny, sent // ny, F_LOC, TB), "y")
        two = whole(middle_second_kernel, sds((nz * RB, 2 * F_LOC, TB), BF), [VMEM] * 2)(
            one, features
        )
        two = exchange(two, ("zl",) + COL)
        return whole(
            functools.partial(agg_kernel, False), sds((RB, 2 * F_LOC, TB), BF), [VMEM] * 2
        )(two, degree2)

    full = lax.cond(
        lax.axis_index("k") == 0, first_collect, second_collect, dense, features, degree2
    )
    hidden, back = whole(
        dense_layer_kernel,
        (sds(cotangent.shape, BF), sds((RB, 112, TB), BF)),
        [VMEM] * 6,
    )(full, w_self, w_neigh, bias.reshape(1, -1), cotangent, degree2)
    back = exchange(back, COL)

    tiles = ny * (nz * RB + EXTRA)

    def in_two_steps(first, second):
        def run(back):
            n1, n2 = lax.axis_size(first), lax.axis_size(second)
            one = whole(first_step_kernel, sds((n1, RB + EXTRA, F_LOC, TB), BF), [VMEM])(back)
            one = exchange(one, first)
            two = whole(second_step_kernel, sds((n2, tiles // n2, F_LOC, TB), BF), [VMEM])(one)
            two = exchange(two, second)
            share, bias_sum = whole(
                functools.partial(share_kernel, n1 * RB),
                (sds((2 * RB, 64, TB), BF), sds((F_LOC, TB), BF)),
                [ANY],
                [pltpu.VMEM((n2, EXTRA, F_LOC, TB), BF), pltpu.SemaphoreType.DMA((n2,))],
            )(two)
            return two.reshape(tiles, F_LOC, TB), share, bias_sum

        return run

    portion, share, bias_sum = lax.cond(
        lax.axis_index("k") == 0, in_two_steps("zl", "y"), in_two_steps("y", "zl"), back
    )
    chunks = exchange(share, ("k",) + COL)
    own, other = whole(
        functools.partial(pick_kernel, ny, nz),
        (sds((TILES_DEV, F_LOC, TB), BF), sds((TILES_DEV + 1, F_LOC, TB), BF)),
        [SMEM, SMEM, SMEM, VMEM, VMEM],
        cost=lasting(1.2),
    )(tile_dest, tile_count, dest_other, portion, bias_sum)
    given = lax.ppermute(other, "k", swap)
    grad_x = tile_back(tile_source, own, given, back, tile_values)
    grad_self, grad_neigh, grad_bias = whole(
        normal_kernel,
        (sds(w_self.shape, F32), sds(w_self.shape, F32), sds((2, TB), F32)),
        [VMEM] * 3,
    )(chunks, bias_sum, given)
    return hidden, grad_x, grad_self, grad_neigh, grad_bias.reshape(-1)


def solution(mesh):
    vtx, col = mesh.shape["vtx"], mesh.shape["col"]
    fine = Mesh(mesh.devices.reshape(Y, vtx // (2 * Y), 2, 2, col // 2), AXES)
    placed = (
        P(COL, VTX),
        P(VTX, None, None),
        P(VTX),
        P(VTX),
        P(VTX),
        P(VTX),
        P(),
        P(),
        P(),
        P(None, AXES),
    )
    return jax.shard_map(
        local,
        mesh=fine,
        in_specs=placed,
        out_specs=(P(None, AXES), P(COL, VTX), P(), P(), P()),
        check_vma=False,
    )
```

```python
import functools

import jax
import jax.numpy as jnp
from jax import lax
from jax.experimental import pallas as pl
from jax.experimental.pallas import tpu as pltpu
from jax.sharding import Mesh
from jax.sharding import PartitionSpec as P

TB = 128
TILES_DEV = 64
RB = 8
F_LOC = 16
Y = 8
NX = 4
STEP = 16
EXTRA = 5

EPS = 1e-06
BF = jnp.bfloat16
F32 = jnp.float32

AXES = ("y", "zl", "k", "zh", "x")
COL = ("zh", "x")
VTX = ("y", "zl", "k")

VMEM = pl.BlockSpec(memory_space=pltpu.VMEM)
SMEM = pl.BlockSpec(memory_space=pltpu.SMEM)
HBM = pl.BlockSpec(memory_space=pltpu.HBM)
ANY = pl.BlockSpec(memory_space=pl.ANY)
PARAMS = pltpu.CompilerParams(vmem_limit_bytes=32 * 1024 * 1024)
FULL_PARAMS = pltpu.CompilerParams(vmem_limit_bytes=59 * 1024 * 1024)


def whole(kernel, out_shape, in_specs, scratch=(), out_specs=None, cost=None):
    many = isinstance(out_shape, (tuple, list))
    return pl.pallas_call(
        kernel,
        out_shape=out_shape,
        in_specs=in_specs,
        out_specs=out_specs or ([VMEM] * len(out_shape) if many else VMEM),
        scratch_shapes=list(scratch),
        compiler_params=PARAMS,
        cost_estimate=cost,
    )


def lasting(us):
    return pl.CostEstimate(flops=0, transcendentals=0, bytes_accessed=int(us * 3.6e6))


def sds(shape, dtype):
    return jax.ShapeDtypeStruct(shape, dtype)


def terms_kernel(
    src_h, dest_h, count_h, feats_h, vals_h, out, src, dest, count, feats, vals, sems, val_sems
):
    small = [
        pltpu.make_async_copy(a, b, sems.at[n])
        for n, (a, b) in enumerate(
            ((src_h, src), (feats_h, feats), (dest_h, dest), (count_h, count))
        )
    ]
    parts = TILES_DEV // STEP
    large = [
        pltpu.make_async_copy(
            vals_h.at[pl.ds(g * STEP, STEP)], vals.at[pl.ds(g * STEP, STEP)], val_sems.at[g]
        )
        for g in range(parts)
    ]
    for copy in small + large:
        copy.start()
    for copy in small:
        copy.wait()
    slot = lax.broadcasted_iota(jnp.int32, (16, TB), 1)
    row = lax.broadcasted_iota(jnp.int32, (16, TB), 0)
    d = jnp.concatenate([dest[...], dest[...]], axis=1)
    d = jnp.where(slot < count[0], jnp.broadcast_to(d, (16, TB)), -1)
    coded = jnp.where(row == 0, d >> 3, d & 7)
    out[TILES_DEV] = coded.astype(F32).astype(BF)
    for g in range(parts):
        large[g].wait()
        for t in range(g * STEP, (g + 1) * STEP):
            start = pl.multiple_of(src[t] * TB, TB)
            block = feats[:, pl.ds(start, TB)]
            term = lax.dot_general(
                block, vals[t], (((1,), (1,)), ((), ())), preferred_element_type=F32
            )
            out[t] = term.astype(BF)


def tile_terms(src, dest, count, feats, vals):
    return pl.pallas_call(
        terms_kernel,
        out_shape=sds((TILES_DEV + 1, F_LOC, TB), BF),
        in_specs=[HBM] * 5,
        out_specs=VMEM,
        scratch_shapes=[
            pltpu.SMEM((TILES_DEV,), jnp.int32),
            pltpu.VMEM((1, TILES_DEV), jnp.int32),
            pltpu.SMEM((1,), jnp.int32),
            pltpu.VMEM(feats.shape, BF),
            pltpu.VMEM(vals.shape, BF),
            pltpu.SemaphoreType.DMA((4,)),
            pltpu.SemaphoreType.DMA((TILES_DEV // STEP,)),
        ],
        compiler_params=FULL_PARAMS,
    )(src, dest, count, feats, vals)


def dense_kernel(ny, nz, dest_own, count, own, other, feats, out, dest_other, acc, coded, sem):
    k = lax.axis_index("k")
    size = ny * NX + NX
    of_y = jnp.where(k == 1, NX, 2 * nz * size // ny)
    of_z = jnp.where(k == 1, size, RB)
    of_zh = jnp.where(k == 1, nz * size, NX)
    bits = nz.bit_length() - 1
    dump = acc.shape[0] - 1
    given = other[TILES_DEV].astype(F32)
    coded[...] = (given[0:1] * 8.0 + given[1:2]).astype(jnp.int32)
    copy = pltpu.make_async_copy(coded, dest_other, sem)
    copy.start()
    acc[...] = jnp.zeros_like(acc)

    def add_to(d, used, term):
        mine = jnp.logical_and(used, ((d >> 3) & 1) == k)
        at = (d >> (4 + bits)) * of_y + ((d >> 4) & (nz - 1)) * of_z
        at = at + ((d >> 2) & 1) * of_zh + (d & (NX - 1))
        at = jnp.where(mine, at, dump)
        acc[at] = acc[at] + term.astype(F32)

    def add_own(s, carry):
        add_to(dest_own[s], s < count[0], own[s])
        return carry

    lax.fori_loop(0, TILES_DEV, add_own, 0, unroll=8)
    copy.wait()

    def add_other(s, carry):
        d = dest_other[0, s]
        add_to(d, d >= 0, other[s])
        return carry

    lax.fori_loop(0, TILES_DEV, add_other, 0, unroll=8)
    out[...] = acc[0:dump].astype(BF)

    @pl.when(k == 1)
    def _():
        for m in range(2 * nz):
            for x in range(NX):
                b = (m // nz) * NX + x
                out[m * size + ny * NX + x] = feats[:, b * TB : (b + 1) * TB]


def middle_z_kernel(nz, recv, out):
    ny = out.shape[0] // NX
    here = lax.axis_index("zl")
    for h in range(2):
        for n in range(ny * NX):
            total = recv[h * nz, n].astype(F32)
            for z in range(1, nz):
                total = total + recv[h * nz + z, n].astype(F32)
            out[n, h * F_LOC : (h + 1) * F_LOC] = total.astype(BF)
        for x in range(NX):
            tile = recv[h * nz + here, ny * NX + x]
            for y in range(ny):
                out[y * NX + x, (2 + h) * F_LOC : (3 + h) * F_LOC] = tile


def middle_y_kernel(recv, feats, out):
    places = out.shape[0] // RB
    for b in range(RB):
        own = feats[:, b * TB : (b + 1) * TB]
        for p in range(places):
            total = jnp.sum(recv[:, p * RB + b].astype(F32), axis=0)
            out[p * RB + b, 0:F_LOC] = total.astype(BF)
            out[p * RB + b, F_LOC : 2 * F_LOC] = own


def agg_kernel(z_first, recv, degree, out):
    halves = 2 if z_first else 1
    size = RB // halves
    places = recv.shape[0] // size
    here = lax.axis_index("y" if z_first else "zl") * size
    deg = degree[pl.ds(lax.axis_index(COL), 1), :].astype(F32)
    for c in range(RB):
        h, n = c // size, c % size
        rows = slice(h * F_LOC, (h + 1) * F_LOC)
        total = recv[n, rows].astype(F32)
        for p in range(1, places):
            total = total + recv[p * size + n, rows].astype(F32)
        out[c, 0:F_LOC] = (total / deg).astype(BF)
        rows = slice((halves + h) * F_LOC, (halves + h + 1) * F_LOC)
        out[c, F_LOC : 2 * F_LOC] = recv[here + n, rows]


def dense_layer_kernel(recv, w_self, w_neigh, bias, cot, degree, hidden, out):
    agg = recv[:, 0:F_LOC].reshape(RB * F_LOC, TB)
    feats = recv[:, F_LOC : 2 * F_LOC].reshape(RB * F_LOC, TB)
    ws = w_self[...]
    wn = w_neigh[...]
    first = (((0,), (0,)), ((), ()))
    last = (((1,), (1,)), ((), ()))
    preact = lax.dot_general(ws, feats, first, preferred_element_type=F32)
    preact = preact + lax.dot_general(wn, agg, first, preferred_element_type=F32)
    preact = preact + jnp.broadcast_to(bias[...], (TB, bias.shape[1])).T
    sigma = 1.0 / (1.0 + jnp.exp(-preact))
    hidden[...] = (preact * sigma).astype(BF)
    slope = sigma * (1.0 + preact * (1.0 - sigma))
    grad_pre = (cot[...].astype(F32) * slope).astype(BF)
    part_self = lax.dot_general(feats, grad_pre, last, preferred_element_type=F32)
    part_neigh = lax.dot_general(agg, grad_pre, last, preferred_element_type=F32)
    ones = jnp.ones((8, TB), BF)
    part_bias = lax.dot_general(ones, grad_pre, last, preferred_element_type=F32)[0:1]
    dx_self = jnp.dot(ws, grad_pre, preferred_element_type=F32).astype(BF)
    dagg = jnp.dot(wn, grad_pre, preferred_element_type=F32).astype(BF)
    deg = degree[pl.ds(lax.axis_index(COL), 1), :].astype(F32)
    dsum = (dagg.astype(F32) / deg).astype(BF)
    two = jnp.concatenate([part_bias[:, 0:TB], part_bias[:, TB:]], axis=0)
    high = two.astype(BF).astype(F32)
    tail = jnp.concatenate([high, two - high, jnp.zeros((12, TB), F32)], axis=0).astype(BF)
    for c in range(RB):
        rows = slice(c * F_LOC, (c + 1) * F_LOC)
        out[c, 0:16] = dsum[rows]
        out[c, 16:32] = dx_self[rows]
        out[c, 32:48] = part_self[rows, 0:TB].astype(BF)
        out[c, 48:64] = part_self[rows, TB:].astype(BF)
        out[c, 64:80] = part_neigh[rows, 0:TB].astype(BF)
        out[c, 80:96] = part_neigh[rows, TB:].astype(BF)
        out[c, 96:112] = tail


def parted(tail):
    two = tail[0:2] + tail[2:4]
    high = two.astype(BF).astype(F32)
    return jnp.concatenate([high, two - high, jnp.zeros((12, TB), F32)], axis=0).astype(BF)


def first_step_kernel(recv, out):
    blocks = recv[:, 0:F_LOC]
    sums = jnp.sum(recv[:, 32:96].astype(F32), axis=0).astype(BF)
    tail = parted(jnp.sum(recv[:, 96:112].astype(F32), axis=0))
    for p in range(out.shape[0]):
        out[p, 0:RB] = blocks
        for n in range(4):
            out[p, RB + n] = sums[n * F_LOC : (n + 1) * F_LOC]
        out[p, RB + 4] = tail


def second_step_kernel(recv, out):
    came = recv.shape[0]
    sums = [jnp.sum(recv[:, RB + n].astype(F32), axis=0) for n in range(EXTRA)]
    sums = [x.astype(BF) for x in sums[:4]] + [parted(sums[4])]
    for p in range(out.shape[0]):
        for q in range(came):
            out[p, q * RB : (q + 1) * RB] = recv[q, 0:RB]
        for n in range(EXTRA):
            out[p, came * RB + n] = sums[n]


def share_kernel(first, recv_h, out, bias_out, recv, sems):
    copies = [
        pltpu.make_async_copy(recv_h.at[p, pl.ds(first, EXTRA)], recv.at[p], sems.at[p])
        for p in range(recv.shape[0])
    ]
    for copy in copies:
        copy.start()
    for copy in copies:
        copy.wait()
    sums = [jnp.sum(recv[:, n].astype(F32), axis=0) for n in range(EXTRA)]
    rows = [x.astype(BF) for x in sums[:4]]
    for p in range(out.shape[0]):
        for n in range(4):
            out[p, n * F_LOC : (n + 1) * F_LOC] = rows[n]
    bias_out[...] = parted(sums[4])


def pick_kernel(ny, nz, dest_own, count, dest_other, recv, bias_sum, own, other):
    k = lax.axis_index("k")
    of_y = jnp.where(k == 0, nz * RB + EXTRA, RB)
    of_z = jnp.where(k == 0, RB, ny * (nz * RB + EXTRA) // nz)
    bits = nz.bit_length() - 1

    def pick(d, used):
        mine = jnp.logical_and(used, ((d >> 3) & 1) == k)
        d = jnp.where(mine, d, 0)
        at = (d >> (4 + bits)) * of_y + ((d >> 4) & (nz - 1)) * of_z + (d & 7)
        tile = recv[at]
        return jnp.where(mine, tile, jnp.zeros_like(tile))

    def step(s, carry):
        own[s] = pick(dest_own[s], s < count[0])
        d = dest_other[0, s]
        other[s] = pick(d, d >= 0)
        return carry

    lax.fori_loop(0, TILES_DEV, step, 0, unroll=8)
    other[TILES_DEV] = bias_sum[...]


def back_kernel(src, own, given, recv, vals, out, acc):
    g = pl.program_id(0)

    @pl.when(g == 0)
    def _():
        acc[...] = recv[:, F_LOC : 2 * F_LOC].astype(F32)

    first = g * STEP
    for t in range(STEP):
        grad = own[t] + given[t]
        at = src[first + t]
        acc[at] = acc[at] + jnp.dot(grad, vals[t], preferred_element_type=F32)

    @pl.when(g == pl.num_programs(0) - 1)
    def _():
        for b in range(RB):
            out[:, b * TB : (b + 1) * TB] = acc[b].astype(BF)


def tile_back(src, own, given, recv, vals):
    tiles = pl.BlockSpec((STEP, F_LOC, TB), lambda g, s: (g, 0, 0))
    return pl.pallas_call(
        back_kernel,
        out_shape=sds((F_LOC, RB * TB), BF),
        grid_spec=pltpu.PrefetchScalarGridSpec(
            num_scalar_prefetch=1,
            grid=(TILES_DEV // STEP,),
            in_specs=[
                tiles,
                tiles,
                pl.BlockSpec(recv.shape, lambda g, s: (0, 0, 0)),
                pl.BlockSpec((STEP, TB, TB), lambda g, s: (g, 0, 0)),
            ],
            out_specs=pl.BlockSpec((F_LOC, RB * TB), lambda g, s: (0, 0)),
            scratch_shapes=[pltpu.VMEM((RB, F_LOC, TB), F32)],
        ),
        compiler_params=PARAMS,
        cost_estimate=lasting(2.2),
    )(src, own, given, recv, vals)


def normal_kernel(x, bias_sum, given, grad_self, grad_neigh, grad_bias):
    for first, out in ((0, grad_self), (32, grad_neigh)):
        rows = slice(first, first + 32)
        part = x[0:RB, rows].astype(F32) + x[RB : 2 * RB, rows].astype(F32)
        scale = jnp.sqrt(jnp.sum(part * part) / (RB * 32 * TB) + EPS)
        scaled = part / scale
        for c in range(RB):
            at = slice(c * F_LOC, (c + 1) * F_LOC)
            out[at, 0:TB] = scaled[c, 0:16]
            out[at, TB:] = scaled[c, 16:32]
    mine = bias_sum[...].astype(F32)
    theirs = given[TILES_DEV].astype(F32)
    two = (mine[0:2] + mine[2:4]) + (theirs[0:2] + theirs[2:4])
    grad_bias[...] = two / jnp.sqrt(jnp.mean(two * two) + EPS)


def local(
    features,
    tile_values,
    tile_source,
    tile_dest,
    tile_count,
    degree,
    w_self,
    w_neigh,
    bias,
    cotangent,
):
    ny, nz = lax.axis_size("y"), lax.axis_size("zl")
    swap = [(0, 1), (1, 0)]
    degree2 = degree.reshape(RB, TB)

    terms = tile_terms(
        tile_source, tile_dest.reshape(1, -1), tile_count, features, tile_values
    )
    terms_other = lax.ppermute(terms, "k", swap)
    sent = 2 * nz * (ny + 1) * NX
    dense, dest_other = whole(
        functools.partial(dense_kernel, ny, nz),
        (sds((sent, F_LOC, TB), BF), sds((1, TB), jnp.int32)),
        [SMEM, SMEM, VMEM, VMEM, VMEM],
        [
            pltpu.VMEM((sent + 1, F_LOC, TB), F32),
            pltpu.VMEM((1, TB), jnp.int32),
            pltpu.SemaphoreType.DMA,
        ],
        [VMEM, SMEM],
    )(tile_dest, tile_count, terms, terms_other, features)

    def exchange(array, axes):
        return lax.all_to_all(array, axes, split_axis=0, concat_axis=0, tiled=True)

    def z_collect(dense, features, degree2):
        one = exchange(dense.reshape(2 * nz, (ny + 1) * NX, F_LOC, TB), ("zh", "zl"))
        two = whole(
            functools.partial(middle_z_kernel, nz),
            sds((ny * NX, 4 * F_LOC, TB), BF),
            [VMEM],
        )(one)
        two = exchange(two, ("y", "x"))
        return whole(
            functools.partial(agg_kernel, True), sds((RB, 2 * F_LOC, TB), BF), [VMEM] * 2
        )(two, degree2)

    def y_collect(dense, features, degree2):
        one = exchange(dense.reshape(ny, sent // ny, F_LOC, TB), "y")
        two = whole(middle_y_kernel, sds((nz * RB, 2 * F_LOC, TB), BF), [VMEM] * 2)(
            one, features
        )
        two = exchange(two, ("zl",) + COL)
        return whole(
            functools.partial(agg_kernel, False), sds((RB, 2 * F_LOC, TB), BF), [VMEM] * 2
        )(two, degree2)

    full = lax.cond(
        lax.axis_index("k") == 1, z_collect, y_collect, dense, features, degree2
    )
    hidden, back = whole(
        dense_layer_kernel,
        (sds(cotangent.shape, BF), sds((RB, 112, TB), BF)),
        [VMEM] * 6,
    )(full, w_self, w_neigh, bias.reshape(1, -1), cotangent, degree2)
    back = exchange(back, COL)

    tiles = ny * (nz * RB + EXTRA)

    def in_two_steps(first, second):
        def run(back):
            n1, n2 = lax.axis_size(first), lax.axis_size(second)
            one = whole(first_step_kernel, sds((n1, RB + EXTRA, F_LOC, TB), BF), [VMEM])(back)
            one = exchange(one, first)
            two = whole(second_step_kernel, sds((n2, tiles // n2, F_LOC, TB), BF), [VMEM])(one)
            two = exchange(two, second)
            share, bias_sum = whole(
                functools.partial(share_kernel, n1 * RB),
                (sds((2 * RB, 64, TB), BF), sds((F_LOC, TB), BF)),
                [ANY],
                [pltpu.VMEM((n2, EXTRA, F_LOC, TB), BF), pltpu.SemaphoreType.DMA((n2,))],
            )(two)
            return two.reshape(tiles, F_LOC, TB), share, bias_sum

        return run

    portion, share, bias_sum = lax.cond(
        lax.axis_index("k") == 0, in_two_steps("zl", "y"), in_two_steps("y", "zl"), back
    )
    chunks = exchange(share, ("k",) + COL)
    own, other = whole(
        functools.partial(pick_kernel, ny, nz),
        (sds((TILES_DEV, F_LOC, TB), BF), sds((TILES_DEV + 1, F_LOC, TB), BF)),
        [SMEM, SMEM, SMEM, VMEM, VMEM],
        cost=lasting(1.2),
    )(tile_dest, tile_count, dest_other, portion, bias_sum)
    given = lax.ppermute(other, "k", swap)
    grad_x = tile_back(tile_source, own, given, back, tile_values)
    grad_self, grad_neigh, grad_bias = whole(
        normal_kernel,
        (sds(w_self.shape, F32), sds(w_self.shape, F32), sds((2, TB), F32)),
        [VMEM] * 3,
    )(chunks, bias_sum, given)
    return hidden, grad_x, grad_self, grad_neigh, grad_bias.reshape(-1)


def solution(mesh):
    vtx, col = mesh.shape["vtx"], mesh.shape["col"]
    fine = Mesh(mesh.devices.reshape(Y, vtx // (2 * Y), 2, 2, col // 2), AXES)
    placed = (
        P(COL, VTX),
        P(VTX, None, None),
        P(VTX),
        P(VTX),
        P(VTX),
        P(VTX),
        P(),
        P(),
        P(),
        P(None, AXES),
    )
    return jax.shard_map(
        local,
        mesh=fine,
        in_specs=placed,
        out_specs=(P(None, AXES), P(COL, VTX), P(), P(), P()),
        check_vma=False,
    )
```

```python
import functools

import jax
import jax.numpy as jnp
from jax import lax
from jax.experimental import pallas as pl
from jax.experimental.pallas import tpu as pltpu
from jax.sharding import Mesh
from jax.sharding import PartitionSpec as P

TB = 128
TILES_DEV = 64
RB = 8
F_LOC = 16
Y = 8
NX = 4
STEP = 16
EXTRA = 5

EPS = 1e-06
BF = jnp.bfloat16
F32 = jnp.float32

AXES = ("y", "zl", "k", "zh", "x")
COL = ("zh", "x")
VTX = ("y", "zl", "k")

VMEM = pl.BlockSpec(memory_space=pltpu.VMEM)
SMEM = pl.BlockSpec(memory_space=pltpu.SMEM)
HBM = pl.BlockSpec(memory_space=pltpu.HBM)
ANY = pl.BlockSpec(memory_space=pl.ANY)
PARAMS = pltpu.CompilerParams(vmem_limit_bytes=32 * 1024 * 1024)
FULL_PARAMS = pltpu.CompilerParams(vmem_limit_bytes=59 * 1024 * 1024)


def whole(kernel, out_shape, in_specs, scratch=(), out_specs=None, cost=None):
    many = isinstance(out_shape, (tuple, list))
    return pl.pallas_call(
        kernel,
        out_shape=out_shape,
        in_specs=in_specs,
        out_specs=out_specs or ([VMEM] * len(out_shape) if many else VMEM),
        scratch_shapes=list(scratch),
        compiler_params=PARAMS,
        cost_estimate=cost,
    )


def lasting(us):
    return pl.CostEstimate(flops=0, transcendentals=0, bytes_accessed=int(us * 3.6e6))


def sds(shape, dtype):
    return jax.ShapeDtypeStruct(shape, dtype)


def terms_kernel(
    src_h, dest_h, count_h, feats_h, vals_h, out, src, dest, count, feats, vals, sems, val_sems
):
    small = [
        pltpu.make_async_copy(a, b, sems.at[n])
        for n, (a, b) in enumerate(
            ((src_h, src), (feats_h, feats), (dest_h, dest), (count_h, count))
        )
    ]
    parts = TILES_DEV // STEP
    large = [
        pltpu.make_async_copy(
            vals_h.at[pl.ds(g * STEP, STEP)], vals.at[pl.ds(g * STEP, STEP)], val_sems.at[g]
        )
        for g in range(parts)
    ]
    for copy in small + large:
        copy.start()
    for copy in small:
        copy.wait()
    slot = lax.broadcasted_iota(jnp.int32, (16, TB), 1)
    row = lax.broadcasted_iota(jnp.int32, (16, TB), 0)
    d = jnp.concatenate([dest[...], dest[...]], axis=1)
    d = jnp.where(slot < count[0], jnp.broadcast_to(d, (16, TB)), -1)
    coded = jnp.where(row == 0, d >> 3, d & 7)
    out[TILES_DEV] = coded.astype(F32).astype(BF)
    for g in range(parts):
        large[g].wait()
        for t in range(g * STEP, (g + 1) * STEP):
            start = pl.multiple_of(src[t] * TB, TB)
            block = feats[:, pl.ds(start, TB)]
            term = lax.dot_general(
                block, vals[t], (((1,), (1,)), ((), ())), preferred_element_type=F32
            )
            out[t] = term.astype(BF)


def tile_terms(src, dest, count, feats, vals):
    return pl.pallas_call(
        terms_kernel,
        out_shape=sds((TILES_DEV + 1, F_LOC, TB), BF),
        in_specs=[HBM] * 5,
        out_specs=VMEM,
        scratch_shapes=[
            pltpu.SMEM((TILES_DEV,), jnp.int32),
            pltpu.VMEM((1, TILES_DEV), jnp.int32),
            pltpu.SMEM((1,), jnp.int32),
            pltpu.VMEM(feats.shape, BF),
            pltpu.VMEM(vals.shape, BF),
            pltpu.SemaphoreType.DMA((4,)),
            pltpu.SemaphoreType.DMA((TILES_DEV // STEP,)),
        ],
        compiler_params=FULL_PARAMS,
    )(src, dest, count, feats, vals)


def dense_kernel(ny, nz, dest_own, count, own, other, feats, out, dest_other, acc, coded, sem):
    k = lax.axis_index("k")
    size = ny * NX + NX
    of_y = jnp.where(k == 1, NX, 2 * nz * size // ny)
    of_z = jnp.where(k == 1, size, RB)
    of_zh = jnp.where(k == 1, nz * size, NX)
    bits = nz.bit_length() - 1
    dump = acc.shape[0] - 1
    given = other[TILES_DEV].astype(F32)
    coded[...] = (given[0:1] * 8.0 + given[1:2]).astype(jnp.int32)
    copy = pltpu.make_async_copy(coded, dest_other, sem)
    copy.start()
    acc[...] = jnp.zeros_like(acc)

    def add_to(d, used, term):
        mine = jnp.logical_and(used, ((d >> 3) & 1) == k)
        at = (d >> (4 + bits)) * of_y + ((d >> 4) & (nz - 1)) * of_z
        at = at + ((d >> 2) & 1) * of_zh + (d & (NX - 1))
        at = jnp.where(mine, at, dump)
        acc[at] = acc[at] + term.astype(F32)

    def add_own(s, carry):
        add_to(dest_own[s], s < count[0], own[s])
        return carry

    lax.fori_loop(0, TILES_DEV, add_own, 0, unroll=8)
    copy.wait()

    def add_other(s, carry):
        d = dest_other[0, s]
        add_to(d, d >= 0, other[s])
        return carry

    lax.fori_loop(0, TILES_DEV, add_other, 0, unroll=8)
    out[...] = acc[0:dump].astype(BF)

    @pl.when(k == 1)
    def _():
        for m in range(2 * nz):
            for x in range(NX):
                b = (m // nz) * NX + x
                out[m * size + ny * NX + x] = feats[:, b * TB : (b + 1) * TB]


def middle_z_kernel(nz, recv, out):
    ny = out.shape[0] // NX
    here = lax.axis_index("zl")
    for h in range(2):
        for n in range(ny * NX):
            total = recv[h * nz, n].astype(F32)
            for z in range(1, nz):
                total = total + recv[h * nz + z, n].astype(F32)
            out[n, h * F_LOC : (h + 1) * F_LOC] = total.astype(BF)
        for x in range(NX):
            tile = recv[h * nz + here, ny * NX + x]
            for y in range(ny):
                out[y * NX + x, (2 + h) * F_LOC : (3 + h) * F_LOC] = tile


def middle_y_kernel(recv, feats, out):
    places = out.shape[0] // RB
    for b in range(RB):
        own = feats[:, b * TB : (b + 1) * TB]
        for p in range(places):
            total = jnp.sum(recv[:, p * RB + b].astype(F32), axis=0)
            out[p * RB + b, 0:F_LOC] = total.astype(BF)
            out[p * RB + b, F_LOC : 2 * F_LOC] = own


def agg_kernel(z_first, recv, degree, out):
    halves = 2 if z_first else 1
    size = RB // halves
    places = recv.shape[0] // size
    here = lax.axis_index("y" if z_first else "zl") * size
    deg = degree[pl.ds(lax.axis_index(COL), 1), :].astype(F32)
    for c in range(RB):
        h, n = c // size, c % size
        rows = slice(h * F_LOC, (h + 1) * F_LOC)
        total = recv[n, rows].astype(F32)
        for p in range(1, places):
            total = total + recv[p * size + n, rows].astype(F32)
        out[c, 0:F_LOC] = (total / deg).astype(BF)
        rows = slice((halves + h) * F_LOC, (halves + h + 1) * F_LOC)
        out[c, F_LOC : 2 * F_LOC] = recv[here + n, rows]


def dense_layer_kernel(recv, w_self, w_neigh, bias, cot, degree, hidden, out, dx_out):
    agg = recv[:, 0:F_LOC].reshape(RB * F_LOC, TB)
    feats = recv[:, F_LOC : 2 * F_LOC].reshape(RB * F_LOC, TB)
    ws = w_self[...]
    wn = w_neigh[...]
    first = (((0,), (0,)), ((), ()))
    last = (((1,), (1,)), ((), ()))
    preact = lax.dot_general(ws, feats, first, preferred_element_type=F32)
    preact = preact + lax.dot_general(wn, agg, first, preferred_element_type=F32)
    preact = preact + jnp.broadcast_to(bias[...], (TB, bias.shape[1])).T
    sigma = 1.0 / (1.0 + jnp.exp(-preact))
    hidden[...] = (preact * sigma).astype(BF)
    slope = sigma * (1.0 + preact * (1.0 - sigma))
    grad_pre = (cot[...].astype(F32) * slope).astype(BF)
    part_self = lax.dot_general(feats, grad_pre, last, preferred_element_type=F32)
    part_neigh = lax.dot_general(agg, grad_pre, last, preferred_element_type=F32)
    ones = jnp.ones((8, TB), BF)
    part_bias = lax.dot_general(ones, grad_pre, last, preferred_element_type=F32)[0:1]
    dx_self = jnp.dot(ws, grad_pre, preferred_element_type=F32).astype(BF)
    dagg = jnp.dot(wn, grad_pre, preferred_element_type=F32).astype(BF)
    deg = degree[pl.ds(lax.axis_index(COL), 1), :].astype(F32)
    dsum = (dagg.astype(F32) / deg).astype(BF)
    two = jnp.concatenate([part_bias[:, 0:TB], part_bias[:, TB:]], axis=0)
    high = two.astype(BF).astype(F32)
    tail = jnp.concatenate([high, two - high, jnp.zeros((12, TB), F32)], axis=0).astype(BF)
    for c in range(RB):
        rows = slice(c * F_LOC, (c + 1) * F_LOC)
        h, x = c // NX, c % NX
        dx_out[c] = dx_self[rows]
        out[x, h] = dsum[rows]
        first = 2 + 4 * h
        out[x, first] = part_self[rows, 0:TB].astype(BF)
        out[x, first + 1] = part_self[rows, TB:].astype(BF)
        out[x, first + 2] = part_neigh[rows, 0:TB].astype(BF)
        out[x, first + 3] = part_neigh[rows, TB:].astype(BF)
    for x in range(NX):
        out[x, 10] = tail


def parted(tail):
    two = tail[0:2] + tail[2:4]
    high = two.astype(BF).astype(F32)
    return jnp.concatenate([high, two - high, jnp.zeros((12, TB), F32)], axis=0).astype(BF)


def added(recv, n):
    total = recv[0, n].astype(F32)
    for p in range(1, recv.shape[0]):
        total = total + recv[p, n].astype(F32)
    return total


def first_step_kernel(z_first, recv, out):
    places = out.shape[0]
    bias = parted(added(recv, 10))
    for h in range(2):
        sums = [added(recv, 2 + 4 * h + n).astype(BF) for n in range(4)]
        at = 0 if z_first else NX * h
        sums_at = NX if z_first else 2 * NX + 4 * h
        for p in range(places):
            if z_first and p // (places // 2) != h:
                continue
            for x in range(NX):
                out[p, at + x] = recv[x, h]
            for n in range(4):
                out[p, sums_at + n] = sums[n]
    for p in range(places):
        out[p, out.shape[1] - 1] = bias


def second_step_kernel(z_first, recv, out):
    came, places = recv.shape[0], out.shape[0]
    bias = parted(added(recv, recv.shape[1] - 1))
    if z_first:
        nz = came // 2
        sums = [added(recv, NX + n).astype(BF) for n in range(4)]
        for p in range(places):
            for q in range(came):
                at = (q % nz) * RB + (q // nz) * NX
                out[p, at : at + NX] = recv[q, 0:NX]
            for n in range(4):
                out[p, nz * RB + n] = sums[n]
            out[p, nz * RB + 4] = bias
    else:
        for h in range(2):
            sums = [added(recv, 2 * NX + 4 * h + n).astype(BF) for n in range(4)]
            for p in range(places // 2 * h, places // 2 * (h + 1)):
                for q in range(came):
                    out[p, q * NX : (q + 1) * NX] = recv[q, h * NX : (h + 1) * NX]
                for n in range(4):
                    out[p, came * NX + n] = sums[n]
                out[p, came * NX + 4] = bias


def share_kernel(first, recv_h, dx, out, bias_out, recv, sems):
    copies = [
        pltpu.make_async_copy(recv_h.at[p, pl.ds(first, EXTRA)], recv.at[p], sems.at[p])
        for p in range(recv.shape[0])
    ]
    for copy in copies:
        copy.start()
    for copy in copies:
        copy.wait()
    sums = [jnp.sum(recv[:, n].astype(F32), axis=0) for n in range(EXTRA)]
    rows = [x.astype(BF) for x in sums[:4]]
    for p in range(out.shape[0]):
        for n in range(4):
            out[p, n * F_LOC : (n + 1) * F_LOC] = rows[n]
        out[p, 4 * F_LOC : 5 * F_LOC] = dx[p % RB]
    bias_out[...] = parted(sums[4])


def pick_kernel(nz, size_0, size_1, dest_own, count, dest_other, recv, bias_sum, own, other):
    k = lax.axis_index("k")
    of_y = jnp.where(k == 0, size_0, NX)
    of_zl = jnp.where(k == 0, RB, size_1)
    of_zh = jnp.where(k == 0, NX, nz * size_1)
    bits = nz.bit_length() - 1

    def pick(d, used):
        mine = jnp.logical_and(used, ((d >> 3) & 1) == k)
        d = jnp.where(mine, d, 0)
        at = (d >> (4 + bits)) * of_y + ((d >> 4) & (nz - 1)) * of_zl
        at = at + ((d >> 2) & 1) * of_zh + (d & (NX - 1))
        tile = recv[at]
        return jnp.where(mine, tile, jnp.zeros_like(tile))

    def step(s, carry):
        own[s] = pick(dest_own[s], s < count[0])
        d = dest_other[0, s]
        other[s] = pick(d, d >= 0)
        return carry

    lax.fori_loop(0, TILES_DEV, step, 0, unroll=8)
    other[TILES_DEV] = bias_sum[...]


def back_kernel(src, own, given, vals, acc):
    @pl.when(pl.program_id(0) == 0)
    def _():
        acc[...] = jnp.zeros_like(acc)

    first = pl.program_id(0) * STEP
    for t in range(STEP):
        grad = own[t] + given[t]
        at = src[first + t]
        acc[at] = acc[at] + jnp.dot(grad, vals[t], preferred_element_type=F32)


def tile_back(src, own, given, vals):
    tiles = pl.BlockSpec((STEP, F_LOC, TB), lambda g, s: (g, 0, 0))
    return pl.pallas_call(
        back_kernel,
        out_shape=sds((RB, F_LOC, TB), F32),
        grid_spec=pltpu.PrefetchScalarGridSpec(
            num_scalar_prefetch=1,
            grid=(TILES_DEV // STEP,),
            in_specs=[tiles, tiles, pl.BlockSpec((STEP, TB, TB), lambda g, s: (g, 0, 0))],
            out_specs=pl.BlockSpec((RB, F_LOC, TB), lambda g, s: (0, 0, 0)),
        ),
        compiler_params=PARAMS,
        cost_estimate=lasting(2.2),
    )(src, own, given, vals)


def last_kernel(x, bias_sum, given, dx_neigh, grad_x, grad_self, grad_neigh, grad_bias):
    for first, out in ((0, grad_self), (32, grad_neigh)):
        rows = slice(first, first + 32)
        part = x[0:RB, rows].astype(F32) + x[RB : 2 * RB, rows].astype(F32)
        scale = jnp.sqrt(jnp.sum(part * part) / (RB * 32 * TB) + EPS)
        scaled = part / scale
        for c in range(RB):
            at = slice(c * F_LOC, (c + 1) * F_LOC)
            out[at, 0:TB] = scaled[c, 0:16]
            out[at, TB:] = scaled[c, 16:32]
    mine = bias_sum[...].astype(F32)
    theirs = given[TILES_DEV].astype(F32)
    two = (mine[0:2] + mine[2:4]) + (theirs[0:2] + theirs[2:4])
    grad_bias[...] = two / jnp.sqrt(jnp.mean(two * two) + EPS)
    here = lax.axis_index("k") * RB
    for b in range(RB):
        dx_self = x[here + b, 4 * F_LOC : 5 * F_LOC].astype(F32)
        grad_x[:, b * TB : (b + 1) * TB] = (dx_self + dx_neigh[b]).astype(BF)


def local(
    features,
    tile_values,
    tile_source,
    tile_dest,
    tile_count,
    degree,
    w_self,
    w_neigh,
    bias,
    cotangent,
):
    ny, nz = lax.axis_size("y"), lax.axis_size("zl")
    swap = [(0, 1), (1, 0)]
    degree2 = degree.reshape(RB, TB)

    terms = tile_terms(
        tile_source, tile_dest.reshape(1, -1), tile_count, features, tile_values
    )
    terms_other = lax.ppermute(terms, "k", swap)
    sent = 2 * nz * (ny + 1) * NX
    dense, dest_other = whole(
        functools.partial(dense_kernel, ny, nz),
        (sds((sent, F_LOC, TB), BF), sds((1, TB), jnp.int32)),
        [SMEM, SMEM, VMEM, VMEM, VMEM],
        [
            pltpu.VMEM((sent + 1, F_LOC, TB), F32),
            pltpu.VMEM((1, TB), jnp.int32),
            pltpu.SemaphoreType.DMA,
        ],
        [VMEM, SMEM],
    )(tile_dest, tile_count, terms, terms_other, features)

    def exchange(array, axes):
        return lax.all_to_all(array, axes, split_axis=0, concat_axis=0, tiled=True)

    def z_collect(dense, features, degree2):
        one = exchange(dense.reshape(2 * nz, (ny + 1) * NX, F_LOC, TB), ("zh", "zl"))
        two = whole(
            functools.partial(middle_z_kernel, nz),
            sds((ny * NX, 4 * F_LOC, TB), BF),
            [VMEM],
        )(one)
        two = exchange(two, ("y", "x"))
        return whole(
            functools.partial(agg_kernel, True), sds((RB, 2 * F_LOC, TB), BF), [VMEM] * 2
        )(two, degree2)

    def y_collect(dense, features, degree2):
        one = exchange(dense.reshape(ny, sent // ny, F_LOC, TB), "y")
        two = whole(middle_y_kernel, sds((nz * RB, 2 * F_LOC, TB), BF), [VMEM] * 2)(
            one, features
        )
        two = exchange(two, ("zl",) + COL)
        return whole(
            functools.partial(agg_kernel, False), sds((RB, 2 * F_LOC, TB), BF), [VMEM] * 2
        )(two, degree2)

    full = lax.cond(
        lax.axis_index("k") == 1, z_collect, y_collect, dense, features, degree2
    )
    hidden, back, dx_self = whole(
        dense_layer_kernel,
        (
            sds(cotangent.shape, BF),
            sds((NX, 11, F_LOC, TB), BF),
            sds((RB, F_LOC, TB), BF),
        ),
        [VMEM] * 6,
    )(full, w_self, w_neigh, bias.reshape(1, -1), cotangent, degree2)
    back = exchange(back, "x")

    tiles = max(ny * (nz * RB + EXTRA), 2 * nz * (ny * NX + EXTRA))

    def in_two_steps(z_first):
        zs = ("zh", "zl")
        first, second = (zs, "y") if z_first else ("y", zs)
        n1, n2 = lax.axis_size(first), lax.axis_size(second)
        width = NX + EXTRA if z_first else 2 * NX + 4 + EXTRA
        sums_at = nz * RB if z_first else ny * NX

        def run(back, dx_self):
            one = whole(
                functools.partial(first_step_kernel, z_first),
                sds((n1, width, F_LOC, TB), BF),
                [VMEM],
            )(back)
            one = exchange(one, first)
            two = whole(
                functools.partial(second_step_kernel, z_first),
                sds((n2, tiles // n2, F_LOC, TB), BF),
                [VMEM],
            )(one)
            two = exchange(two, second)
            share, bias_sum = whole(
                functools.partial(share_kernel, sums_at),
                (sds((2 * RB, 5 * F_LOC, TB), BF), sds((F_LOC, TB), BF)),
                [ANY, VMEM],
                [pltpu.VMEM((n2, EXTRA, F_LOC, TB), BF), pltpu.SemaphoreType.DMA((n2,))],
            )(two, dx_self)
            return two.reshape(tiles, F_LOC, TB), share, bias_sum

        return run

    portion, share, bias_sum = lax.cond(
        lax.axis_index("k") == 0, in_two_steps(True), in_two_steps(False), back, dx_self
    )
    chunks = exchange(share, ("k",) + COL)
    own, other = whole(
        functools.partial(pick_kernel, nz, tiles // ny, tiles // (2 * nz)),
        (sds((TILES_DEV, F_LOC, TB), BF), sds((TILES_DEV + 1, F_LOC, TB), BF)),
        [SMEM, SMEM, SMEM, VMEM, VMEM],
        cost=lasting(2.0),
    )(tile_dest, tile_count, dest_other, portion, bias_sum)
    given = lax.ppermute(other, "k", swap)
    dx_neigh = tile_back(tile_source, own, given, tile_values)
    grad_x, grad_self, grad_neigh, grad_bias = whole(
        last_kernel,
        (
            sds(features.shape, BF),
            sds(w_self.shape, F32),
            sds(w_self.shape, F32),
            sds((2, TB), F32),
        ),
        [VMEM] * 4,
    )(chunks, bias_sum, given, dx_neigh)
    return hidden, grad_x, grad_self, grad_neigh, grad_bias.reshape(-1)


def solution(mesh):
    vtx, col = mesh.shape["vtx"], mesh.shape["col"]
    fine = Mesh(mesh.devices.reshape(Y, vtx // (2 * Y), 2, 2, col // 2), AXES)
    placed = (
        P(COL, VTX),
        P(VTX, None, None),
        P(VTX),
        P(VTX),
        P(VTX),
        P(VTX),
        P(),
        P(),
        P(),
        P(None, AXES),
    )
    return jax.shard_map(
        local,
        mesh=fine,
        in_specs=placed,
        out_specs=(P(None, AXES), P(COL, VTX), P(), P(), P()),
        check_vma=False,
    )
```

```python
import functools

import jax
import jax.numpy as jnp
from jax import lax
from jax.experimental import pallas as pl
from jax.experimental.pallas import tpu as pltpu
from jax.sharding import Mesh
from jax.sharding import PartitionSpec as P

TB = 128
TILES_DEV = 64
RB = 8
F_LOC = 16
Y = 8
NX = 4
STEP = 16
EXTRA = 5

EPS = 1e-06
BF = jnp.bfloat16
F32 = jnp.float32

AXES = ("y", "zl", "k", "zh", "x")
COL = ("zh", "x")
VTX = ("y", "zl", "k")

VMEM = pl.BlockSpec(memory_space=pltpu.VMEM)
SMEM = pl.BlockSpec(memory_space=pltpu.SMEM)
HBM = pl.BlockSpec(memory_space=pltpu.HBM)
PARAMS = pltpu.CompilerParams(vmem_limit_bytes=32 * 1024 * 1024)
FULL_PARAMS = pltpu.CompilerParams(vmem_limit_bytes=59 * 1024 * 1024)


def whole(kernel, out_shape, in_specs, scratch=(), out_specs=None, cost=None):
    many = isinstance(out_shape, (tuple, list))
    return pl.pallas_call(
        kernel,
        out_shape=out_shape,
        in_specs=in_specs,
        out_specs=out_specs or ([VMEM] * len(out_shape) if many else VMEM),
        scratch_shapes=list(scratch),
        compiler_params=PARAMS,
        cost_estimate=cost,
    )


def lasting(us):
    return pl.CostEstimate(flops=0, transcendentals=0, bytes_accessed=int(us * 3.6e6))


def sds(shape, dtype):
    return jax.ShapeDtypeStruct(shape, dtype)


def terms_kernel(
    src_h, dest_h, count_h, feats_h, vals_h, out, src, dest, count, feats, vals, sems, val_sems
):
    small = [
        pltpu.make_async_copy(a, b, sems.at[n])
        for n, (a, b) in enumerate(
            ((src_h, src), (feats_h, feats), (dest_h, dest), (count_h, count))
        )
    ]
    parts = TILES_DEV // STEP
    large = [
        pltpu.make_async_copy(
            vals_h.at[pl.ds(g * STEP, STEP)], vals.at[pl.ds(g * STEP, STEP)], val_sems.at[g]
        )
        for g in range(parts)
    ]
    for copy in small + large:
        copy.start()
    for copy in small:
        copy.wait()
    slot = lax.broadcasted_iota(jnp.int32, (16, TB), 1)
    row = lax.broadcasted_iota(jnp.int32, (16, TB), 0)
    d = jnp.concatenate([dest[...], dest[...]], axis=1)
    d = jnp.where(slot < count[0], jnp.broadcast_to(d, (16, TB)), -1)
    coded = jnp.where(row == 0, d >> 3, d & 7)
    out[TILES_DEV] = coded.astype(F32).astype(BF)
    for g in range(parts):
        large[g].wait()
        for t in range(g * STEP, (g + 1) * STEP, 2):
            one, two = (
                feats[:, pl.ds(pl.multiple_of(src[n] * TB, TB), TB)] for n in (t, t + 1)
            )
            zero = jnp.zeros_like(one)
            pair = jnp.concatenate(
                [
                    jnp.concatenate([one, zero], axis=1),
                    jnp.concatenate([zero, two], axis=1),
                ],
                axis=0,
            )
            term = lax.dot_general(
                pair,
                jnp.concatenate([vals[t], vals[t + 1]], axis=1),
                (((1,), (1,)), ((), ())),
                preferred_element_type=F32,
            ).astype(BF)
            out[t] = term[0:F_LOC]
            out[t + 1] = term[F_LOC:]


def tile_terms(src, dest, count, feats, vals):
    return pl.pallas_call(
        terms_kernel,
        out_shape=sds((TILES_DEV + 1, F_LOC, TB), BF),
        in_specs=[HBM] * 5,
        out_specs=VMEM,
        scratch_shapes=[
            pltpu.SMEM((TILES_DEV,), jnp.int32),
            pltpu.VMEM((1, TILES_DEV), jnp.int32),
            pltpu.SMEM((1,), jnp.int32),
            pltpu.VMEM(feats.shape, BF),
            pltpu.VMEM(vals.shape, BF),
            pltpu.SemaphoreType.DMA((4,)),
            pltpu.SemaphoreType.DMA((TILES_DEV // STEP,)),
        ],
        compiler_params=FULL_PARAMS,
    )(src, dest, count, feats, vals)


def add_terms(ny, nz, dest_of, terms, acc):
    k = lax.axis_index("k")
    dump = acc.shape[0] - 1
    size = ny * NX + NX
    of_y = jnp.where(k == 1, NX, nz * RB)
    of_zl = jnp.where(k == 1, size, RB)
    of_zh = jnp.where(k == 1, nz * size, NX)
    bits = nz.bit_length() - 1

    def add(s, carry):
        d, used = dest_of(s)
        mine = jnp.logical_and(used, ((d >> 3) & 1) == k)
        at = (d >> (4 + bits)) * of_y + ((d >> 4) & (nz - 1)) * of_zl
        at = at + ((d >> 2) & 1) * of_zh + (d & (NX - 1))
        at = jnp.where(mine, at, dump)
        acc[at] = acc[at] + terms[s].astype(F32)
        return carry

    lax.fori_loop(0, TILES_DEV, add, 0, unroll=8)


def own_kernel(ny, nz, dest_own, count, own, acc):
    acc[...] = jnp.zeros_like(acc)
    add_terms(ny, nz, lambda s: (dest_own[s], s < count[0]), own, acc)


def both_kernel(ny, nz, first, other, feats, out_y, out_z, dest_other, acc, coded, sem):
    given = other[TILES_DEV].astype(F32)
    coded[...] = (given[0:1] * 8.0 + given[1:2]).astype(jnp.int32)
    copy = pltpu.make_async_copy(coded, dest_other, sem)
    copy.start()
    acc[...] = first[...]
    copy.wait()
    add_terms(ny, nz, lambda s: (dest_other[0, s], dest_other[0, s] >= 0), other, acc)
    k = lax.axis_index("k")

    @pl.when(k == 0)
    def _():
        last = out_y.shape[0]
        out_y[...] = acc[0:last].astype(BF)

    @pl.when(k == 1)
    def _():
        last = out_z.shape[0]
        out_z[...] = acc[0:last].astype(BF)
        for m in range(2 * nz):
            for x in range(NX):
                b = (m // nz) * NX + x
                at = m * (ny * NX + NX) + ny * NX + x
                out_z[at] = feats[:, b * TB : (b + 1) * TB]


def middle_z_kernel(nz, recv, out):
    ny = out.shape[0] // NX
    here = lax.axis_index("zl")
    for h in range(2):
        for n in range(ny * NX):
            total = recv[h * nz, n].astype(F32)
            for z in range(1, nz):
                total = total + recv[h * nz + z, n].astype(F32)
            out[n, h * F_LOC : (h + 1) * F_LOC] = total.astype(BF)
        for x in range(NX):
            tile = recv[h * nz + here, ny * NX + x]
            for y in range(ny):
                out[y * NX + x, (2 + h) * F_LOC : (3 + h) * F_LOC] = tile


def middle_y_kernel(recv, feats, out):
    places = out.shape[0] // RB
    for b in range(RB):
        own = feats[:, b * TB : (b + 1) * TB]
        for p in range(places):
            total = jnp.sum(recv[:, p * RB + b].astype(F32), axis=0)
            out[p * RB + b, 0:F_LOC] = total.astype(BF)
            out[p * RB + b, F_LOC : 2 * F_LOC] = own


def agg_kernel(z_first, recv, degree, out):
    halves = 2 if z_first else 1
    size = RB // halves
    places = recv.shape[0] // size
    here = lax.axis_index("y" if z_first else "zl") * size
    deg = degree[pl.ds(lax.axis_index(COL), 1), :].astype(F32)
    for c in range(RB):
        h, n = c // size, c % size
        rows = slice(h * F_LOC, (h + 1) * F_LOC)
        total = recv[n, rows].astype(F32)
        for p in range(1, places):
            total = total + recv[p * size + n, rows].astype(F32)
        out[c, 0:F_LOC] = (total / deg).astype(BF)
        rows = slice((halves + h) * F_LOC, (halves + h + 1) * F_LOC)
        out[c, F_LOC : 2 * F_LOC] = recv[here + n, rows]


def dense_layer_kernel(recv, w_self, w_neigh, bias, cot, degree, hidden, out, dx_out):
    agg = recv[:, 0:F_LOC].reshape(RB * F_LOC, TB)
    feats = recv[:, F_LOC : 2 * F_LOC].reshape(RB * F_LOC, TB)
    ws = w_self[...]
    wn = w_neigh[...]
    first = (((0,), (0,)), ((), ()))
    last = (((1,), (1,)), ((), ()))
    preact = lax.dot_general(ws, feats, first, preferred_element_type=F32)
    preact = preact + lax.dot_general(wn, agg, first, preferred_element_type=F32)
    preact = preact + jnp.broadcast_to(bias[...], (TB, bias.shape[1])).T
    sigma = 1.0 / (1.0 + jnp.exp(-preact))
    hidden[...] = (preact * sigma).astype(BF)
    slope = sigma * (1.0 + preact * (1.0 - sigma))
    grad_pre = (cot[...].astype(F32) * slope).astype(BF)
    part_self = lax.dot_general(feats, grad_pre, last, preferred_element_type=F32)
    part_neigh = lax.dot_general(agg, grad_pre, last, preferred_element_type=F32)
    ones = jnp.ones((8, TB), BF)
    part_bias = lax.dot_general(ones, grad_pre, last, preferred_element_type=F32)[0:1]
    dx_self = jnp.dot(ws, grad_pre, preferred_element_type=F32).astype(BF)
    dagg = jnp.dot(wn, grad_pre, preferred_element_type=F32).astype(BF)
    deg = degree[pl.ds(lax.axis_index(COL), 1), :].astype(F32)
    dsum = (dagg.astype(F32) / deg).astype(BF)
    two = jnp.concatenate([part_bias[:, 0:TB], part_bias[:, TB:]], axis=0)
    high = two.astype(BF).astype(F32)
    tail = jnp.concatenate([high, two - high, jnp.zeros((12, TB), F32)], axis=0).astype(BF)
    for c in range(RB):
        rows = slice(c * F_LOC, (c + 1) * F_LOC)
        h, x = c // NX, c % NX
        dx_out[c] = dx_self[rows]
        out[x, h] = dsum[rows]
        first = 2 + 4 * h
        out[x, first] = part_self[rows, 0:TB].astype(BF)
        out[x, first + 1] = part_self[rows, TB:].astype(BF)
        out[x, first + 2] = part_neigh[rows, 0:TB].astype(BF)
        out[x, first + 3] = part_neigh[rows, TB:].astype(BF)
    for x in range(NX):
        out[x, 10] = tail


def parted(tail):
    two = tail[0:2] + tail[2:4]
    high = two.astype(BF).astype(F32)
    return jnp.concatenate([high, two - high, jnp.zeros((12, TB), F32)], axis=0).astype(BF)


def added(recv, n):
    total = recv[0, n].astype(F32)
    for p in range(1, recv.shape[0]):
        total = total + recv[p, n].astype(F32)
    return total


def first_step_kernel(z_first, recv, out):
    places = out.shape[0]
    bias = parted(added(recv, 10))
    for h in range(2):
        sums = [added(recv, 2 + 4 * h + n).astype(BF) for n in range(4)]
        at = 0 if z_first else NX * h
        sums_at = NX if z_first else 2 * NX + 4 * h
        for p in range(places):
            if z_first and p // (places // 2) != h:
                continue
            for x in range(NX):
                out[p, at + x] = recv[x, h]
            for n in range(4):
                out[p, sums_at + n] = sums[n]
    for p in range(places):
        out[p, out.shape[1] - 1] = bias


def second_step_kernel(z_first, recv, out):
    came, places = recv.shape[0], out.shape[0]
    sums_at = out.shape[1] - EXTRA
    bias = parted(added(recv, recv.shape[1] - 1))
    if z_first:
        nz = came // 2
        sums = [added(recv, NX + n).astype(BF) for n in range(4)]
        for p in range(places):
            for q in range(came):
                at = (q % nz) * RB + (q // nz) * NX
                out[p, at : at + NX] = recv[q, 0:NX]
            for n in range(4):
                out[p, sums_at + n] = sums[n]
            out[p, sums_at + 4] = bias
    else:
        for h in range(2):
            sums = [added(recv, 2 * NX + 4 * h + n).astype(BF) for n in range(4)]
            for p in range(places // 2 * h, places // 2 * (h + 1)):
                for q in range(came):
                    out[p, q * NX : (q + 1) * NX] = recv[q, h * NX : (h + 1) * NX]
                for n in range(4):
                    out[p, sums_at + n] = sums[n]
                out[p, sums_at + 4] = bias


def share_kernel(sizes, recv, dx, out, bias_out):
    def run(size):
        sums = []
        for n in range(EXTRA):
            at = range(size - EXTRA + n, recv.shape[0], size)
            sums.append(sum(recv[m].astype(F32) for m in at))
        rows = [x.astype(BF) for x in sums[:4]]
        for p in range(out.shape[0]):
            for n in range(4):
                out[p, n * F_LOC : (n + 1) * F_LOC] = rows[n]
            out[p, 4 * F_LOC : 5 * F_LOC] = dx[p % RB]
        bias_out[...] = parted(sums[4])

    if sizes[0] == sizes[1]:
        run(sizes[0])
    else:
        for k in range(2):
            pl.when(lax.axis_index("k") == k)(functools.partial(run, sizes[k]))


def pick_kernel(nz, size_0, size_1, dest_own, count, dest_other, recv, bias_sum, own, other):
    k = lax.axis_index("k")
    of_y = jnp.where(k == 0, size_0, NX)
    of_zl = jnp.where(k == 0, RB, size_1)
    of_zh = jnp.where(k == 0, NX, nz * size_1)
    bits = nz.bit_length() - 1

    def pick(d, used):
        mine = jnp.logical_and(used, ((d >> 3) & 1) == k)
        d = jnp.where(mine, d, 0)
        at = (d >> (4 + bits)) * of_y + ((d >> 4) & (nz - 1)) * of_zl
        at = at + ((d >> 2) & 1) * of_zh + (d & (NX - 1))
        tile = recv[at]
        return jnp.where(mine, tile, jnp.zeros_like(tile))

    def step(s, carry):
        own[s] = pick(dest_own[s], s < count[0])
        d = dest_other[0, s]
        other[s] = pick(d, d >= 0)
        return carry

    lax.fori_loop(0, TILES_DEV, step, 0, unroll=8)
    other[TILES_DEV] = bias_sum[...]


def back_kernel(src, own, given, vals, acc):
    @pl.when(pl.program_id(0) == 0)
    def _():
        acc[...] = jnp.zeros_like(acc)

    first = pl.program_id(0) * STEP
    for t in range(STEP):
        grad = own[t] + given[t]
        at = src[first + t]
        acc[at] = acc[at] + jnp.dot(grad, vals[t], preferred_element_type=F32)


def tile_back(src, own, given, vals):
    tiles = pl.BlockSpec((STEP, F_LOC, TB), lambda g, s: (g, 0, 0))
    return pl.pallas_call(
        back_kernel,
        out_shape=sds((RB, F_LOC, TB), F32),
        grid_spec=pltpu.PrefetchScalarGridSpec(
            num_scalar_prefetch=1,
            grid=(TILES_DEV // STEP,),
            in_specs=[tiles, tiles, pl.BlockSpec((STEP, TB, TB), lambda g, s: (g, 0, 0))],
            out_specs=pl.BlockSpec((RB, F_LOC, TB), lambda g, s: (0, 0, 0)),
        ),
        compiler_params=PARAMS,
        cost_estimate=lasting(2.2),
    )(src, own, given, vals)


def last_kernel(x, bias_sum, given, dx_neigh, grad_x, grad_self, grad_neigh, grad_bias):
    for first, out in ((0, grad_self), (32, grad_neigh)):
        rows = slice(first, first + 32)
        part = x[0:RB, rows].astype(F32) + x[RB : 2 * RB, rows].astype(F32)
        scale = jnp.sqrt(jnp.sum(part * part) / (RB * 32 * TB) + EPS)
        scaled = part / scale
        for c in range(RB):
            at = slice(c * F_LOC, (c + 1) * F_LOC)
            out[at, 0:TB] = scaled[c, 0:16]
            out[at, TB:] = scaled[c, 16:32]
    mine = bias_sum[...].astype(F32)
    theirs = given[TILES_DEV].astype(F32)
    two = (mine[0:2] + mine[2:4]) + (theirs[0:2] + theirs[2:4])
    grad_bias[...] = two / jnp.sqrt(jnp.mean(two * two) + EPS)
    here = lax.axis_index("k") * RB
    for b in range(RB):
        dx_self = x[here + b, 4 * F_LOC : 5 * F_LOC].astype(F32)
        grad_x[:, b * TB : (b + 1) * TB] = (dx_self + dx_neigh[b]).astype(BF)


def local(
    features,
    tile_values,
    tile_source,
    tile_dest,
    tile_count,
    degree,
    w_self,
    w_neigh,
    bias,
    cotangent,
):
    ny, nz = lax.axis_size("y"), lax.axis_size("zl")
    swap = [(0, 1), (1, 0)]
    degree2 = degree.reshape(RB, TB)

    terms = tile_terms(
        tile_source, tile_dest.reshape(1, -1), tile_count, features, tile_values
    )
    terms_other = lax.ppermute(terms, "k", swap)
    sent = 2 * nz * (ny + 1) * NX
    first = whole(
        functools.partial(own_kernel, ny, nz),
        sds((sent + 1, F_LOC, TB), F32),
        [SMEM, SMEM, VMEM],
        cost=lasting(1.2),
    )(tile_dest, tile_count, terms)
    dense_y, dense_z, dest_other = whole(
        functools.partial(both_kernel, ny, nz),
        (
            sds((ny * nz * RB, F_LOC, TB), BF),
            sds((sent, F_LOC, TB), BF),
            sds((1, TB), jnp.int32),
        ),
        [VMEM] * 3,
        [
            pltpu.VMEM((sent + 1, F_LOC, TB), F32),
            pltpu.VMEM((1, TB), jnp.int32),
            pltpu.SemaphoreType.DMA,
        ],
        [VMEM, VMEM, SMEM],
    )(first, terms_other, features)

    def exchange(array, axes):
        return lax.all_to_all(array, axes, split_axis=0, concat_axis=0, tiled=True)

    def z_collect(dense_y, dense_z, features, degree2):
        one = exchange(dense_z.reshape(2 * nz, (ny + 1) * NX, F_LOC, TB), ("zh", "zl"))
        two = whole(
            functools.partial(middle_z_kernel, nz),
            sds((ny * NX, 4 * F_LOC, TB), BF),
            [VMEM],
        )(one)
        two = exchange(two, ("y", "x"))
        return whole(
            functools.partial(agg_kernel, True), sds((RB, 2 * F_LOC, TB), BF), [VMEM] * 2
        )(two, degree2)

    def y_collect(dense_y, dense_z, features, degree2):
        one = exchange(dense_y.reshape(ny, nz * RB, F_LOC, TB), "y")
        two = whole(middle_y_kernel, sds((nz * RB, 2 * F_LOC, TB), BF), [VMEM] * 2)(
            one, features
        )
        two = exchange(two, ("zl",) + COL)
        return whole(
            functools.partial(agg_kernel, False), sds((RB, 2 * F_LOC, TB), BF), [VMEM] * 2
        )(two, degree2)

    full = lax.cond(
        lax.axis_index("k") == 1, z_collect, y_collect, dense_y, dense_z, features, degree2
    )
    hidden, back, dx_self = whole(
        dense_layer_kernel,
        (
            sds(cotangent.shape, BF),
            sds((NX, 11, F_LOC, TB), BF),
            sds((RB, F_LOC, TB), BF),
        ),
        [VMEM] * 6,
    )(full, w_self, w_neigh, bias.reshape(1, -1), cotangent, degree2)
    back = exchange(back, "x")

    tiles = max(ny * (nz * RB + EXTRA), 2 * nz * (ny * NX + EXTRA))

    def in_two_steps(z_first):
        zs = ("zh", "zl")
        first, second = (zs, "y") if z_first else ("y", zs)
        n1, n2 = lax.axis_size(first), lax.axis_size(second)
        width = NX + EXTRA if z_first else 2 * NX + 4 + EXTRA

        def run(back):
            one = whole(
                functools.partial(first_step_kernel, z_first),
                sds((n1, width, F_LOC, TB), BF),
                [VMEM],
            )(back)
            one = exchange(one, first)
            two = whole(
                functools.partial(second_step_kernel, z_first),
                sds((n2, tiles // n2, F_LOC, TB), BF),
                [VMEM],
            )(one)
            two = exchange(two, second)
            return two.reshape(tiles, F_LOC, TB)

        return run

    portion = lax.cond(lax.axis_index("k") == 0, in_two_steps(True), in_two_steps(False), back)
    share, bias_sum = whole(
        functools.partial(share_kernel, (tiles // ny, tiles // (2 * nz))),
        (sds((2 * RB, 5 * F_LOC, TB), BF), sds((F_LOC, TB), BF)),
        [VMEM] * 2,
    )(portion, dx_self)
    chunks = exchange(share, ("k",) + COL)
    own, other = whole(
        functools.partial(pick_kernel, nz, tiles // ny, tiles // (2 * nz)),
        (sds((TILES_DEV, F_LOC, TB), BF), sds((TILES_DEV + 1, F_LOC, TB), BF)),
        [SMEM, SMEM, SMEM, VMEM, VMEM],
        cost=lasting(2.0),
    )(tile_dest, tile_count, dest_other, portion, bias_sum)
    given = lax.ppermute(other, "k", swap)
    dx_neigh = tile_back(tile_source, own, given, tile_values)
    grad_x, grad_self, grad_neigh, grad_bias = whole(
        last_kernel,
        (
            sds(features.shape, BF),
            sds(w_self.shape, F32),
            sds(w_self.shape, F32),
            sds((2, TB), F32),
        ),
        [VMEM] * 4,
    )(chunks, bias_sum, given, dx_neigh)
    return hidden, grad_x, grad_self, grad_neigh, grad_bias.reshape(-1)


def solution(mesh):
    vtx, col = mesh.shape["vtx"], mesh.shape["col"]
    fine = Mesh(mesh.devices.reshape(Y, vtx // (2 * Y), 2, 2, col // 2), AXES)
    placed = (
        P(COL, VTX),
        P(VTX, None, None),
        P(VTX),
        P(VTX),
        P(VTX),
        P(VTX),
        P(),
        P(),
        P(),
        P(None, AXES),
    )
    return jax.shard_map(
        local,
        mesh=fine,
        in_specs=placed,
        out_specs=(P(None, AXES), P(COL, VTX), P(), P(), P()),
        check_vma=False,
    )
```

```python
import functools

import jax
import jax.numpy as jnp
from jax import lax
from jax.experimental import pallas as pl
from jax.experimental.pallas import tpu as pltpu
from jax.sharding import Mesh
from jax.sharding import PartitionSpec as P

TB = 128
TILES_DEV = 64
RB = 8
F_LOC = 16
Y = 8
NX = 4
STEP = 16
EXTRA = 5

EPS = 1e-06
BF = jnp.bfloat16
F32 = jnp.float32

AXES = ("y", "zl", "k", "zh", "x")
COL = ("zh", "x")
VTX = ("y", "zl", "k")

VMEM = pl.BlockSpec(memory_space=pltpu.VMEM)
SMEM = pl.BlockSpec(memory_space=pltpu.SMEM)
HBM = pl.BlockSpec(memory_space=pltpu.HBM)
PARAMS = pltpu.CompilerParams(vmem_limit_bytes=32 * 1024 * 1024)
FULL_PARAMS = pltpu.CompilerParams(vmem_limit_bytes=59 * 1024 * 1024)


def whole(kernel, out_shape, in_specs, scratch=(), out_specs=None, cost=None):
    many = isinstance(out_shape, (tuple, list))
    return pl.pallas_call(
        kernel,
        out_shape=out_shape,
        in_specs=in_specs,
        out_specs=out_specs or ([VMEM] * len(out_shape) if many else VMEM),
        scratch_shapes=list(scratch),
        compiler_params=PARAMS,
        cost_estimate=cost,
    )


def lasting(us):
    return pl.CostEstimate(flops=0, transcendentals=0, bytes_accessed=int(us * 3.6e6))


def sds(shape, dtype):
    return jax.ShapeDtypeStruct(shape, dtype)


def terms_kernel(
    src_h, dest_h, count_h, feats_h, vals_h, out, src, dest, count, feats, vals, sems, val_sems
):
    small = [
        pltpu.make_async_copy(a, b, sems.at[n])
        for n, (a, b) in enumerate(
            ((src_h, src), (feats_h, feats), (dest_h, dest), (count_h, count))
        )
    ]
    parts = TILES_DEV // STEP
    large = [
        pltpu.make_async_copy(
            vals_h.at[pl.ds(g * STEP, STEP)], vals.at[pl.ds(g * STEP, STEP)], val_sems.at[g]
        )
        for g in range(parts)
    ]
    for copy in small + large:
        copy.start()
    for copy in small:
        copy.wait()
    slot = lax.broadcasted_iota(jnp.int32, (16, TB), 1)
    row = lax.broadcasted_iota(jnp.int32, (16, TB), 0)
    d = jnp.concatenate([dest[...], dest[...]], axis=1)
    d = jnp.where(slot < count[0], jnp.broadcast_to(d, (16, TB)), -1)
    coded = jnp.where(row == 0, d >> 3, d & 7)
    out[TILES_DEV] = coded.astype(F32).astype(BF)
    for g in range(parts):
        large[g].wait()
        for t in range(g * STEP, (g + 1) * STEP, 2):
            one, two = (
                feats[:, pl.ds(pl.multiple_of(src[n] * TB, TB), TB)] for n in (t, t + 1)
            )
            zero = jnp.zeros_like(one)
            pair = jnp.concatenate(
                [
                    jnp.concatenate([one, zero], axis=1),
                    jnp.concatenate([zero, two], axis=1),
                ],
                axis=0,
            )
            term = lax.dot_general(
                pair,
                jnp.concatenate([vals[t], vals[t + 1]], axis=1),
                (((1,), (1,)), ((), ())),
                preferred_element_type=F32,
            ).astype(BF)
            out[t] = term[0:F_LOC]
            out[t + 1] = term[F_LOC:]


def tile_terms(src, dest, count, feats, vals):
    return pl.pallas_call(
        terms_kernel,
        out_shape=sds((TILES_DEV + 1, F_LOC, TB), BF),
        in_specs=[HBM] * 5,
        out_specs=VMEM,
        scratch_shapes=[
            pltpu.SMEM((TILES_DEV,), jnp.int32),
            pltpu.VMEM((1, TILES_DEV), jnp.int32),
            pltpu.SMEM((1,), jnp.int32),
            pltpu.VMEM(feats.shape, BF),
            pltpu.VMEM(vals.shape, BF),
            pltpu.SemaphoreType.DMA((4,)),
            pltpu.SemaphoreType.DMA((TILES_DEV // STEP,)),
        ],
        compiler_params=FULL_PARAMS,
    )(src, dest, count, feats, vals)


def add_terms(ny, nz, dest_of, terms, acc):
    k = lax.axis_index("k")
    dump = acc.shape[0] - 1
    size = ny * NX + NX
    of_y = jnp.where(k == 1, NX, nz * RB)
    of_zl = jnp.where(k == 1, size, RB)
    of_zh = jnp.where(k == 1, nz * size, NX)
    bits = nz.bit_length() - 1

    def add(s, carry):
        d, used = dest_of(s)
        mine = jnp.logical_and(used, ((d >> 3) & 1) == k)
        at = (d >> (4 + bits)) * of_y + ((d >> 4) & (nz - 1)) * of_zl
        at = at + ((d >> 2) & 1) * of_zh + (d & (NX - 1))
        at = jnp.where(mine, at, dump)
        acc[at] = acc[at] + terms[s].astype(F32)
        return carry

    lax.fori_loop(0, TILES_DEV, add, 0, unroll=8)


def own_kernel(ny, nz, dest_own, count, own, acc):
    acc[...] = jnp.zeros_like(acc)
    add_terms(ny, nz, lambda s: (dest_own[s], s < count[0]), own, acc)


def both_kernel(ny, nz, first, other, feats, out_y, out_z, dest_other, acc, coded, sem):
    given = other[TILES_DEV].astype(F32)
    coded[...] = (given[0:1] * 8.0 + given[1:2]).astype(jnp.int32)
    copy = pltpu.make_async_copy(coded, dest_other, sem)
    copy.start()
    acc[...] = first[...]
    copy.wait()
    add_terms(ny, nz, lambda s: (dest_other[0, s], dest_other[0, s] >= 0), other, acc)
    k = lax.axis_index("k")

    @pl.when(k == 0)
    def _():
        last = out_y.shape[0]
        out_y[...] = acc[0:last].astype(BF)

    @pl.when(k == 1)
    def _():
        last = out_z.shape[0]
        out_z[...] = acc[0:last].astype(BF)
        for m in range(2 * nz):
            for x in range(NX):
                b = (m // nz) * NX + x
                at = m * (ny * NX + NX) + ny * NX + x
                out_z[at] = feats[:, b * TB : (b + 1) * TB]


def middle_z_kernel(nz, recv, out):
    ny = out.shape[0] // NX
    here = lax.axis_index("zl")
    for h in range(2):
        for n in range(ny * NX):
            total = recv[h * nz, n].astype(F32)
            for z in range(1, nz):
                total = total + recv[h * nz + z, n].astype(F32)
            out[n, h * F_LOC : (h + 1) * F_LOC] = total.astype(BF)
        for x in range(NX):
            tile = recv[h * nz + here, ny * NX + x]
            for y in range(ny):
                out[y * NX + x, (2 + h) * F_LOC : (3 + h) * F_LOC] = tile


def middle_y_kernel(recv, feats, out):
    places = out.shape[0] // RB
    for b in range(RB):
        own = feats[:, b * TB : (b + 1) * TB]
        for p in range(places):
            total = jnp.sum(recv[:, p * RB + b].astype(F32), axis=0)
            out[p * RB + b, 0:F_LOC] = total.astype(BF)
            out[p * RB + b, F_LOC : 2 * F_LOC] = own


def agg_kernel(z_first, recv, degree, out):
    halves = 2 if z_first else 1
    size = RB // halves
    places = recv.shape[0] // size
    here = lax.axis_index("y" if z_first else "zl") * size
    deg = degree[pl.ds(lax.axis_index(COL), 1), :].astype(F32)
    for c in range(RB):
        h, n = c // size, c % size
        rows = slice(h * F_LOC, (h + 1) * F_LOC)
        total = recv[n, rows].astype(F32)
        for p in range(1, places):
            total = total + recv[p * size + n, rows].astype(F32)
        out[c, 0:F_LOC] = (total / deg).astype(BF)
        rows = slice((halves + h) * F_LOC, (halves + h + 1) * F_LOC)
        out[c, F_LOC : 2 * F_LOC] = recv[here + n, rows]


def dense_layer_kernel(recv, w_self, w_neigh, bias, cot, degree, hidden, out, dx_out):
    agg = recv[:, 0:F_LOC].reshape(RB * F_LOC, TB)
    feats = recv[:, F_LOC : 2 * F_LOC].reshape(RB * F_LOC, TB)
    ws = w_self[...]
    wn = w_neigh[...]
    first = (((0,), (0,)), ((), ()))
    last = (((1,), (1,)), ((), ()))
    preact = lax.dot_general(ws, feats, first, preferred_element_type=F32)
    preact = preact + lax.dot_general(wn, agg, first, preferred_element_type=F32)
    preact = preact + jnp.broadcast_to(bias[...], (TB, bias.shape[1])).T
    sigma = 1.0 / (1.0 + jnp.exp(-preact))
    hidden[...] = (preact * sigma).astype(BF)
    slope = sigma * (1.0 + preact * (1.0 - sigma))
    grad_pre = (cot[...].astype(F32) * slope).astype(BF)
    part_self = lax.dot_general(feats, grad_pre, last, preferred_element_type=F32)
    part_neigh = lax.dot_general(agg, grad_pre, last, preferred_element_type=F32)
    ones = jnp.ones((8, TB), BF)
    part_bias = lax.dot_general(ones, grad_pre, last, preferred_element_type=F32)[0:1]
    dx_self = jnp.dot(ws, grad_pre, preferred_element_type=F32).astype(BF)
    dagg = jnp.dot(wn, grad_pre, preferred_element_type=F32).astype(BF)
    deg = degree[pl.ds(lax.axis_index(COL), 1), :].astype(F32)
    dsum = (dagg.astype(F32) / deg).astype(BF)
    two = jnp.concatenate([part_bias[:, 0:TB], part_bias[:, TB:]], axis=0)
    high = two.astype(BF).astype(F32)
    tail = jnp.concatenate([high, two - high, jnp.zeros((12, TB), F32)], axis=0).astype(BF)
    for c in range(RB):
        rows = slice(c * F_LOC, (c + 1) * F_LOC)
        h, x = c // NX, c % NX
        dx_out[c] = dx_self[rows]
        out[x, h] = dsum[rows]
        first = 2 + 4 * h
        out[x, first] = part_self[rows, 0:TB].astype(BF)
        out[x, first + 1] = part_self[rows, TB:].astype(BF)
        out[x, first + 2] = part_neigh[rows, 0:TB].astype(BF)
        out[x, first + 3] = part_neigh[rows, TB:].astype(BF)
    for x in range(NX):
        out[x, 10] = tail


def parted(tail):
    two = tail[0:2] + tail[2:4]
    high = two.astype(BF).astype(F32)
    return jnp.concatenate([high, two - high, jnp.zeros((12, TB), F32)], axis=0).astype(BF)


def added(recv, n):
    total = recv[0, n].astype(F32)
    for p in range(1, recv.shape[0]):
        total = total + recv[p, n].astype(F32)
    return total


def first_step_kernel(z_first, recv, out):
    places = out.shape[0]
    bias = parted(added(recv, 10))
    for h in range(2):
        sums = [added(recv, 2 + 4 * h + n).astype(BF) for n in range(4)]
        at = 0 if z_first else NX * h
        sums_at = NX if z_first else 2 * NX + 4 * h
        for p in range(places):
            if z_first and p // (places // 2) != h:
                continue
            for x in range(NX):
                out[p, at + x] = recv[x, h]
            for n in range(4):
                out[p, sums_at + n] = sums[n]
    for p in range(places):
        out[p, out.shape[1] - 1] = bias


def second_step_kernel(z_first, recv, out):
    came, places = recv.shape[0], out.shape[0]
    sums_at = out.shape[1] - EXTRA
    bias = parted(added(recv, recv.shape[1] - 1))
    if z_first:
        nz = came // 2
        sums = [added(recv, NX + n).astype(BF) for n in range(4)]
        for p in range(places):
            for q in range(came):
                at = (q % nz) * RB + (q // nz) * NX
                out[p, at : at + NX] = recv[q, 0:NX]
            for n in range(4):
                out[p, sums_at + n] = sums[n]
            out[p, sums_at + 4] = bias
    else:
        for h in range(2):
            sums = [added(recv, 2 * NX + 4 * h + n).astype(BF) for n in range(4)]
            for p in range(places // 2 * h, places // 2 * (h + 1)):
                for q in range(came):
                    out[p, q * NX : (q + 1) * NX] = recv[q, h * NX : (h + 1) * NX]
                for n in range(4):
                    out[p, sums_at + n] = sums[n]
                out[p, sums_at + 4] = bias


def share_kernel(sizes, recv, dx, out, bias_out):
    def run(size):
        sums = []
        for n in range(EXTRA):
            at = range(size - EXTRA + n, recv.shape[0], size)
            sums.append(sum(recv[m].astype(F32) for m in at))
        rows = [x.astype(BF) for x in sums[:4]]
        for p in range(out.shape[0]):
            for n in range(4):
                out[p, n * F_LOC : (n + 1) * F_LOC] = rows[n]
            out[p, 4 * F_LOC : 5 * F_LOC] = dx[p % RB]
        bias_out[...] = parted(sums[4])

    if sizes[0] == sizes[1]:
        run(sizes[0])
    else:
        for k in range(2):
            pl.when(lax.axis_index("k") == k)(functools.partial(run, sizes[k]))


def pick_kernel(nz, size_0, size_1, dest_own, count, dest_other, recv, bias_sum, own, other):
    k = lax.axis_index("k")
    of_y = jnp.where(k == 0, size_0, NX)
    of_zl = jnp.where(k == 0, RB, size_1)
    of_zh = jnp.where(k == 0, NX, nz * size_1)
    bits = nz.bit_length() - 1

    def pick(d, used):
        mine = jnp.logical_and(used, ((d >> 3) & 1) == k)
        d = jnp.where(mine, d, 0)
        at = (d >> (4 + bits)) * of_y + ((d >> 4) & (nz - 1)) * of_zl
        at = at + ((d >> 2) & 1) * of_zh + (d & (NX - 1))
        tile = recv[at]
        return jnp.where(mine, tile, jnp.zeros_like(tile))

    def step(s, carry):
        own[s] = pick(dest_own[s], s < count[0])
        d = dest_other[0, s]
        other[s] = pick(d, d >= 0)
        return carry

    lax.fori_loop(0, TILES_DEV, step, 0, unroll=8)
    other[TILES_DEV] = bias_sum[...]


def back_kernel(src, own, given, vals, acc):
    @pl.when(pl.program_id(0) == 0)
    def _():
        acc[...] = jnp.zeros_like(acc)

    first = pl.program_id(0) * STEP
    for t in range(STEP):
        grad = own[t] + given[t]
        at = src[first + t]
        acc[at] = acc[at] + jnp.dot(grad, vals[t], preferred_element_type=F32)


def tile_back(src, own, given, vals):
    tiles = pl.BlockSpec((STEP, F_LOC, TB), lambda g, s: (g, 0, 0))
    return pl.pallas_call(
        back_kernel,
        out_shape=sds((RB, F_LOC, TB), F32),
        grid_spec=pltpu.PrefetchScalarGridSpec(
            num_scalar_prefetch=1,
            grid=(TILES_DEV // STEP,),
            in_specs=[tiles, tiles, pl.BlockSpec((STEP, TB, TB), lambda g, s: (g, 0, 0))],
            out_specs=pl.BlockSpec((RB, F_LOC, TB), lambda g, s: (0, 0, 0)),
        ),
        compiler_params=PARAMS,
        cost_estimate=lasting(2.2),
    )(src, own, given, vals)


def last_kernel(x, bias_sum, given, dx_neigh, grad_x, grad_self, grad_neigh, grad_bias):
    for first, out in ((0, grad_self), (32, grad_neigh)):
        rows = slice(first, first + 32)
        part = x[0:RB, rows].astype(F32) + x[RB : 2 * RB, rows].astype(F32)
        scale = jnp.sqrt(jnp.sum(part * part) / (RB * 32 * TB) + EPS)
        scaled = part / scale
        for c in range(RB):
            at = slice(c * F_LOC, (c + 1) * F_LOC)
            out[at, 0:TB] = scaled[c, 0:16]
            out[at, TB:] = scaled[c, 16:32]
    mine = bias_sum[...].astype(F32)
    theirs = given[TILES_DEV].astype(F32)
    two = (mine[0:2] + mine[2:4]) + (theirs[0:2] + theirs[2:4])
    grad_bias[...] = two / jnp.sqrt(jnp.mean(two * two) + EPS)
    here = lax.axis_index("k") * RB
    for b in range(RB):
        dx_self = x[here + b, 4 * F_LOC : 5 * F_LOC].astype(F32)
        grad_x[:, b * TB : (b + 1) * TB] = (dx_self + dx_neigh[b]).astype(BF)


def local(
    features,
    tile_values,
    tile_source,
    tile_dest,
    tile_count,
    degree,
    w_self,
    w_neigh,
    bias,
    cotangent,
):
    ny, nz = lax.axis_size("y"), lax.axis_size("zl")
    swap = [(0, 1), (1, 0)]
    is_first = lax.axis_index("k") == 0
    degree2 = degree.reshape(RB, TB)

    terms = tile_terms(
        tile_source, tile_dest.reshape(1, -1), tile_count, features, tile_values
    )
    terms_other = lax.ppermute(terms, "k", swap)
    sent = 2 * nz * (ny + 1) * NX
    first = whole(
        functools.partial(own_kernel, ny, nz),
        sds((sent + 1, F_LOC, TB), F32),
        [SMEM, SMEM, VMEM],
        cost=lasting(1.2),
    )(tile_dest, tile_count, terms)
    dense_y, dense_z, dest_other = whole(
        functools.partial(both_kernel, ny, nz),
        (
            sds((ny * nz * RB, F_LOC, TB), BF),
            sds((sent, F_LOC, TB), BF),
            sds((1, TB), jnp.int32),
        ),
        [VMEM] * 3,
        [
            pltpu.VMEM((sent + 1, F_LOC, TB), F32),
            pltpu.VMEM((1, TB), jnp.int32),
            pltpu.SemaphoreType.DMA,
        ],
        [VMEM, VMEM, SMEM],
    )(first, terms_other, features)

    def exchange(array, axes):
        return lax.all_to_all(array, axes, split_axis=0, concat_axis=0, tiled=True)

    def z_collect(dense_y, dense_z, features, degree2):
        one = exchange(dense_z.reshape(2 * nz, (ny + 1) * NX, F_LOC, TB), ("zh", "zl"))
        two = whole(
            functools.partial(middle_z_kernel, nz),
            sds((ny * NX, 4 * F_LOC, TB), BF),
            [VMEM],
        )(one)
        two = exchange(two, ("y", "x"))
        return whole(
            functools.partial(agg_kernel, True), sds((RB, 2 * F_LOC, TB), BF), [VMEM] * 2
        )(two, degree2)

    def y_collect(dense_y, dense_z, features, degree2):
        one = exchange(dense_y.reshape(ny, nz * RB, F_LOC, TB), "y")
        two = whole(middle_y_kernel, sds((nz * RB, 2 * F_LOC, TB), BF), [VMEM] * 2)(
            one, features
        )
        two = exchange(two, ("zl",) + COL)
        return whole(
            functools.partial(agg_kernel, False), sds((RB, 2 * F_LOC, TB), BF), [VMEM] * 2
        )(two, degree2)

    full = lax.cond(
        is_first, y_collect, z_collect, dense_y, dense_z, features, degree2
    )
    hidden, back, dx_self = whole(
        dense_layer_kernel,
        (
            sds(cotangent.shape, BF),
            sds((NX, 11, F_LOC, TB), BF),
            sds((RB, F_LOC, TB), BF),
        ),
        [VMEM] * 6,
    )(full, w_self, w_neigh, bias.reshape(1, -1), cotangent, degree2)
    back = exchange(back, "x")

    tiles = max(ny * (nz * RB + EXTRA), 2 * nz * (ny * NX + EXTRA))

    def in_two_steps(z_first):
        zs = ("zh", "zl")
        first, second = (zs, "y") if z_first else ("y", zs)
        n1, n2 = lax.axis_size(first), lax.axis_size(second)
        width = NX + EXTRA if z_first else 2 * NX + 4 + EXTRA

        def run(back):
            one = whole(
                functools.partial(first_step_kernel, z_first),
                sds((n1, width, F_LOC, TB), BF),
                [VMEM],
            )(back)
            one = exchange(one, first)
            two = whole(
                functools.partial(second_step_kernel, z_first),
                sds((n2, tiles // n2, F_LOC, TB), BF),
                [VMEM],
            )(one)
            two = exchange(two, second)
            return two.reshape(tiles, F_LOC, TB)

        return run

    portion = lax.cond(is_first, in_two_steps(True), in_two_steps(False), back)
    share, bias_sum = whole(
        functools.partial(share_kernel, (tiles // ny, tiles // (2 * nz))),
        (sds((2 * RB, 5 * F_LOC, TB), BF), sds((F_LOC, TB), BF)),
        [VMEM] * 2,
    )(portion, dx_self)
    chunks = exchange(share, ("k",) + COL)
    own, other = whole(
        functools.partial(pick_kernel, nz, tiles // ny, tiles // (2 * nz)),
        (sds((TILES_DEV, F_LOC, TB), BF), sds((TILES_DEV + 1, F_LOC, TB), BF)),
        [SMEM, SMEM, SMEM, VMEM, VMEM],
        cost=lasting(2.0),
    )(tile_dest, tile_count, dest_other, portion, bias_sum)
    given = lax.ppermute(other, "k", swap)
    dx_neigh = tile_back(tile_source, own, given, tile_values)
    grad_x, grad_self, grad_neigh, grad_bias = whole(
        last_kernel,
        (
            sds(features.shape, BF),
            sds(w_self.shape, F32),
            sds(w_self.shape, F32),
            sds((2, TB), F32),
        ),
        [VMEM] * 4,
    )(chunks, bias_sum, given, dx_neigh)
    return hidden, grad_x, grad_self, grad_neigh, grad_bias.reshape(-1)


def solution(mesh):
    vtx, col = mesh.shape["vtx"], mesh.shape["col"]
    fine = Mesh(mesh.devices.reshape(Y, vtx // (2 * Y), 2, 2, col // 2), AXES)
    placed = (
        P(COL, VTX),
        P(VTX, None, None),
        P(VTX),
        P(VTX),
        P(VTX),
        P(VTX),
        P(),
        P(),
        P(),
        P(None, AXES),
    )
    return jax.shard_map(
        local,
        mesh=fine,
        in_specs=placed,
        out_specs=(P(None, AXES), P(COL, VTX), P(), P(), P()),
        check_vma=False,
    )
```

```python
import functools

import jax
import jax.numpy as jnp
from jax import lax
from jax.experimental import pallas as pl
from jax.experimental.pallas import tpu as pltpu
from jax.sharding import Mesh
from jax.sharding import PartitionSpec as P

TB = 128
TILES_DEV = 64
RB = 8
F_LOC = 16
Y = 8
NX = 4
STEP = 16
EXTRA = 3

EPS = 1e-06
BF = jnp.bfloat16
F32 = jnp.float32

AXES = ("y", "zl", "k", "zh", "x")
COL = ("zh", "x")
VTX = ("y", "zl", "k")

VMEM = pl.BlockSpec(memory_space=pltpu.VMEM)
SMEM = pl.BlockSpec(memory_space=pltpu.SMEM)
HBM = pl.BlockSpec(memory_space=pltpu.HBM)
PARAMS = pltpu.CompilerParams(vmem_limit_bytes=32 * 1024 * 1024)
FULL_PARAMS = pltpu.CompilerParams(vmem_limit_bytes=59 * 1024 * 1024)


def whole(kernel, out_shape, in_specs, scratch=(), out_specs=None, cost=None):
    many = isinstance(out_shape, (tuple, list))
    return pl.pallas_call(
        kernel,
        out_shape=out_shape,
        in_specs=in_specs,
        out_specs=out_specs or ([VMEM] * len(out_shape) if many else VMEM),
        scratch_shapes=list(scratch),
        compiler_params=PARAMS,
        cost_estimate=cost,
    )


def lasting(us):
    return pl.CostEstimate(flops=0, transcendentals=0, bytes_accessed=int(us * 3.6e6))


def sds(shape, dtype):
    return jax.ShapeDtypeStruct(shape, dtype)


def terms_kernel(
    src_h, dest_h, count_h, feats_h, vals_h, out, src, dest, count, feats, vals, sems, val_sems
):
    small = [
        pltpu.make_async_copy(a, b, sems.at[n])
        for n, (a, b) in enumerate(
            ((src_h, src), (feats_h, feats), (dest_h, dest), (count_h, count))
        )
    ]
    parts = TILES_DEV // STEP
    large = [
        pltpu.make_async_copy(
            vals_h.at[pl.ds(g * STEP, STEP)], vals.at[pl.ds(g * STEP, STEP)], val_sems.at[g]
        )
        for g in range(parts)
    ]
    for copy in small + large:
        copy.start()
    for copy in small:
        copy.wait()
    slot = lax.broadcasted_iota(jnp.int32, (16, TB), 1)
    row = lax.broadcasted_iota(jnp.int32, (16, TB), 0)
    d = jnp.concatenate([dest[...], dest[...]], axis=1)
    d = jnp.where(slot < count[0], jnp.broadcast_to(d, (16, TB)), -1)
    coded = jnp.where(row == 0, d >> 3, d & 7)
    out[TILES_DEV] = coded.astype(F32).astype(BF)
    for g in range(parts):
        large[g].wait()
        for t in range(g * STEP, (g + 1) * STEP, 2):
            one, two = (
                feats[:, pl.ds(pl.multiple_of(src[n] * TB, TB), TB)] for n in (t, t + 1)
            )
            zero = jnp.zeros_like(one)
            pair = jnp.concatenate(
                [
                    jnp.concatenate([one, zero], axis=1),
                    jnp.concatenate([zero, two], axis=1),
                ],
                axis=0,
            )
            term = lax.dot_general(
                pair,
                jnp.concatenate([vals[t], vals[t + 1]], axis=1),
                (((1,), (1,)), ((), ())),
                preferred_element_type=F32,
            ).astype(BF)
            out[t] = term[0:F_LOC]
            out[t + 1] = term[F_LOC:]


def tile_terms(src, dest, count, feats, vals):
    return pl.pallas_call(
        terms_kernel,
        out_shape=sds((TILES_DEV + 1, F_LOC, TB), BF),
        in_specs=[HBM] * 5,
        out_specs=VMEM,
        scratch_shapes=[
            pltpu.SMEM((TILES_DEV,), jnp.int32),
            pltpu.VMEM((1, TILES_DEV), jnp.int32),
            pltpu.SMEM((1,), jnp.int32),
            pltpu.VMEM(feats.shape, BF),
            pltpu.VMEM(vals.shape, BF),
            pltpu.SemaphoreType.DMA((4,)),
            pltpu.SemaphoreType.DMA((TILES_DEV // STEP,)),
        ],
        compiler_params=FULL_PARAMS,
    )(src, dest, count, feats, vals)


def add_terms(ny, nz, dest_of, terms, acc):
    k = lax.axis_index("k")
    dump = acc.shape[0] - 1
    size = ny * NX + NX
    of_y = jnp.where(k == 1, NX, nz * RB)
    of_zl = jnp.where(k == 1, size, RB)
    of_zh = jnp.where(k == 1, nz * size, NX)
    bits = nz.bit_length() - 1

    def add(s, carry):
        d, used = dest_of(s)
        mine = jnp.logical_and(used, ((d >> 3) & 1) == k)
        at = (d >> (4 + bits)) * of_y + ((d >> 4) & (nz - 1)) * of_zl
        at = at + ((d >> 2) & 1) * of_zh + (d & (NX - 1))
        at = jnp.where(mine, at, dump)
        acc[at] = acc[at] + terms[s].astype(F32)
        return carry

    lax.fori_loop(0, TILES_DEV, add, 0, unroll=8)


def own_kernel(ny, nz, dest_own, count, own, acc):
    acc[...] = jnp.zeros_like(acc)
    add_terms(ny, nz, lambda s: (dest_own[s], s < count[0]), own, acc)


def both_kernel(ny, nz, first, other, feats, out_y, out_z, dest_other, acc, coded, sem):
    given = other[TILES_DEV].astype(F32)
    coded[...] = (given[0:1] * 8.0 + given[1:2]).astype(jnp.int32)
    copy = pltpu.make_async_copy(coded, dest_other, sem)
    copy.start()
    acc[...] = first[...]
    copy.wait()
    add_terms(ny, nz, lambda s: (dest_other[0, s], dest_other[0, s] >= 0), other, acc)
    k = lax.axis_index("k")

    @pl.when(k == 0)
    def _():
        last = out_y.shape[0]
        out_y[...] = acc[0:last].astype(BF)

    @pl.when(k == 1)
    def _():
        last = out_z.shape[0]
        out_z[...] = acc[0:last].astype(BF)
        for m in range(2 * nz):
            for x in range(NX):
                b = (m // nz) * NX + x
                at = m * (ny * NX + NX) + ny * NX + x
                out_z[at] = feats[:, b * TB : (b + 1) * TB]


def middle_z_kernel(nz, recv, out):
    ny = out.shape[0] // NX
    here = lax.axis_index("zl")
    for h in range(2):
        for n in range(ny * NX):
            total = recv[h * nz, n].astype(F32)
            for z in range(1, nz):
                total = total + recv[h * nz + z, n].astype(F32)
            out[n, h * F_LOC : (h + 1) * F_LOC] = total.astype(BF)
        for x in range(NX):
            tile = recv[h * nz + here, ny * NX + x]
            for y in range(ny):
                out[y * NX + x, (2 + h) * F_LOC : (3 + h) * F_LOC] = tile


def middle_y_kernel(recv, feats, out):
    places = out.shape[0] // RB
    for b in range(RB):
        own = feats[:, b * TB : (b + 1) * TB]
        for p in range(places):
            total = jnp.sum(recv[:, p * RB + b].astype(F32), axis=0)
            out[p * RB + b, 0:F_LOC] = total.astype(BF)
            out[p * RB + b, F_LOC : 2 * F_LOC] = own


def agg_kernel(z_first, recv, degree, out):
    halves = 2 if z_first else 1
    size = RB // halves
    places = recv.shape[0] // size
    here = lax.axis_index("y" if z_first else "zl") * size
    deg = degree[pl.ds(lax.axis_index(COL), 1), :].astype(F32)
    for c in range(RB):
        h, n = c // size, c % size
        rows = slice(h * F_LOC, (h + 1) * F_LOC)
        total = recv[n, rows].astype(F32)
        for p in range(1, places):
            total = total + recv[p * size + n, rows].astype(F32)
        out[c, 0:F_LOC] = (total / deg).astype(BF)
        rows = slice((halves + h) * F_LOC, (halves + h + 1) * F_LOC)
        out[c, F_LOC : 2 * F_LOC] = recv[here + n, rows]


def dense_layer_kernel(recv, w_self, w_neigh, bias, cot, degree, hidden, out, dx_out):
    agg = recv[:, 0:F_LOC].reshape(RB * F_LOC, TB)
    feats = recv[:, F_LOC : 2 * F_LOC].reshape(RB * F_LOC, TB)
    ws = w_self[...]
    wn = w_neigh[...]
    first = (((0,), (0,)), ((), ()))
    last = (((1,), (1,)), ((), ()))
    preact = lax.dot_general(ws, feats, first, preferred_element_type=F32)
    preact = preact + lax.dot_general(wn, agg, first, preferred_element_type=F32)
    preact = preact + jnp.broadcast_to(bias[...], (TB, bias.shape[1])).T
    sigma = 1.0 / (1.0 + jnp.exp(-preact))
    hidden[...] = (preact * sigma).astype(BF)
    slope = sigma * (1.0 + preact * (1.0 - sigma))
    grad_pre = (cot[...].astype(F32) * slope).astype(BF)
    part_self = lax.dot_general(feats, grad_pre, last, preferred_element_type=F32)
    part_neigh = lax.dot_general(agg, grad_pre, last, preferred_element_type=F32)
    ones = jnp.ones((8, TB), BF)
    part_bias = lax.dot_general(ones, grad_pre, last, preferred_element_type=F32)[0:1]
    dx_self = jnp.dot(ws, grad_pre, preferred_element_type=F32).astype(BF)
    dagg = jnp.dot(wn, grad_pre, preferred_element_type=F32).astype(BF)
    deg = degree[pl.ds(lax.axis_index(COL), 1), :].astype(F32)
    dsum = (dagg.astype(F32) / deg).astype(BF)
    two = jnp.concatenate([part_bias[:, 0:TB], part_bias[:, TB:]], axis=0)
    high = two.astype(BF).astype(F32)
    tail = jnp.concatenate([high, two - high, jnp.zeros((12, TB), F32)], axis=0).astype(BF)
    for c in range(RB):
        rows = slice(c * F_LOC, (c + 1) * F_LOC)
        h, x = c // NX, c % NX
        dx_out[c] = dx_self[rows]
        for k, part in enumerate((part_self, part_neigh)):
            at = k * NX + x
            out[at, h] = dsum[rows]
            out[at, 2 + 2 * h] = part[rows, 0:TB].astype(BF)
            out[at, 3 + 2 * h] = part[rows, TB:].astype(BF)
    for at in range(2 * NX):
        out[at, 6] = tail


def parted(tail):
    two = tail[0:2] + tail[2:4]
    high = two.astype(BF).astype(F32)
    return jnp.concatenate([high, two - high, jnp.zeros((12, TB), F32)], axis=0).astype(BF)


def added(recv, n):
    total = recv[0, n].astype(F32)
    for p in range(1, recv.shape[0]):
        total = total + recv[p, n].astype(F32)
    return total


def first_step_kernel(z_first, recv, out):
    places = out.shape[0]
    mine = 0 if z_first else NX
    bias = parted(added(recv, 6))
    for h in range(2):
        sums = [added(recv, 2 + 2 * h + n).astype(BF) for n in range(2)]
        at = 0 if z_first else NX * h
        sums_at = NX if z_first else 2 * NX + 2 * h
        for p in range(places):
            if z_first and p // (places // 2) != h:
                continue
            for x in range(NX):
                out[p, at + x] = recv[mine + x, h]
            for n in range(2):
                out[p, sums_at + n] = sums[n]
    for p in range(places):
        out[p, out.shape[1] - 1] = bias


def second_step_kernel(z_first, recv, out):
    came, places = recv.shape[0], out.shape[0]
    sums_at = out.shape[1] - EXTRA
    bias = parted(added(recv, recv.shape[1] - 1))
    if z_first:
        nz = came // 2
        sums = [added(recv, NX + n).astype(BF) for n in range(2)]
        for p in range(places):
            for q in range(came):
                at = (q % nz) * RB + (q // nz) * NX
                out[p, at : at + NX] = recv[q, 0:NX]
            for n in range(2):
                out[p, sums_at + n] = sums[n]
            out[p, sums_at + 2] = bias
    else:
        for h in range(2):
            sums = [added(recv, 2 * NX + 2 * h + n).astype(BF) for n in range(2)]
            for p in range(places // 2 * h, places // 2 * (h + 1)):
                for q in range(came):
                    out[p, q * NX : (q + 1) * NX] = recv[q, h * NX : (h + 1) * NX]
                for n in range(2):
                    out[p, sums_at + n] = sums[n]
                out[p, sums_at + 2] = bias


def share_kernel(sizes, recv, dx, out, bias_out):
    def run(size):
        sums = []
        for n in range(EXTRA):
            at = range(size - EXTRA + n, recv.shape[0], size)
            sums.append(sum(recv[m].astype(F32) for m in at))
        rows = [x.astype(BF) for x in sums[:2]]
        for p in range(out.shape[0]):
            for n in range(2):
                out[p, n * F_LOC : (n + 1) * F_LOC] = rows[n]
            out[p, 2 * F_LOC : 3 * F_LOC] = dx[p % RB]
        bias_out[...] = parted(sums[2])

    if sizes[0] == sizes[1]:
        run(sizes[0])
    else:
        for k in range(2):
            pl.when(lax.axis_index("k") == k)(functools.partial(run, sizes[k]))


def pick_kernel(nz, size_0, size_1, dest_own, count, dest_other, recv, bias_sum, own, other):
    k = lax.axis_index("k")
    of_y = jnp.where(k == 0, size_0, NX)
    of_zl = jnp.where(k == 0, RB, size_1)
    of_zh = jnp.where(k == 0, NX, nz * size_1)
    bits = nz.bit_length() - 1

    def pick(d, used):
        mine = jnp.logical_and(used, ((d >> 3) & 1) == k)
        d = jnp.where(mine, d, 0)
        at = (d >> (4 + bits)) * of_y + ((d >> 4) & (nz - 1)) * of_zl
        at = at + ((d >> 2) & 1) * of_zh + (d & (NX - 1))
        tile = recv[at]
        return jnp.where(mine, tile, jnp.zeros_like(tile))

    def step(s, carry):
        own[s] = pick(dest_own[s], s < count[0])
        d = dest_other[0, s]
        other[s] = pick(d, d >= 0)
        return carry

    lax.fori_loop(0, TILES_DEV, step, 0, unroll=8)
    other[TILES_DEV] = bias_sum[...]


def back_kernel(src, own, given, vals, acc):
    @pl.when(pl.program_id(0) == 0)
    def _():
        acc[...] = jnp.zeros_like(acc)

    first = pl.program_id(0) * STEP
    for t in range(STEP):
        grad = own[t] + given[t]
        at = src[first + t]
        acc[at] = acc[at] + jnp.dot(grad, vals[t], preferred_element_type=F32)


def tile_back(src, own, given, vals):
    tiles = pl.BlockSpec((STEP, F_LOC, TB), lambda g, s: (g, 0, 0))
    return pl.pallas_call(
        back_kernel,
        out_shape=sds((RB, F_LOC, TB), F32),
        grid_spec=pltpu.PrefetchScalarGridSpec(
            num_scalar_prefetch=1,
            grid=(TILES_DEV // STEP,),
            in_specs=[tiles, tiles, pl.BlockSpec((STEP, TB, TB), lambda g, s: (g, 0, 0))],
            out_specs=pl.BlockSpec((RB, F_LOC, TB), lambda g, s: (0, 0, 0)),
        ),
        compiler_params=PARAMS,
        cost_estimate=lasting(2.2),
    )(src, own, given, vals)


def last_kernel(x, bias_sum, given, dx_neigh, grad_x, grad_self, grad_neigh, grad_bias):
    for k, out in enumerate((grad_self, grad_neigh)):
        part = x[k * RB : (k + 1) * RB, 0 : 2 * F_LOC].astype(F32)
        scale = jnp.sqrt(jnp.sum(part * part) / (RB * 32 * TB) + EPS)
        scaled = part / scale
        for c in range(RB):
            at = slice(c * F_LOC, (c + 1) * F_LOC)
            out[at, 0:TB] = scaled[c, 0:16]
            out[at, TB:] = scaled[c, 16:32]
    k = lax.axis_index("k")
    tail = jnp.where(k == 0, bias_sum[...], given[TILES_DEV]).astype(F32)
    two = tail[0:2] + tail[2:4]
    grad_bias[...] = two / jnp.sqrt(jnp.mean(two * two) + EPS)
    for b in range(RB):
        dx_self = x[k * RB + b, 2 * F_LOC : 3 * F_LOC].astype(F32)
        grad_x[:, b * TB : (b + 1) * TB] = (dx_self + dx_neigh[b]).astype(BF)


def local(
    features,
    tile_values,
    tile_source,
    tile_dest,
    tile_count,
    degree,
    w_self,
    w_neigh,
    bias,
    cotangent,
):
    ny, nz = lax.axis_size("y"), lax.axis_size("zl")
    swap = [(0, 1), (1, 0)]
    is_first = lax.axis_index("k") == 0
    degree2 = degree.reshape(RB, TB)

    terms = tile_terms(
        tile_source, tile_dest.reshape(1, -1), tile_count, features, tile_values
    )
    terms_other = lax.ppermute(terms, "k", swap)
    sent = 2 * nz * (ny + 1) * NX
    first = whole(
        functools.partial(own_kernel, ny, nz),
        sds((sent + 1, F_LOC, TB), F32),
        [SMEM, SMEM, VMEM],
        cost=lasting(1.2),
    )(tile_dest, tile_count, terms)
    dense_y, dense_z, dest_other = whole(
        functools.partial(both_kernel, ny, nz),
        (
            sds((ny * nz * RB, F_LOC, TB), BF),
            sds((sent, F_LOC, TB), BF),
            sds((1, TB), jnp.int32),
        ),
        [VMEM] * 3,
        [
            pltpu.VMEM((sent + 1, F_LOC, TB), F32),
            pltpu.VMEM((1, TB), jnp.int32),
            pltpu.SemaphoreType.DMA,
        ],
        [VMEM, VMEM, SMEM],
    )(first, terms_other, features)

    def exchange(array, axes):
        return lax.all_to_all(array, axes, split_axis=0, concat_axis=0, tiled=True)

    def z_collect(dense_y, dense_z, features, degree2):
        one = exchange(dense_z.reshape(2 * nz, (ny + 1) * NX, F_LOC, TB), ("zh", "zl"))
        two = whole(
            functools.partial(middle_z_kernel, nz),
            sds((ny * NX, 4 * F_LOC, TB), BF),
            [VMEM],
        )(one)
        two = exchange(two, ("y", "x"))
        return whole(
            functools.partial(agg_kernel, True), sds((RB, 2 * F_LOC, TB), BF), [VMEM] * 2
        )(two, degree2)

    def y_collect(dense_y, dense_z, features, degree2):
        one = exchange(dense_y.reshape(ny, nz * RB, F_LOC, TB), "y")
        two = whole(middle_y_kernel, sds((nz * RB, 2 * F_LOC, TB), BF), [VMEM] * 2)(
            one, features
        )
        two = exchange(two, ("zl",) + COL)
        return whole(
            functools.partial(agg_kernel, False), sds((RB, 2 * F_LOC, TB), BF), [VMEM] * 2
        )(two, degree2)

    full = lax.cond(
        is_first, y_collect, z_collect, dense_y, dense_z, features, degree2
    )
    hidden, back, dx_self = whole(
        dense_layer_kernel,
        (
            sds(cotangent.shape, BF),
            sds((2 * NX, 7, F_LOC, TB), BF),
            sds((RB, F_LOC, TB), BF),
        ),
        [VMEM] * 6,
    )(full, w_self, w_neigh, bias.reshape(1, -1), cotangent, degree2)
    back = exchange(back, ("k", "x"))

    tiles = max(ny * (nz * RB + EXTRA), 2 * nz * (ny * NX + EXTRA))

    def in_two_steps(z_first):
        zs = ("zh", "zl")
        first, second = (zs, "y") if z_first else ("y", zs)
        n1, n2 = lax.axis_size(first), lax.axis_size(second)
        width = NX + EXTRA if z_first else 2 * NX + 2 + EXTRA

        def run(back):
            one = whole(
                functools.partial(first_step_kernel, z_first),
                sds((n1, width, F_LOC, TB), BF),
                [VMEM],
            )(back)
            one = exchange(one, first)
            two = whole(
                functools.partial(second_step_kernel, z_first),
                sds((n2, tiles // n2, F_LOC, TB), BF),
                [VMEM],
            )(one)
            two = exchange(two, second)
            return two.reshape(tiles, F_LOC, TB)

        return run

    portion = lax.cond(is_first, in_two_steps(True), in_two_steps(False), back)
    share, bias_sum = whole(
        functools.partial(share_kernel, (tiles // ny, tiles // (2 * nz))),
        (sds((2 * RB, 3 * F_LOC, TB), BF), sds((F_LOC, TB), BF)),
        [VMEM] * 2,
    )(portion, dx_self)
    chunks = exchange(share, ("k",) + COL)
    own, other = whole(
        functools.partial(pick_kernel, nz, tiles // ny, tiles // (2 * nz)),
        (sds((TILES_DEV, F_LOC, TB), BF), sds((TILES_DEV + 1, F_LOC, TB), BF)),
        [SMEM, SMEM, SMEM, VMEM, VMEM],
        cost=lasting(2.0),
    )(tile_dest, tile_count, dest_other, portion, bias_sum)
    given = lax.ppermute(other, "k", swap)
    dx_neigh = tile_back(tile_source, own, given, tile_values)
    grad_x, grad_self, grad_neigh, grad_bias = whole(
        last_kernel,
        (
            sds(features.shape, BF),
            sds(w_self.shape, F32),
            sds(w_self.shape, F32),
            sds((2, TB), F32),
        ),
        [VMEM] * 4,
    )(chunks, bias_sum, given, dx_neigh)
    return hidden, grad_x, grad_self, grad_neigh, grad_bias.reshape(-1)


def solution(mesh):
    vtx, col = mesh.shape["vtx"], mesh.shape["col"]
    fine = Mesh(mesh.devices.reshape(Y, vtx // (2 * Y), 2, 2, col // 2), AXES)
    placed = (
        P(COL, VTX),
        P(VTX, None, None),
        P(VTX),
        P(VTX),
        P(VTX),
        P(VTX),
        P(),
        P(),
        P(),
        P(None, AXES),
    )
    return jax.shard_map(
        local,
        mesh=fine,
        in_specs=placed,
        out_specs=(P(None, AXES), P(COL, VTX), P(), P(), P()),
        check_vma=False,
    )
```

```python
import functools

import jax
import jax.numpy as jnp
from jax import lax
from jax.experimental import pallas as pl
from jax.experimental.pallas import tpu as pltpu
from jax.sharding import Mesh
from jax.sharding import PartitionSpec as P

TB = 128
TILES_DEV = 64
RB = 8
F_LOC = 16
Y = 8
NX = 4
STEP = 16
EXTRA = 3

EPS = 1e-06
BF = jnp.bfloat16
F32 = jnp.float32

AXES = ("y", "zl", "k", "zh", "x")
COL = ("zh", "x")
VTX = ("y", "zl", "k")

VMEM = pl.BlockSpec(memory_space=pltpu.VMEM)
SMEM = pl.BlockSpec(memory_space=pltpu.SMEM)
HBM = pl.BlockSpec(memory_space=pltpu.HBM)
PARAMS = pltpu.CompilerParams(vmem_limit_bytes=32 * 1024 * 1024)
FULL_PARAMS = pltpu.CompilerParams(vmem_limit_bytes=59 * 1024 * 1024)


def whole(kernel, out_shape, in_specs, scratch=(), out_specs=None, cost=None):
    many = isinstance(out_shape, (tuple, list))
    return pl.pallas_call(
        kernel,
        out_shape=out_shape,
        in_specs=in_specs,
        out_specs=out_specs or ([VMEM] * len(out_shape) if many else VMEM),
        scratch_shapes=list(scratch),
        compiler_params=PARAMS,
        cost_estimate=cost,
    )


def lasting(us):
    return pl.CostEstimate(flops=0, transcendentals=0, bytes_accessed=int(us * 3.6e6))


def sds(shape, dtype):
    return jax.ShapeDtypeStruct(shape, dtype)


def terms_kernel(
    src_h, dest_h, count_h, feats_h, vals_h, out, src, dest, count, feats, vals, sems, val_sems
):
    small = [
        pltpu.make_async_copy(a, b, sems.at[n])
        for n, (a, b) in enumerate(
            ((src_h, src), (feats_h, feats), (dest_h, dest), (count_h, count))
        )
    ]
    parts = TILES_DEV // STEP
    large = [
        pltpu.make_async_copy(
            vals_h.at[pl.ds(g * STEP, STEP)], vals.at[pl.ds(g * STEP, STEP)], val_sems.at[g]
        )
        for g in range(parts)
    ]
    for copy in small + large:
        copy.start()
    for copy in small:
        copy.wait()
    slot = lax.broadcasted_iota(jnp.int32, (16, TB), 1)
    row = lax.broadcasted_iota(jnp.int32, (16, TB), 0)
    d = jnp.concatenate([dest[...], dest[...]], axis=1)
    d = jnp.where(slot < count[0], jnp.broadcast_to(d, (16, TB)), -1)
    coded = jnp.where(row == 0, d >> 3, d & 7)
    out[TILES_DEV] = coded.astype(F32).astype(BF)
    for g in range(parts):
        large[g].wait()
        for t in range(g * STEP, (g + 1) * STEP, 2):
            one, two = (
                feats[:, pl.ds(pl.multiple_of(src[n] * TB, TB), TB)] for n in (t, t + 1)
            )
            zero = jnp.zeros_like(one)
            pair = jnp.concatenate(
                [
                    jnp.concatenate([one, zero], axis=1),
                    jnp.concatenate([zero, two], axis=1),
                ],
                axis=0,
            )
            term = lax.dot_general(
                pair,
                jnp.concatenate([vals[t], vals[t + 1]], axis=1),
                (((1,), (1,)), ((), ())),
                preferred_element_type=F32,
            ).astype(BF)
            out[t] = term[0:F_LOC]
            out[t + 1] = term[F_LOC:]


def tile_terms(src, dest, count, feats, vals):
    return pl.pallas_call(
        terms_kernel,
        out_shape=sds((TILES_DEV + 1, F_LOC, TB), BF),
        in_specs=[HBM] * 5,
        out_specs=VMEM,
        scratch_shapes=[
            pltpu.SMEM((TILES_DEV,), jnp.int32),
            pltpu.VMEM((1, TILES_DEV), jnp.int32),
            pltpu.SMEM((1,), jnp.int32),
            pltpu.VMEM(feats.shape, BF),
            pltpu.VMEM(vals.shape, BF),
            pltpu.SemaphoreType.DMA((4,)),
            pltpu.SemaphoreType.DMA((TILES_DEV // STEP,)),
        ],
        compiler_params=FULL_PARAMS,
    )(src, dest, count, feats, vals)


def add_terms(ny, nz, dest_of, terms, acc):
    k = lax.axis_index("k")
    dump = acc.shape[0] - 1
    size = ny * NX + NX
    of_y = jnp.where(k == 1, NX, nz * RB)
    of_zl = jnp.where(k == 1, size, RB)
    of_zh = jnp.where(k == 1, nz * size, NX)
    bits = nz.bit_length() - 1

    def add(s, carry):
        d, used = dest_of(s)
        mine = jnp.logical_and(used, ((d >> 3) & 1) == k)
        at = (d >> (4 + bits)) * of_y + ((d >> 4) & (nz - 1)) * of_zl
        at = at + ((d >> 2) & 1) * of_zh + (d & (NX - 1))
        at = jnp.where(mine, at, dump)
        acc[at] = acc[at] + terms[s].astype(F32)
        return carry

    lax.fori_loop(0, TILES_DEV, add, 0, unroll=8)


def own_kernel(ny, nz, dest_own, count, own, acc):
    acc[...] = jnp.zeros_like(acc)
    add_terms(ny, nz, lambda s: (dest_own[s], s < count[0]), own, acc)


def both_kernel(ny, nz, first, other, feats, out_y, out_z, dest_other, acc, coded, sem):
    given = other[TILES_DEV].astype(F32)
    coded[...] = (given[0:1] * 8.0 + given[1:2]).astype(jnp.int32)
    copy = pltpu.make_async_copy(coded, dest_other, sem)
    copy.start()
    acc[...] = first[...]
    copy.wait()
    add_terms(ny, nz, lambda s: (dest_other[0, s], dest_other[0, s] >= 0), other, acc)
    k = lax.axis_index("k")

    @pl.when(k == 0)
    def _():
        last = out_y.shape[0]
        out_y[...] = acc[0:last].astype(BF)

    @pl.when(k == 1)
    def _():
        last = out_z.shape[0]
        out_z[...] = acc[0:last].astype(BF)
        for m in range(2 * nz):
            for x in range(NX):
                b = (m // nz) * NX + x
                at = m * (ny * NX + NX) + ny * NX + x
                out_z[at] = feats[:, b * TB : (b + 1) * TB]


def middle_z_kernel(nz, recv, out):
    ny = out.shape[0] // NX
    here = lax.axis_index("zl")
    for h in range(2):
        for n in range(ny * NX):
            total = recv[h * nz, n].astype(F32)
            for z in range(1, nz):
                total = total + recv[h * nz + z, n].astype(F32)
            out[n, h * F_LOC : (h + 1) * F_LOC] = total.astype(BF)
        for x in range(NX):
            tile = recv[h * nz + here, ny * NX + x]
            for y in range(ny):
                out[y * NX + x, (2 + h) * F_LOC : (3 + h) * F_LOC] = tile


def middle_y_kernel(recv, feats, out):
    places = out.shape[0] // RB
    for b in range(RB):
        own = feats[:, b * TB : (b + 1) * TB]
        for p in range(places):
            total = jnp.sum(recv[:, p * RB + b].astype(F32), axis=0)
            out[p * RB + b, 0:F_LOC] = total.astype(BF)
            out[p * RB + b, F_LOC : 2 * F_LOC] = own


def agg_kernel(z_first, recv, degree, out):
    halves = 2 if z_first else 1
    size = RB // halves
    places = recv.shape[0] // size
    here = lax.axis_index("y" if z_first else "zl") * size
    deg = degree[pl.ds(lax.axis_index(COL), 1), :].astype(F32)
    for c in range(RB):
        h, n = c // size, c % size
        rows = slice(h * F_LOC, (h + 1) * F_LOC)
        total = recv[n, rows].astype(F32)
        for p in range(1, places):
            total = total + recv[p * size + n, rows].astype(F32)
        out[c, 0:F_LOC] = (total / deg).astype(BF)
        rows = slice((halves + h) * F_LOC, (halves + h + 1) * F_LOC)
        out[c, F_LOC : 2 * F_LOC] = recv[here + n, rows]


def dense_layer_kernel(recv, w_self, w_neigh, bias, cot, degree, hidden, out, dx_out):
    agg = recv[:, 0:F_LOC].reshape(RB * F_LOC, TB)
    feats = recv[:, F_LOC : 2 * F_LOC].reshape(RB * F_LOC, TB)
    ws = w_self[...]
    wn = w_neigh[...]
    first = (((0,), (0,)), ((), ()))
    last = (((1,), (1,)), ((), ()))
    preact = lax.dot_general(ws, feats, first, preferred_element_type=F32)
    preact = preact + lax.dot_general(wn, agg, first, preferred_element_type=F32)
    preact = preact + jnp.broadcast_to(bias[...], (TB, bias.shape[1])).T
    sigma = 1.0 / (1.0 + jnp.exp(-preact))
    hidden[...] = (preact * sigma).astype(BF)
    slope = sigma * (1.0 + preact * (1.0 - sigma))
    grad_pre = (cot[...].astype(F32) * slope).astype(BF)
    part_self = lax.dot_general(feats, grad_pre, last, preferred_element_type=F32)
    part_neigh = lax.dot_general(agg, grad_pre, last, preferred_element_type=F32)
    ones = jnp.ones((8, TB), BF)
    part_bias = lax.dot_general(ones, grad_pre, last, preferred_element_type=F32)[0:1]
    dx_self = jnp.dot(ws, grad_pre, preferred_element_type=F32).astype(BF)
    dagg = jnp.dot(wn, grad_pre, preferred_element_type=F32).astype(BF)
    deg = degree[pl.ds(lax.axis_index(COL), 1), :].astype(F32)
    dsum = (dagg.astype(F32) / deg).astype(BF)
    two = jnp.concatenate([part_bias[:, 0:TB], part_bias[:, TB:]], axis=0)
    high = two.astype(BF).astype(F32)
    tail = jnp.concatenate([high, two - high, jnp.zeros((12, TB), F32)], axis=0).astype(BF)
    here = lax.axis_index("k") * NX
    for c in range(RB):
        rows = slice(c * F_LOC, (c + 1) * F_LOC)
        h, x = c // NX, c % NX
        dx_out[c] = dx_self[rows]
        out[here + x, h] = dsum[rows]
        for k, part in enumerate((part_self, part_neigh)):
            at = k * NX + x
            out[at, 2 + 2 * h] = part[rows, 0:TB].astype(BF)
            out[at, 3 + 2 * h] = part[rows, TB:].astype(BF)
    for x in range(NX):
        out[NX - here + x, 0] = tail
        out[NX - here + x, 1] = tail


def parted(tail):
    two = tail[0:2] + tail[2:4]
    high = two.astype(BF).astype(F32)
    return jnp.concatenate([high, two - high, jnp.zeros((12, TB), F32)], axis=0).astype(BF)


def added(recv, n):
    total = recv[0, n].astype(F32)
    for p in range(1, recv.shape[0]):
        total = total + recv[p, n].astype(F32)
    return total


def first_step_kernel(z_first, recv, out):
    places = out.shape[0]
    mine = 0 if z_first else NX
    bias = parted(sum(recv[NX - mine + x, 0].astype(F32) for x in range(NX)))
    for h in range(2):
        sums = [added(recv, 2 + 2 * h + n).astype(BF) for n in range(2)]
        at = 0 if z_first else NX * h
        sums_at = NX if z_first else 2 * NX + 2 * h
        for p in range(places):
            if z_first and p // (places // 2) != h:
                continue
            for x in range(NX):
                out[p, at + x] = recv[mine + x, h]
            for n in range(2):
                out[p, sums_at + n] = sums[n]
    for p in range(places):
        out[p, out.shape[1] - 1] = bias


def second_step_kernel(z_first, recv, out):
    came, places = recv.shape[0], out.shape[0]
    sums_at = out.shape[1] - EXTRA
    bias = parted(added(recv, recv.shape[1] - 1))
    if z_first:
        nz = came // 2
        sums = [added(recv, NX + n).astype(BF) for n in range(2)]
        for p in range(places):
            for q in range(came):
                at = (q % nz) * RB + (q // nz) * NX
                out[p, at : at + NX] = recv[q, 0:NX]
            for n in range(2):
                out[p, sums_at + n] = sums[n]
            out[p, sums_at + 2] = bias
    else:
        for h in range(2):
            sums = [added(recv, 2 * NX + 2 * h + n).astype(BF) for n in range(2)]
            for p in range(places // 2 * h, places // 2 * (h + 1)):
                for q in range(came):
                    out[p, q * NX : (q + 1) * NX] = recv[q, h * NX : (h + 1) * NX]
                for n in range(2):
                    out[p, sums_at + n] = sums[n]
                out[p, sums_at + 2] = bias


def share_kernel(sizes, recv, dx, out, bias_out):
    def run(size):
        sums = []
        for n in range(EXTRA):
            at = range(size - EXTRA + n, recv.shape[0], size)
            sums.append(sum(recv[m].astype(F32) for m in at))
        rows = [x.astype(BF) for x in sums[:2]]
        for p in range(out.shape[0]):
            for n in range(2):
                out[p, n * F_LOC : (n + 1) * F_LOC] = rows[n]
            out[p, 2 * F_LOC : 3 * F_LOC] = dx[p % RB]
        bias_out[...] = parted(sums[2])

    if sizes[0] == sizes[1]:
        run(sizes[0])
    else:
        for k in range(2):
            pl.when(lax.axis_index("k") == k)(functools.partial(run, sizes[k]))


def pick_kernel(nz, size_0, size_1, dest_own, count, dest_other, recv, bias_sum, own, other):
    k = lax.axis_index("k")
    of_y = jnp.where(k == 0, size_0, NX)
    of_zl = jnp.where(k == 0, RB, size_1)
    of_zh = jnp.where(k == 0, NX, nz * size_1)
    bits = nz.bit_length() - 1

    def pick(d, used):
        mine = jnp.logical_and(used, ((d >> 3) & 1) == k)
        d = jnp.where(mine, d, 0)
        at = (d >> (4 + bits)) * of_y + ((d >> 4) & (nz - 1)) * of_zl
        at = at + ((d >> 2) & 1) * of_zh + (d & (NX - 1))
        tile = recv[at]
        return jnp.where(mine, tile, jnp.zeros_like(tile))

    def step(s, carry):
        own[s] = pick(dest_own[s], s < count[0])
        d = dest_other[0, s]
        other[s] = pick(d, d >= 0)
        return carry

    lax.fori_loop(0, TILES_DEV, step, 0, unroll=8)
    other[TILES_DEV] = bias_sum[...]


def back_kernel(src, own, given, vals, acc):
    @pl.when(pl.program_id(0) == 0)
    def _():
        acc[...] = jnp.zeros_like(acc)

    first = pl.program_id(0) * STEP
    for t in range(STEP):
        grad = own[t] + given[t]
        at = src[first + t]
        acc[at] = acc[at] + jnp.dot(grad, vals[t], preferred_element_type=F32)


def tile_back(src, own, given, vals):
    tiles = pl.BlockSpec((STEP, F_LOC, TB), lambda g, s: (g, 0, 0))
    return pl.pallas_call(
        back_kernel,
        out_shape=sds((RB, F_LOC, TB), F32),
        grid_spec=pltpu.PrefetchScalarGridSpec(
            num_scalar_prefetch=1,
            grid=(TILES_DEV // STEP,),
            in_specs=[tiles, tiles, pl.BlockSpec((STEP, TB, TB), lambda g, s: (g, 0, 0))],
            out_specs=pl.BlockSpec((RB, F_LOC, TB), lambda g, s: (0, 0, 0)),
        ),
        compiler_params=PARAMS,
        cost_estimate=lasting(2.2),
    )(src, own, given, vals)


def last_kernel(x, bias_sum, given, dx_neigh, grad_x, grad_self, grad_neigh, grad_bias):
    for k, out in enumerate((grad_self, grad_neigh)):
        part = x[k * RB : (k + 1) * RB, 0 : 2 * F_LOC].astype(F32)
        scale = jnp.sqrt(jnp.sum(part * part) / (RB * 32 * TB) + EPS)
        scaled = part / scale
        for c in range(RB):
            at = slice(c * F_LOC, (c + 1) * F_LOC)
            out[at, 0:TB] = scaled[c, 0:16]
            out[at, TB:] = scaled[c, 16:32]
    k = lax.axis_index("k")
    mine = bias_sum[...].astype(F32)
    theirs = given[TILES_DEV].astype(F32)
    two = (mine[0:2] + mine[2:4]) + (theirs[0:2] + theirs[2:4])
    grad_bias[...] = two / jnp.sqrt(jnp.mean(two * two) + EPS)
    for b in range(RB):
        dx_self = x[k * RB + b, 2 * F_LOC : 3 * F_LOC].astype(F32)
        grad_x[:, b * TB : (b + 1) * TB] = (dx_self + dx_neigh[b]).astype(BF)


def local(
    features,
    tile_values,
    tile_source,
    tile_dest,
    tile_count,
    degree,
    w_self,
    w_neigh,
    bias,
    cotangent,
):
    ny, nz = lax.axis_size("y"), lax.axis_size("zl")
    swap = [(0, 1), (1, 0)]
    is_first = lax.axis_index("k") == 0
    degree2 = degree.reshape(RB, TB)

    terms = tile_terms(
        tile_source, tile_dest.reshape(1, -1), tile_count, features, tile_values
    )
    terms_other = lax.ppermute(terms, "k", swap)
    sent = 2 * nz * (ny + 1) * NX
    first = whole(
        functools.partial(own_kernel, ny, nz),
        sds((sent + 1, F_LOC, TB), F32),
        [SMEM, SMEM, VMEM],
        cost=lasting(1.2),
    )(tile_dest, tile_count, terms)
    dense_y, dense_z, dest_other = whole(
        functools.partial(both_kernel, ny, nz),
        (
            sds((ny * nz * RB, F_LOC, TB), BF),
            sds((sent, F_LOC, TB), BF),
            sds((1, TB), jnp.int32),
        ),
        [VMEM] * 3,
        [
            pltpu.VMEM((sent + 1, F_LOC, TB), F32),
            pltpu.VMEM((1, TB), jnp.int32),
            pltpu.SemaphoreType.DMA,
        ],
        [VMEM, VMEM, SMEM],
    )(first, terms_other, features)

    def exchange(array, axes):
        return lax.all_to_all(array, axes, split_axis=0, concat_axis=0, tiled=True)

    def z_collect(dense_y, dense_z, features, degree2):
        one = exchange(dense_z.reshape(2 * nz, (ny + 1) * NX, F_LOC, TB), ("zh", "zl"))
        two = whole(
            functools.partial(middle_z_kernel, nz),
            sds((ny * NX, 4 * F_LOC, TB), BF),
            [VMEM],
        )(one)
        two = exchange(two, ("y", "x"))
        return whole(
            functools.partial(agg_kernel, True), sds((RB, 2 * F_LOC, TB), BF), [VMEM] * 2
        )(two, degree2)

    def y_collect(dense_y, dense_z, features, degree2):
        one = exchange(dense_y.reshape(ny, nz * RB, F_LOC, TB), "y")
        two = whole(middle_y_kernel, sds((nz * RB, 2 * F_LOC, TB), BF), [VMEM] * 2)(
            one, features
        )
        two = exchange(two, ("zl",) + COL)
        return whole(
            functools.partial(agg_kernel, False), sds((RB, 2 * F_LOC, TB), BF), [VMEM] * 2
        )(two, degree2)

    full = lax.cond(
        is_first, y_collect, z_collect, dense_y, dense_z, features, degree2
    )
    hidden, back, dx_self = whole(
        dense_layer_kernel,
        (
            sds(cotangent.shape, BF),
            sds((2 * NX, 6, F_LOC, TB), BF),
            sds((RB, F_LOC, TB), BF),
        ),
        [VMEM] * 6,
    )(full, w_self, w_neigh, bias.reshape(1, -1), cotangent, degree2)
    back = exchange(back, ("k", "x"))

    tiles = max(ny * (nz * RB + EXTRA), 2 * nz * (ny * NX + EXTRA))

    def in_two_steps(z_first):
        zs = ("zh", "zl")
        first, second = (zs, "y") if z_first else ("y", zs)
        n1, n2 = lax.axis_size(first), lax.axis_size(second)
        width = NX + EXTRA if z_first else 2 * NX + 2 + EXTRA

        def run(back):
            one = whole(
                functools.partial(first_step_kernel, z_first),
                sds((n1, width, F_LOC, TB), BF),
                [VMEM],
            )(back)
            one = exchange(one, first)
            two = whole(
                functools.partial(second_step_kernel, z_first),
                sds((n2, tiles // n2, F_LOC, TB), BF),
                [VMEM],
            )(one)
            two = exchange(two, second)
            return two.reshape(tiles, F_LOC, TB)

        return run

    portion = lax.cond(is_first, in_two_steps(True), in_two_steps(False), back)
    share, bias_sum = whole(
        functools.partial(share_kernel, (tiles // ny, tiles // (2 * nz))),
        (sds((2 * RB, 3 * F_LOC, TB), BF), sds((F_LOC, TB), BF)),
        [VMEM] * 2,
    )(portion, dx_self)
    chunks = exchange(share, ("k",) + COL)
    own, other = whole(
        functools.partial(pick_kernel, nz, tiles // ny, tiles // (2 * nz)),
        (sds((TILES_DEV, F_LOC, TB), BF), sds((TILES_DEV + 1, F_LOC, TB), BF)),
        [SMEM, SMEM, SMEM, VMEM, VMEM],
        cost=lasting(2.0),
    )(tile_dest, tile_count, dest_other, portion, bias_sum)
    given = lax.ppermute(other, "k", swap)
    dx_neigh = tile_back(tile_source, own, given, tile_values)
    grad_x, grad_self, grad_neigh, grad_bias = whole(
        last_kernel,
        (
            sds(features.shape, BF),
            sds(w_self.shape, F32),
            sds(w_self.shape, F32),
            sds((2, TB), F32),
        ),
        [VMEM] * 4,
    )(chunks, bias_sum, given, dx_neigh)
    return hidden, grad_x, grad_self, grad_neigh, grad_bias.reshape(-1)


def solution(mesh):
    vtx, col = mesh.shape["vtx"], mesh.shape["col"]
    fine = Mesh(mesh.devices.reshape(Y, vtx // (2 * Y), 2, 2, col // 2), AXES)
    placed = (
        P(COL, VTX),
        P(VTX, None, None),
        P(VTX),
        P(VTX),
        P(VTX),
        P(VTX),
        P(),
        P(),
        P(),
        P(None, AXES),
    )
    return jax.shard_map(
        local,
        mesh=fine,
        in_specs=placed,
        out_specs=(P(None, AXES), P(COL, VTX), P(), P(), P()),
        check_vma=False,
    )
```

```python
import functools

import jax
import jax.numpy as jnp
from jax import lax
from jax.experimental import pallas as pl
from jax.experimental.pallas import tpu as pltpu
from jax.sharding import Mesh
from jax.sharding import PartitionSpec as P

TB = 128
TILES_DEV = 64
RB = 8
F_LOC = 16
Y = 8
NX = 4
STEP = 32
EXTRA = 3

EPS = 1e-06
BF = jnp.bfloat16
F32 = jnp.float32

AXES = ("y", "zl", "k", "zh", "x")
COL = ("zh", "x")
VTX = ("y", "zl", "k")

VMEM = pl.BlockSpec(memory_space=pltpu.VMEM)
SMEM = pl.BlockSpec(memory_space=pltpu.SMEM)
HBM = pl.BlockSpec(memory_space=pltpu.HBM)
PARAMS = pltpu.CompilerParams(vmem_limit_bytes=32 * 1024 * 1024)
FULL_PARAMS = pltpu.CompilerParams(vmem_limit_bytes=59 * 1024 * 1024)


def whole(kernel, out_shape, in_specs, scratch=(), out_specs=None, cost=None):
    many = isinstance(out_shape, (tuple, list))
    return pl.pallas_call(
        kernel,
        out_shape=out_shape,
        in_specs=in_specs,
        out_specs=out_specs or ([VMEM] * len(out_shape) if many else VMEM),
        scratch_shapes=list(scratch),
        compiler_params=PARAMS,
        cost_estimate=cost,
    )


def lasting(us):
    return pl.CostEstimate(flops=0, transcendentals=0, bytes_accessed=int(us * 3.6e6))


def sds(shape, dtype):
    return jax.ShapeDtypeStruct(shape, dtype)


def terms_kernel(
    src_h, dest_h, count_h, feats_h, vals_h, out, src, dest, count, feats, vals, sems, val_sems
):
    small = [
        pltpu.make_async_copy(a, b, sems.at[n])
        for n, (a, b) in enumerate(
            ((src_h, src), (feats_h, feats), (dest_h, dest), (count_h, count))
        )
    ]
    parts = TILES_DEV // STEP
    large = [
        pltpu.make_async_copy(
            vals_h.at[pl.ds(g * STEP, STEP)], vals.at[pl.ds(g * STEP, STEP)], val_sems.at[g]
        )
        for g in range(parts)
    ]
    for copy in small + large:
        copy.start()
    for copy in small:
        copy.wait()
    slot = lax.broadcasted_iota(jnp.int32, (16, TB), 1)
    row = lax.broadcasted_iota(jnp.int32, (16, TB), 0)
    d = jnp.concatenate([dest[...], dest[...]], axis=1)
    d = jnp.where(slot < count[0], jnp.broadcast_to(d, (16, TB)), -1)
    coded = jnp.where(row == 0, d >> 3, d & 7)
    out[TILES_DEV] = coded.astype(F32).astype(BF)
    for g in range(parts):
        large[g].wait()
        for t in range(g * STEP, (g + 1) * STEP, 2):
            one, two = (
                feats[:, pl.ds(pl.multiple_of(src[n] * TB, TB), TB)] for n in (t, t + 1)
            )
            zero = jnp.zeros_like(one)
            pair = jnp.concatenate(
                [
                    jnp.concatenate([one, zero], axis=1),
                    jnp.concatenate([zero, two], axis=1),
                ],
                axis=0,
            )
            term = lax.dot_general(
                pair,
                jnp.concatenate([vals[t], vals[t + 1]], axis=1),
                (((1,), (1,)), ((), ())),
                preferred_element_type=F32,
            ).astype(BF)
            out[t] = term[0:F_LOC]
            out[t + 1] = term[F_LOC:]


def tile_terms(src, dest, count, feats, vals):
    return pl.pallas_call(
        terms_kernel,
        out_shape=sds((TILES_DEV + 1, F_LOC, TB), BF),
        in_specs=[HBM] * 5,
        out_specs=VMEM,
        scratch_shapes=[
            pltpu.SMEM((TILES_DEV,), jnp.int32),
            pltpu.VMEM((1, TILES_DEV), jnp.int32),
            pltpu.SMEM((1,), jnp.int32),
            pltpu.VMEM(feats.shape, BF),
            pltpu.VMEM(vals.shape, BF),
            pltpu.SemaphoreType.DMA((4,)),
            pltpu.SemaphoreType.DMA((TILES_DEV // STEP,)),
        ],
        compiler_params=FULL_PARAMS,
    )(src, dest, count, feats, vals)


def add_terms(ny, nz, dest_of, terms, acc):
    k = lax.axis_index("k")
    dump = acc.shape[0] - 1
    size = ny * NX + NX
    of_y = jnp.where(k == 1, NX, nz * RB)
    of_zl = jnp.where(k == 1, size, RB)
    of_zh = jnp.where(k == 1, nz * size, NX)
    bits = nz.bit_length() - 1

    def add(s, carry):
        d, used = dest_of(s)
        mine = jnp.logical_and(used, ((d >> 3) & 1) == k)
        at = (d >> (4 + bits)) * of_y + ((d >> 4) & (nz - 1)) * of_zl
        at = at + ((d >> 2) & 1) * of_zh + (d & (NX - 1))
        at = jnp.where(mine, at, dump)
        acc[at] = acc[at] + terms[s].astype(F32)
        return carry

    lax.fori_loop(0, TILES_DEV, add, 0, unroll=8)


def own_kernel(ny, nz, dest_own, count, own, acc):
    acc[...] = jnp.zeros_like(acc)
    add_terms(ny, nz, lambda s: (dest_own[s], s < count[0]), own, acc)


def both_kernel(ny, nz, first, other, feats, out_y, out_z, dest_other, acc, coded, sem):
    given = other[TILES_DEV].astype(F32)
    coded[...] = (given[0:1] * 8.0 + given[1:2]).astype(jnp.int32)
    copy = pltpu.make_async_copy(coded, dest_other, sem)
    copy.start()
    acc[...] = first[...]
    copy.wait()
    add_terms(ny, nz, lambda s: (dest_other[0, s], dest_other[0, s] >= 0), other, acc)
    k = lax.axis_index("k")

    @pl.when(k == 0)
    def _():
        last = out_y.shape[0]
        out_y[...] = acc[0:last].astype(BF)

    @pl.when(k == 1)
    def _():
        last = out_z.shape[0]
        out_z[...] = acc[0:last].astype(BF)
        for m in range(2 * nz):
            for x in range(NX):
                b = (m // nz) * NX + x
                at = m * (ny * NX + NX) + ny * NX + x
                out_z[at] = feats[:, b * TB : (b + 1) * TB]


def middle_z_kernel(nz, recv, out):
    ny = out.shape[0] // NX
    here = lax.axis_index("zl")
    for h in range(2):
        for n in range(ny * NX):
            total = recv[h * nz, n].astype(F32)
            for z in range(1, nz):
                total = total + recv[h * nz + z, n].astype(F32)
            out[n, h * F_LOC : (h + 1) * F_LOC] = total.astype(BF)
        for x in range(NX):
            tile = recv[h * nz + here, ny * NX + x]
            for y in range(ny):
                out[y * NX + x, (2 + h) * F_LOC : (3 + h) * F_LOC] = tile


def middle_y_kernel(recv, feats, out):
    places = out.shape[0] // RB
    for b in range(RB):
        own = feats[:, b * TB : (b + 1) * TB]
        for p in range(places):
            total = jnp.sum(recv[:, p * RB + b].astype(F32), axis=0)
            out[p * RB + b, 0:F_LOC] = total.astype(BF)
            out[p * RB + b, F_LOC : 2 * F_LOC] = own


def agg_kernel(z_first, recv, degree, out):
    halves = 2 if z_first else 1
    size = RB // halves
    places = recv.shape[0] // size
    here = lax.axis_index("y" if z_first else "zl") * size
    deg = degree[pl.ds(lax.axis_index(COL), 1), :].astype(F32)
    for c in range(RB):
        h, n = c // size, c % size
        rows = slice(h * F_LOC, (h + 1) * F_LOC)
        total = recv[n, rows].astype(F32)
        for p in range(1, places):
            total = total + recv[p * size + n, rows].astype(F32)
        out[c, 0:F_LOC] = (total / deg).astype(BF)
        rows = slice((halves + h) * F_LOC, (halves + h + 1) * F_LOC)
        out[c, F_LOC : 2 * F_LOC] = recv[here + n, rows]


def dense_layer_kernel(recv, w_self, w_neigh, bias, cot, degree, hidden, out, dx_out):
    agg = recv[:, 0:F_LOC].reshape(RB * F_LOC, TB)
    feats = recv[:, F_LOC : 2 * F_LOC].reshape(RB * F_LOC, TB)
    ws = w_self[...]
    wn = w_neigh[...]
    first = (((0,), (0,)), ((), ()))
    last = (((1,), (1,)), ((), ()))
    preact = lax.dot_general(ws, feats, first, preferred_element_type=F32)
    preact = preact + lax.dot_general(wn, agg, first, preferred_element_type=F32)
    preact = preact + jnp.broadcast_to(bias[...], (TB, bias.shape[1])).T
    sigma = 1.0 / (1.0 + jnp.exp(-preact))
    hidden[...] = (preact * sigma).astype(BF)
    slope = sigma * (1.0 + preact * (1.0 - sigma))
    grad_pre = (cot[...].astype(F32) * slope).astype(BF)
    part_self = lax.dot_general(feats, grad_pre, last, preferred_element_type=F32)
    part_neigh = lax.dot_general(agg, grad_pre, last, preferred_element_type=F32)
    ones = jnp.ones((8, TB), BF)
    part_bias = lax.dot_general(ones, grad_pre, last, preferred_element_type=F32)[0:1]
    dx_self = jnp.dot(ws, grad_pre, preferred_element_type=F32).astype(BF)
    dagg = jnp.dot(wn, grad_pre, preferred_element_type=F32).astype(BF)
    deg = degree[pl.ds(lax.axis_index(COL), 1), :].astype(F32)
    dsum = (dagg.astype(F32) / deg).astype(BF)
    two = jnp.concatenate([part_bias[:, 0:TB], part_bias[:, TB:]], axis=0)
    high = two.astype(BF).astype(F32)
    tail = jnp.concatenate([high, two - high, jnp.zeros((12, TB), F32)], axis=0).astype(BF)
    here = lax.axis_index("k") * NX
    for c in range(RB):
        rows = slice(c * F_LOC, (c + 1) * F_LOC)
        h, x = c // NX, c % NX
        dx_out[c] = dx_self[rows]
        out[here + x, h] = dsum[rows]
        for k, part in enumerate((part_self, part_neigh)):
            at = k * NX + x
            out[at, 2 + 2 * h] = part[rows, 0:TB].astype(BF)
            out[at, 3 + 2 * h] = part[rows, TB:].astype(BF)
    for x in range(NX):
        out[NX - here + x, 0] = tail
        out[NX - here + x, 1] = tail


def parted(tail):
    two = tail[0:2] + tail[2:4]
    high = two.astype(BF).astype(F32)
    return jnp.concatenate([high, two - high, jnp.zeros((12, TB), F32)], axis=0).astype(BF)


def added(recv, n):
    total = recv[0, n].astype(F32)
    for p in range(1, recv.shape[0]):
        total = total + recv[p, n].astype(F32)
    return total


def first_step_kernel(z_first, recv, out):
    places = out.shape[0]
    mine = 0 if z_first else NX
    bias = parted(sum(recv[NX - mine + x, 0].astype(F32) for x in range(NX)))
    for h in range(2):
        sums = [added(recv, 2 + 2 * h + n).astype(BF) for n in range(2)]
        at = 0 if z_first else NX * h
        sums_at = NX if z_first else 2 * NX + 2 * h
        for p in range(places):
            if z_first and p // (places // 2) != h:
                continue
            for x in range(NX):
                out[p, at + x] = recv[mine + x, h]
            for n in range(2):
                out[p, sums_at + n] = sums[n]
    for p in range(places):
        out[p, out.shape[1] - 1] = bias


def second_step_kernel(z_first, recv, out):
    came, places = recv.shape[0], out.shape[0]
    sums_at = out.shape[1] - EXTRA
    bias = parted(added(recv, recv.shape[1] - 1))
    if z_first:
        nz = came // 2
        sums = [added(recv, NX + n).astype(BF) for n in range(2)]
        for p in range(places):
            for q in range(came):
                at = (q % nz) * RB + (q // nz) * NX
                out[p, at : at + NX] = recv[q, 0:NX]
            for n in range(2):
                out[p, sums_at + n] = sums[n]
            out[p, sums_at + 2] = bias
    else:
        for h in range(2):
            sums = [added(recv, 2 * NX + 2 * h + n).astype(BF) for n in range(2)]
            for p in range(places // 2 * h, places // 2 * (h + 1)):
                for q in range(came):
                    out[p, q * NX : (q + 1) * NX] = recv[q, h * NX : (h + 1) * NX]
                for n in range(2):
                    out[p, sums_at + n] = sums[n]
                out[p, sums_at + 2] = bias


def share_kernel(sizes, recv, dx, out, bias_out):
    def run(size):
        sums = []
        for n in range(EXTRA):
            at = range(size - EXTRA + n, recv.shape[0], size)
            sums.append(sum(recv[m].astype(F32) for m in at))
        rows = [x.astype(BF) for x in sums[:2]]
        for p in range(out.shape[0]):
            for n in range(2):
                out[p, n * F_LOC : (n + 1) * F_LOC] = rows[n]
            out[p, 2 * F_LOC : 3 * F_LOC] = dx[p % RB]
        bias_out[...] = parted(sums[2])

    if sizes[0] == sizes[1]:
        run(sizes[0])
    else:
        for k in range(2):
            pl.when(lax.axis_index("k") == k)(functools.partial(run, sizes[k]))


def pick_kernel(nz, size_0, size_1, dest_own, count, dest_other, recv, bias_sum, own, other):
    k = lax.axis_index("k")
    of_y = jnp.where(k == 0, size_0, NX)
    of_zl = jnp.where(k == 0, RB, size_1)
    of_zh = jnp.where(k == 0, NX, nz * size_1)
    bits = nz.bit_length() - 1

    def pick(d, used):
        mine = jnp.logical_and(used, ((d >> 3) & 1) == k)
        d = jnp.where(mine, d, 0)
        at = (d >> (4 + bits)) * of_y + ((d >> 4) & (nz - 1)) * of_zl
        at = at + ((d >> 2) & 1) * of_zh + (d & (NX - 1))
        tile = recv[at]
        return jnp.where(mine, tile, jnp.zeros_like(tile))

    def step(s, carry):
        own[s] = pick(dest_own[s], s < count[0])
        d = dest_other[0, s]
        other[s] = pick(d, d >= 0)
        return carry

    lax.fori_loop(0, TILES_DEV, step, 0, unroll=8)
    other[TILES_DEV] = bias_sum[...]


def back_kernel(src, own, given, vals, acc):
    @pl.when(pl.program_id(0) == 0)
    def _():
        acc[...] = jnp.zeros_like(acc)

    first = pl.program_id(0) * STEP
    for t in range(STEP):
        grad = own[t] + given[t]
        at = src[first + t]
        acc[at] = acc[at] + jnp.dot(grad, vals[t], preferred_element_type=F32)


def tile_back(src, own, given, vals):
    tiles = pl.BlockSpec((STEP, F_LOC, TB), lambda g, s: (g, 0, 0))
    return pl.pallas_call(
        back_kernel,
        out_shape=sds((RB, F_LOC, TB), F32),
        grid_spec=pltpu.PrefetchScalarGridSpec(
            num_scalar_prefetch=1,
            grid=(TILES_DEV // STEP,),
            in_specs=[tiles, tiles, pl.BlockSpec((STEP, TB, TB), lambda g, s: (g, 0, 0))],
            out_specs=pl.BlockSpec((RB, F_LOC, TB), lambda g, s: (0, 0, 0)),
        ),
        compiler_params=PARAMS,
        cost_estimate=lasting(2.2),
    )(src, own, given, vals)


def last_kernel(x, bias_sum, given, dx_neigh, grad_x, grad_self, grad_neigh, grad_bias):
    for k, out in enumerate((grad_self, grad_neigh)):
        part = x[k * RB : (k + 1) * RB, 0 : 2 * F_LOC].astype(F32)
        scale = jnp.sqrt(jnp.sum(part * part) / (RB * 32 * TB) + EPS)
        scaled = part / scale
        for c in range(RB):
            at = slice(c * F_LOC, (c + 1) * F_LOC)
            out[at, 0:TB] = scaled[c, 0:16]
            out[at, TB:] = scaled[c, 16:32]
    k = lax.axis_index("k")
    mine = bias_sum[...].astype(F32)
    theirs = given[TILES_DEV].astype(F32)
    two = (mine[0:2] + mine[2:4]) + (theirs[0:2] + theirs[2:4])
    grad_bias[...] = two / jnp.sqrt(jnp.mean(two * two) + EPS)
    for b in range(RB):
        dx_self = x[k * RB + b, 2 * F_LOC : 3 * F_LOC].astype(F32)
        grad_x[:, b * TB : (b + 1) * TB] = (dx_self + dx_neigh[b]).astype(BF)


def local(
    features,
    tile_values,
    tile_source,
    tile_dest,
    tile_count,
    degree,
    w_self,
    w_neigh,
    bias,
    cotangent,
):
    ny, nz = lax.axis_size("y"), lax.axis_size("zl")
    swap = [(0, 1), (1, 0)]
    is_first = lax.axis_index("k") == 0
    degree2 = degree.reshape(RB, TB)

    terms = tile_terms(
        tile_source, tile_dest.reshape(1, -1), tile_count, features, tile_values
    )
    terms_other = lax.ppermute(terms, "k", swap)
    sent = 2 * nz * (ny + 1) * NX
    first = whole(
        functools.partial(own_kernel, ny, nz),
        sds((sent + 1, F_LOC, TB), F32),
        [SMEM, SMEM, VMEM],
        cost=lasting(1.2),
    )(tile_dest, tile_count, terms)
    dense_y, dense_z, dest_other = whole(
        functools.partial(both_kernel, ny, nz),
        (
            sds((ny * nz * RB, F_LOC, TB), BF),
            sds((sent, F_LOC, TB), BF),
            sds((1, TB), jnp.int32),
        ),
        [VMEM] * 3,
        [
            pltpu.VMEM((sent + 1, F_LOC, TB), F32),
            pltpu.VMEM((1, TB), jnp.int32),
            pltpu.SemaphoreType.DMA,
        ],
        [VMEM, VMEM, SMEM],
    )(first, terms_other, features)

    def exchange(array, axes):
        return lax.all_to_all(array, axes, split_axis=0, concat_axis=0, tiled=True)

    def z_collect(dense_y, dense_z, features, degree2):
        one = exchange(dense_z.reshape(2 * nz, (ny + 1) * NX, F_LOC, TB), ("zh", "zl"))
        two = whole(
            functools.partial(middle_z_kernel, nz),
            sds((ny * NX, 4 * F_LOC, TB), BF),
            [VMEM],
        )(one)
        two = exchange(two, ("y", "x"))
        return whole(
            functools.partial(agg_kernel, True), sds((RB, 2 * F_LOC, TB), BF), [VMEM] * 2
        )(two, degree2)

    def y_collect(dense_y, dense_z, features, degree2):
        one = exchange(dense_y.reshape(ny, nz * RB, F_LOC, TB), "y")
        two = whole(middle_y_kernel, sds((nz * RB, 2 * F_LOC, TB), BF), [VMEM] * 2)(
            one, features
        )
        two = exchange(two, ("zl",) + COL)
        return whole(
            functools.partial(agg_kernel, False), sds((RB, 2 * F_LOC, TB), BF), [VMEM] * 2
        )(two, degree2)

    full = lax.cond(
        is_first, y_collect, z_collect, dense_y, dense_z, features, degree2
    )
    hidden, back, dx_self = whole(
        dense_layer_kernel,
        (
            sds(cotangent.shape, BF),
            sds((2 * NX, 6, F_LOC, TB), BF),
            sds((RB, F_LOC, TB), BF),
        ),
        [VMEM] * 6,
    )(full, w_self, w_neigh, bias.reshape(1, -1), cotangent, degree2)
    back = exchange(back, ("k", "x"))

    tiles = max(ny * (nz * RB + EXTRA), 2 * nz * (ny * NX + EXTRA))

    def in_two_steps(z_first):
        zs = ("zh", "zl")
        first, second = (zs, "y") if z_first else ("y", zs)
        n1, n2 = lax.axis_size(first), lax.axis_size(second)
        width = NX + EXTRA if z_first else 2 * NX + 2 + EXTRA

        def run(back):
            one = whole(
                functools.partial(first_step_kernel, z_first),
                sds((n1, width, F_LOC, TB), BF),
                [VMEM],
            )(back)
            one = exchange(one, first)
            two = whole(
                functools.partial(second_step_kernel, z_first),
                sds((n2, tiles // n2, F_LOC, TB), BF),
                [VMEM],
            )(one)
            two = exchange(two, second)
            return two.reshape(tiles, F_LOC, TB)

        return run

    portion = lax.cond(is_first, in_two_steps(True), in_two_steps(False), back)
    share, bias_sum = whole(
        functools.partial(share_kernel, (tiles // ny, tiles // (2 * nz))),
        (sds((2 * RB, 3 * F_LOC, TB), BF), sds((F_LOC, TB), BF)),
        [VMEM] * 2,
    )(portion, dx_self)
    chunks = exchange(share, ("k",) + COL)
    own, other = whole(
        functools.partial(pick_kernel, nz, tiles // ny, tiles // (2 * nz)),
        (sds((TILES_DEV, F_LOC, TB), BF), sds((TILES_DEV + 1, F_LOC, TB), BF)),
        [SMEM, SMEM, SMEM, VMEM, VMEM],
        cost=lasting(2.0),
    )(tile_dest, tile_count, dest_other, portion, bias_sum)
    given = lax.ppermute(other, "k", swap)
    dx_neigh = tile_back(tile_source, own, given, tile_values)
    grad_x, grad_self, grad_neigh, grad_bias = whole(
        last_kernel,
        (
            sds(features.shape, BF),
            sds(w_self.shape, F32),
            sds(w_self.shape, F32),
            sds((2, TB), F32),
        ),
        [VMEM] * 4,
    )(chunks, bias_sum, given, dx_neigh)
    return hidden, grad_x, grad_self, grad_neigh, grad_bias.reshape(-1)


def solution(mesh):
    vtx, col = mesh.shape["vtx"], mesh.shape["col"]
    fine = Mesh(mesh.devices.reshape(Y, vtx // (2 * Y), 2, 2, col // 2), AXES)
    placed = (
        P(COL, VTX),
        P(VTX, None, None),
        P(VTX),
        P(VTX),
        P(VTX),
        P(VTX),
        P(),
        P(),
        P(),
        P(None, AXES),
    )
    return jax.shard_map(
        local,
        mesh=fine,
        in_specs=placed,
        out_specs=(P(None, AXES), P(COL, VTX), P(), P(), P()),
        check_vma=False,
    )
```
